256 devices in a mesh: seq: 32 (over z, x), mp: 8 (over y, core), dp: 1.
Axes of the slice: x: 4, y: 4, z: 8, core: 2. Of those that a mesh axis runs over, the one named last changes fastest.
Arguments:
- tokens: bfloat16 [65536, 4096], P(('dp', 'seq'), 'mp'), may hold values from -6 to 6
- flags: int32 [65536], P(('dp', 'seq')), may hold values from 0 to 1, as said below
- norm_gain: float32 [4096], replicated, may hold values from 0.5 to 1.5
- w_query: bfloat16 [4096, 2048], P(None, 'mp'), may hold values from -0.09375 to 0.09375
- w_key: bfloat16 [4096, 2048], P(None, 'mp'), may hold values from -0.09375 to 0.09375
- w_value: bfloat16 [4096, 2048], P(None, 'mp'), may hold values from -0.09375 to 0.09375
- w_out: bfloat16 [2048, 4096], P('mp'), may hold values from -0.5 to 0.5
Outputs:
- upsampled: bfloat16 [65536, 4096], P(('dp', 'seq'), 'mp')
The draws below stay inside these ranges and needn't reach their ends.
Inputs may be any that keep to these rules, and one draw needn't show every extreme that they name: flags of the first token is 1, and each aligned block of 2048 tokens holds exactly 256 flags equal to 1.
All inputs are finite; a program needn't handle non-finite values.
Results may differ from the reference program's by a relative error of at most 0.019.
Values may be sent and summed in bfloat16 or wider, within the bound.
No kernel may reach another device: no remote copies, remote signals or barrier semaphores. Data moves between devices by JAX's collectives and lax.ppermute only.
A program may use at most 128 MiB of HBM per device.

```python
import jax
import jax.numpy as jnp
from jax import lax

D = 4096
HEADS = 16
HD = 128
TOK_DEV = 2048
TOKENS = 65536
SEG_DEV = 256
NSEG = 8192


def draw_flags(key, part):
    key = jax.random.fold_in(key, 11)
    count = TOKENS // TOK_DEV
    keys = jax.random.split(key, count)
    perms = jax.vmap(lambda k: jax.random.permutation(k, TOK_DEV))(keys)
    first = perms[0]
    forced = jnp.where(first == 0, first[0], first).at[0].set(0)
    perms = perms.at[0].set(forced)
    marks = (perms < SEG_DEV).astype(jnp.int32)
    return marks.reshape(TOKENS)


def levels(stream_key, extent, pieces, least, largest):
    loudness, own = 1.0, jax.random.fold_in(stream_key, 6)
    for dim, parts in pieces:
        steps = jnp.exp(jax.random.uniform(jax.random.fold_in(own, dim), (parts,), jnp.float32, least / len(pieces), largest / len(pieces)))
        loudness = loudness * jnp.repeat(steps, extent[dim] // parts).reshape([-1 if axis == dim else 1 for axis in range(len(extent))])
    return loudness


def normal_values(stream_key, shape, deviation, limit, cuts=(), held_as=jnp.bfloat16):
    gain = levels(stream_key, shape, cuts, -0.22, 0.18) if cuts else 1.0
    values = jax.random.normal(stream_key, shape, jnp.float32) * deviation * gain
    return jnp.minimum(jnp.maximum(values, -limit), limit).astype(held_as)


def setup_inputs(seed: int = 0, part: int = 0) -> dict:
    key_list = jax.random.split(jax.random.key(seed), 8)
    own_keys = jax.random.split(jax.random.fold_in(key_list[7], part), 8)
    tokens = normal_values(own_keys[0], (TOKENS, D), 1.0, 6.0, ((0, 32), (1, 8)))
    flags = draw_flags(jax.random.fold_in(jax.random.fold_in(key_list[7], part), 71), part)
    norm_gain = jnp.clip(1.0 + 0.1 * jax.random.normal(key_list[2], (D,), jnp.float32), 0.5, 1.5)
    w_query = normal_values(key_list[3], (D, HEADS * HD), D ** -0.5, 0.09375, ((1, 8),))
    w_key = normal_values(key_list[4], (D, HEADS * HD), D ** -0.5, 0.09375, ((1, 8),))
    w_value = normal_values(key_list[5], (D, HEADS * HD), D ** -0.5, 0.09375, ((1, 8),))
    w_out = normal_values(key_list[6], (HEADS * HD, D), HD ** -0.5, 0.5, ((0, 8),))
    return dict(tokens=tokens, flags=flags, norm_gain=norm_gain, w_query=w_query, w_key=w_key, w_value=w_value, w_out=w_out)


def reference(tokens, flags, norm_gain, w_query, w_key, w_value, w_out):
    ids = (jnp.cumsum(flags) - 1).astype(jnp.int32)
    sums = jax.ops.segment_sum(tokens.astype(jnp.float32), ids, num_segments=NSEG)
    sizes = jax.ops.segment_sum(jnp.ones(ids.shape, jnp.float32), ids, num_segments=NSEG)
    means = sums / sizes[:, None]
    rstd = lax.rsqrt(lax.optimization_barrier(jnp.mean(means * means, axis=1, keepdims=True)) + 1e-05)
    normed = (means * rstd * norm_gain[None, :]).astype(jnp.bfloat16)
    query = jnp.dot(normed, w_query, preferred_element_type=jnp.float32).astype(jnp.bfloat16)
    keyed = jnp.dot(normed, w_key, preferred_element_type=jnp.float32).astype(jnp.bfloat16)
    valued = jnp.dot(normed, w_value, preferred_element_type=jnp.float32).astype(jnp.bfloat16)
    bias = jnp.log(sizes).astype(jnp.bfloat16).astype(jnp.float32)
    order = jnp.arange(NSEG).astype(jnp.int32)
    allowed = order[None, :] <= order[:, None]

    def one_head(head):
        start = (head * HD).astype(jnp.int32)
        q_part = lax.dynamic_slice_in_dim(query, start, HD, 1)
        k_part = lax.dynamic_slice_in_dim(keyed, start, HD, 1)
        v_part = lax.dynamic_slice_in_dim(valued, start, HD, 1)
        scores = jnp.dot(q_part, k_part.T, preferred_element_type=jnp.float32) * HD ** (-0.5) + bias[None, :]
        scores = jnp.where(allowed, scores, -jnp.inf)
        peak = lax.optimization_barrier(jnp.max(scores, axis=1, keepdims=True))
        expo = jnp.exp(scores - peak)
        weights = (expo / lax.optimization_barrier(jnp.sum(expo, axis=1, keepdims=True))).astype(jnp.bfloat16)
        return jnp.dot(weights, v_part, preferred_element_type=jnp.float32).astype(jnp.bfloat16)
    heads = lax.map(one_head, jnp.arange(HEADS).astype(jnp.int32))
    attended = jnp.transpose(heads, (1, 0, 2)).reshape(NSEG, HEADS * HD)
    coarse = (means + jnp.dot(attended, w_out, preferred_element_type=jnp.float32)).astype(jnp.bfloat16)
    picked = jnp.take(coarse, ids, axis=0).astype(jnp.float32)
    return (tokens.astype(jnp.float32) + picked).astype(jnp.bfloat16)
```

```python
import functools

import jax
import jax.numpy as jnp
import numpy as np
from jax import lax
from jax.experimental import pallas as pl
from jax.experimental.pallas import tpu as pltpu
from jax.sharding import PartitionSpec as P

HD = 128
NZ, NX, NY, NC = 8, 4, 4, 2
SEG = 256
ROWS = SEG + 16
TOK = 2048
FEAT = 512
COLS = 256
WIDTH = 4096
SCORE = 1.4426950408889634 * HD**-0.5
LOG2E = 1.4426950408889634
LOW = -1e30
VMEM_LIMIT = 48 * 1024 * 1024
F32, BF16 = jnp.float32, jnp.bfloat16


def number(z, x, y, c):
    return ((z % NZ) * NX + x % NX) * (NY * NC) + (y % NY) * NC + c % NC


def everywhere():
    return [(z, x, y, c) for z in range(NZ) for x in range(NX) for y in range(NY) for c in range(NC)]


def way(c):
    return 1 if c == 0 else -1


def move(value, target):
    pairs = [(number(*d), number(*target(*d))) for d in everywhere()]
    return lax.ppermute(value, ("seq", "mp"), pairs)


def swap(value):
    return move(value, lambda z, x, y, c: (z, x, y, 1 - c))


def y_one(value):
    return move(value, lambda z, x, y, c: (z, x, y + way(c), c))


def y_other(value):
    return move(value, lambda z, x, y, c: (z, x, y - way(c), c))


def z_one(value):
    return move(value, lambda z, x, y, c: (z + way(c), x, y, c))


def z_other(value):
    return move(value, lambda z, x, y, c: (z - way(c), x, y, c))


def x_by(value, by):
    return move(value, lambda z, x, y, c: (z, x + by, y, c))


def sources(y, c):
    own = [(y, c), (y - way(c), c), (y + way(c), c), (y + 2, c)]
    o = 1 - c
    other = [(y, o), (y - way(o), o), (y + way(o), o), (y + 2, o)]
    return [((b[0] % NY) * NC + b[1]) for b in own + other]


def mp_exchange(value):
    first = y_one(value)
    second = y_other(value)
    sibling = swap(value)
    far = y_one(first)
    return [value, first, second, far, sibling, swap(first), swap(second), swap(far)]


def device_table():
    rows = []
    for z, x, y, c in everywhere():
        row = [y * NC + c] + sources(y, c)
        row += [x] + [(x - k) % NX for k in (1, 2, 3)]
        for k in (1, 2, 3, 4):
            row += [int((z - way(c) * k) % NZ < z), int((z + way(c) * k) % NZ < z)]
        row += [0] * (32 - len(row))
        rows.append(row)
    return np.asarray(rows, np.int32)


I_MP, I_SRC, I_X, I_OK = 0, 1, 9, 13
SMEM = pl.BlockSpec(memory_space=pltpu.SMEM)
WHOLE = pl.BlockSpec(memory_space=pltpu.VMEM)


def call(body, outs, ins, flops=0, moved=0, scratch=(), aliases=None):
    return pl.pallas_call(
        body,
        out_shape=outs,
        in_specs=[SMEM] + [WHOLE] * (len(ins) - 1),
        out_specs=[WHOLE] * len(outs),
        scratch_shapes=list(scratch),
        compiler_params=pltpu.CompilerParams(vmem_limit_bytes=VMEM_LIMIT),
        cost_estimate=pl.CostEstimate(flops=flops, bytes_accessed=moved, transcendentals=0),
    )(*ins)


def shape(dims, dtype):
    return jax.ShapeDtypeStruct(dims, dtype)


def dot(a, b):
    return jnp.dot(a, b, preferred_element_type=F32)


def iota(dims, axis):
    return lax.broadcasted_iota(jnp.int32, dims, axis)


def ones_where(condition):
    return jnp.where(condition, 1.0, 0.0).astype(BF16)


def edge_kernel(info, flags, tokens, ids_out, head_out, tail_out, marks):
    f = flags[...].astype(F32).astype(BF16)
    upto = ones_where(iota((128, 128), 0) <= iota((128, 128), 1))
    inside = dot(f, upto)
    rows = dot(f, jnp.ones((128, 128), BF16)).astype(BF16)
    before = dot(ones_where(iota((16, 16), 1) < iota((16, 16), 0)), rows)
    ids_out[...] = (inside + before - 1.0).astype(jnp.int32)
    wanted = jnp.where(iota((16, 128), 0) < 8, -1, SEG - 1)
    for r in range(16):
        marks[:, r * 128 : (r + 1) * 128] = ones_where(ids_out[r : r + 1, :] == wanted)
    sums = dot(marks[...], tokens[...])
    counts = dot(marks[...], jnp.ones((TOK, 128), BF16))
    head_out[:, :FEAT] = sums[:8]
    head_out[:, FEAT:] = counts[:8]
    tail_out[:, :FEAT] = sums[8:]
    tail_out[:, FEAT:] = counts[8:]


def pool_kernel(info, ids, tokens, sums_out, counts_out, hot):
    segment = iota((SEG, 128), 0)
    for r in range(16):
        hot[:, r * 128 : (r + 1) * 128] = ones_where(ids[r : r + 1, :] == segment)
    sums_out[...] = dot(hot[...], tokens[...])
    counts_out[...] = dot(hot[...], jnp.ones((TOK, 128), BF16))


def wide(column, times):
    return jnp.concatenate([column] * times, axis=1)


def split(value, parts):
    out = []
    for _ in range(parts):
        high = value.astype(BF16).astype(F32)
        out.append(high)
        value = value - high
    return out


def norm_kernel(info, sums, counts, head, above, below, gain, means_out, u_out, bias_out):
    g = gain[pl.ds(info[I_MP], 1), :]
    last = iota((SEG, 128), 0) == SEG - 1
    size = counts[...] + jnp.where(last, above[0:1, FEAT:], 0.0)
    total = sums[...] + jnp.where(iota((SEG, FEAT), 0) == SEG - 1, above[0:1, :FEAT], 0.0)
    size = jnp.maximum(size, 1.0)
    means = total / wide(size, 4)
    means_out[:SEG, :] = means
    u_out[:SEG, :] = (means * g).astype(BF16)
    squares = jnp.sum(means * means, axis=1, keepdims=True)
    squares = jnp.transpose(jnp.broadcast_to(squares, (SEG, 128)))[:16]
    high, low = split(squares, 2)
    extra_size = jnp.maximum(head[0:1, FEAT:] + below[0:1, FEAT:], 1.0)
    extra = (head[0:1, :FEAT] + below[0:1, :FEAT]) / wide(extra_size, 4)
    extra_squares = jnp.broadcast_to(jnp.sum(extra * extra, axis=1, keepdims=True), (16, SEG))
    extra_high, extra_low = split(extra_squares, 2)
    row = iota((16, FEAT), 0)
    means_out[SEG:, :] = jnp.where(row == 0, extra, 0.0)
    tail = jnp.where(row == 0, extra * g, 0.0)
    tail = jnp.where(row == 1, jnp.concatenate([high, low], axis=1), tail)
    tail = jnp.where(row == 2, jnp.concatenate([extra_high, extra_low], axis=1), tail)
    u_out[SEG:, :] = tail.astype(BF16)
    bias = jnp.log(jnp.transpose(size)[:16])
    bias_out[...] = jnp.concatenate([bias, bias], axis=1).astype(BF16)


def project_kernel(info, *refs):
    blocks = refs[:8]
    w_query, w_key, w_value, bias, q_out, kv_out = refs[8:]
    tail = jnp.zeros((16, FEAT), F32)
    for u in blocks:
        tail = tail + u[SEG:, :].astype(F32)
    squares = tail[:, :SEG] + tail[:, SEG:]
    scale = lax.rsqrt(squares / WIDTH + 1e-05)
    column = jnp.transpose(jnp.broadcast_to(scale[1:2, :], (128, SEG)))
    column = wide(column, 2)

    def product(weight, rows):
        acc = jnp.zeros((rows, COLS), F32)
        for i, u in enumerate(blocks):
            start = pl.multiple_of(info[I_SRC + i] * FEAT, FEAT)
            acc = acc + dot(u[:rows, :], weight[pl.ds(start, FEAT), :])
        return acc

    query = product(w_query, ROWS)
    q_out[:SEG, :] = (query[:SEG] * column * SCORE).astype(BF16)
    extra = query[SEG:] * scale[2:3, :] * SCORE
    q_out[SEG:, :] = jnp.where(iota((16, COLS), 0) == 0, extra, 0.0).astype(BF16)
    kv_out[:SEG, :COLS] = (product(w_key, SEG) * column).astype(BF16)
    kv_out[:SEG, COLS:] = (product(w_value, SEG) * column).astype(BF16)
    kv_out[SEG:, :] = bias[...]


def nt_dot(a, b):
    return lax.dot_general(a, b, (((1,), (1,)), ((), ())), preferred_element_type=F32)


def attend(q, k, v, bias, acc_ref, m_ref, l_ref, where, h, mask=None):
    lanes = slice(h * HD, (h + 1) * HD)
    scores = nt_dot(q[:, lanes], k) + bias
    if mask is not None:
        scores = jnp.where(mask, scores, LOW)
    old = m_ref[where, h]
    peak = jnp.maximum(old, jnp.max(scores, axis=1, keepdims=True))
    expo = jnp.exp2(scores - peak[:, :1])
    if mask is not None:
        expo = jnp.where(mask, expo, 0.0)
    fade = jnp.exp2(old - peak)
    m_ref[where, h] = peak
    l_ref[where, h] = l_ref[where, h] * fade + jnp.sum(expo, axis=1, keepdims=True)
    acc_ref[where, :, lanes] = acc_ref[where, :, lanes] * fade + dot(expo.astype(BF16), v)


def attend_kernel(step, first, final, info, *refs):
    refs = list(refs)
    queries = [refs.pop(0) for _ in range(4)]
    own = refs.pop(0) if first else None
    others = [refs.pop(0) for _ in range(1 if final else 2)]
    if not first:
        state_in = [refs.pop(0) for _ in range(3)]
    if final:
        payloads = [refs.pop(0) for _ in range(4)]
    acc, m, l = refs[:3]
    if first:
        acc[...] = jnp.zeros_like(acc)
        m[...] = jnp.full(m.shape, LOW, F32)
        l[...] = jnp.zeros_like(l)
        bias = own[SEG : SEG + 1, :SEG].astype(F32) * LOG2E
        for j in range(4):

            def one(j=j):
                mask = None
                if j == 0:
                    r, k = iota((ROWS, SEG), 0), iota((ROWS, SEG), 1)
                    mask = (k <= r) & (r < SEG)
                for h in range(2):
                    k = own[:SEG, h * HD : (h + 1) * HD]
                    v = own[:SEG, COLS + h * HD : COLS + (h + 1) * HD]
                    attend(queries[j], k, v, bias, acc, m, l, j, h, mask)

            if j == 0:
                one()
            else:
                pl.when(info[I_X] < info[I_X + j])(one)
    else:
        for source, target in zip(state_in, (acc, m, l)):
            target[...] = source[...]
    ok = [info[I_OK + 2 * (step - 1) + i] for i in range(len(others))]
    some = ok[0] if final else ok[0] + ok[1]

    @pl.when(some > 0)
    def _():
        biases = []
        for kv, good in zip(others, ok):
            row = kv[SEG : SEG + 1, :SEG].astype(F32) * LOG2E
            biases.append(jnp.where(good > 0, row, LOW))
        bias = jnp.concatenate(biases, axis=1)
        for h in range(2):
            k = jnp.concatenate([kv[:SEG, h * HD : (h + 1) * HD] for kv in others], axis=0)
            v = jnp.concatenate([kv[:SEG, COLS + h * HD : COLS + (h + 1) * HD] for kv in others], axis=0)
            for j in range(4):
                attend(queries[j], k, v, bias, acc, m, l, j, h)

    if final:
        row = iota((16, COLS), 0)
        for j in range(4):
            tail = jnp.zeros((16, COLS), F32)
            ends = []
            for h in range(2):
                total = l[j, h]
                some_keys = total > 0.0
                total = jnp.where(some_keys, total, 1.0)
                out = acc[j, :, h * HD : (h + 1) * HD] / total
                logs = jnp.where(some_keys, m[j, h] + jnp.log2(total), LOW)
                payloads[j][:SEG, h * HD : (h + 1) * HD] = out[:SEG].astype(BF16)
                ends.append(out[SEG:])
                parts = split(jnp.transpose(logs[:SEG])[:16], 3)
                for i, part in enumerate(parts):
                    tail = jnp.where(row == 1 + 3 * h + i, part, tail)
                parts = split(wide(logs[SEG : SEG + 1], 2), 3)
                for i, part in enumerate(parts):
                    tail = jnp.where(row == 7 + 3 * h + i, part, tail)
            tail = jnp.where(row == 0, jnp.concatenate(ends, axis=1), tail)
            payloads[j][SEG:, :] = tail.astype(BF16)


STATE = [
    shape((4, ROWS, COLS), F32),
    shape((4, 2, ROWS, 128), F32),
    shape((4, 2, ROWS, 128), F32),
]


def attend_step(step, info, queries, own, others, state):
    first, final = own is not None, len(others) == 1
    ins = [info] + queries + ([own] if first else []) + others + list(state or [])
    flops = 4 * 1088 * SEG * (len(others) + (1 if first else 0)) * COLS
    if final:
        outs, scratch = [shape((ROWS, COLS), BF16)] * 4, [pltpu.VMEM(s.shape, s.dtype) for s in STATE]
    else:
        outs, scratch = STATE, []
    body = functools.partial(attend_kernel, step, first, final)
    return call(body, outs, ins, flops=flops, moved=4 << 20, scratch=scratch)


def merge_kernel(info, a, b, c, d, out):
    parts = (a, b, c, d)
    tails = [p[SEG:, :].astype(F32) for p in parts]
    weights, end_weights = [], []
    for h in range(2):
        for base, store in ((1 + 3 * h, weights), (7 + 3 * h, end_weights)):
            logs = [t[base : base + 1] + t[base + 1 : base + 2] + t[base + 2 : base + 3] for t in tails]
            peak = functools.reduce(jnp.maximum, logs)
            expo = [jnp.exp2(v - peak) for v in logs]
            whole = functools.reduce(jnp.add, expo)
            store.append([e / whole for e in expo])
    flat = weights[0] + weights[1]
    columns = jnp.transpose(jnp.concatenate(flat + [jnp.zeros((120, SEG), F32)], axis=0))
    ends = []
    for h in range(2):
        lanes = slice(h * HD, (h + 1) * HD)
        acc = jnp.zeros((SEG, HD), F32)
        end = jnp.zeros((16, HD), F32)
        for j, p in enumerate(parts):
            acc = acc + columns[:, 4 * h + j : 4 * h + j + 1] * p[:SEG, lanes].astype(F32)
            end = end + end_weights[h][j][:, :HD] * tails[j][:, lanes]
        out[:SEG, lanes] = acc.astype(BF16)
        ends.append(end)
    end = jnp.concatenate(ends, axis=1)
    out[SEG:, :] = jnp.where(iota((16, COLS), 0) == 0, end, 0.0).astype(BF16)


BLOCK = 512
TALL = 384


def output_kernel(*refs):
    attended, weights = refs[:8], refs[8:16]
    means, ids, tokens, out, coarse = refs[16:]

    @pl.when(pl.program_id(0) == 0)
    def _():
        acc = means[...]
        for a, w in zip(attended, weights):
            acc = acc + dot(a[...], w[...])
        coarse[:ROWS, :] = acc.astype(BF16)
        coarse[ROWS:, :] = jnp.zeros((TALL - ROWS, FEAT), BF16)

    base = pl.multiple_of(pl.program_id(0) * (BLOCK // 128), BLOCK // 128)
    lane = iota((128, 128), 1)
    chunks = []
    for r in range(BLOCK // 128):
        row = ids[pl.ds(base + r, 1), :].astype(F32)
        column = jnp.transpose(jnp.broadcast_to(row, (128, 128))).astype(jnp.int32)
        chunks.append(
            jnp.concatenate(
                [
                    ones_where(column == lane),
                    ones_where(column == lane + 128),
                    ones_where((column == -1) & (lane == 0)),
                ],
                axis=1,
            )
        )
    hot = jnp.concatenate(chunks, axis=0)
    picked = dot(hot, coarse[...])
    out[...] = (tokens[...].astype(F32) + picked).astype(BF16)


def output(attended, weights, means, ids, tokens):
    whole = [WHOLE] * 18
    return pl.pallas_call(
        output_kernel,
        grid=(TOK // BLOCK,),
        out_shape=shape((TOK, FEAT), BF16),
        in_specs=whole + [pl.BlockSpec((BLOCK, FEAT), lambda i: (i, 0))],
        out_specs=pl.BlockSpec((BLOCK, FEAT), lambda i: (i, 0)),
        scratch_shapes=[pltpu.VMEM((TALL, FEAT), BF16)],
        compiler_params=pltpu.CompilerParams(vmem_limit_bytes=VMEM_LIMIT),
        cost_estimate=pl.CostEstimate(flops=2 << 30, bytes_accessed=6 << 20, transcendentals=0),
    )(*attended, *weights, means, ids, tokens)


def out_weights(w_out, device_mp):
    blocks = []
    for i in range(8):
        target = np.zeros(8, np.int32)
        pairs = []
        for y in range(NY):
            for c in range(NC):
                source = sources(y, c)[i]
                target[source] = y * NC + c
                pairs.append((source, y * NC + c))
        column = jnp.asarray(target)[device_mp] * FEAT
        piece = lax.dynamic_slice_in_dim(w_out, column, FEAT, 1)
        blocks.append(piece if i == 0 else lax.ppermute(piece, "mp", pairs))
    return blocks


def shards(tokens, flags, norm_gain, w_query, w_key, w_value, w_out):
    seq, mp = lax.axis_index("seq"), lax.axis_index("mp")
    info = jnp.asarray(device_table())[seq * (NY * NC) + mp]
    edge = shape((8, FEAT + 128), F32)
    ids, head, tail = call(
        edge_kernel,
        [shape((16, 128), jnp.int32), edge, edge],
        [info, flags.reshape(16, 128), tokens],
        flops=1 << 28,
        moved=2 << 20,
        scratch=[pltpu.VMEM((16, TOK), BF16)],
    )
    count = NZ * NX
    above = lax.ppermute(head, "seq", [(i, i - 1) for i in range(1, count)])
    below = lax.ppermute(tail, "seq", [(i, i + 1) for i in range(count - 1)])
    sums, sizes = call(
        pool_kernel,
        [shape((SEG, FEAT), F32), shape((SEG, 128), F32)],
        [info, ids, tokens],
        flops=1 << 30,
        moved=2 << 20,
        scratch=[pltpu.VMEM((SEG, TOK), BF16)],
    )
    means, u, bias = call(
        norm_kernel,
        [shape((ROWS, FEAT), F32), shape((ROWS, FEAT), BF16), shape((16, FEAT), BF16)],
        [info, sums, sizes, head, above, below, norm_gain.reshape(8, FEAT)],
        moved=2 << 20,
    )
    blocks = mp_exchange(u)
    query, kv = call(
        project_kernel,
        [shape((ROWS, COLS), BF16), shape((ROWS, 2 * COLS), BF16)],
        [info] + blocks + [w_query, w_key, w_value, bias],
        flops=2 * ROWS * WIDTH * 3 * COLS,
        moved=8 << 20,
    )
    one, other = z_one(kv), z_other(kv)
    queries = [query] + [x_by(query, k) for k in (1, 2, 3)]
    w_out, query = lax.optimization_barrier((w_out, query))
    weights = out_weights(w_out, mp)
    state = attend_step(1, info, queries, kv, [one, other], None)
    for step in (2, 3):
        one, other = z_one(one), z_other(other)
        state = attend_step(step, info, queries, None, [one, other], state)
    one = z_one(one)
    partial = attend_step(4, info, queries, None, [one], state)
    partial = [partial[0]] + [x_by(partial[k], -k) for k in (1, 2, 3)]
    (attended,) = call(merge_kernel, [shape((ROWS, COLS), BF16)], [info] + partial, moved=1 << 20)
    return output(mp_exchange(attended), weights, means, ids, tokens)


def solution(mesh):
    placed = (
        P(("dp", "seq"), "mp"),
        P(("dp", "seq")),
        P(),
        P(None, "mp"),
        P(None, "mp"),
        P(None, "mp"),
        P("mp", None),
    )
    return jax.shard_map(
        shards, mesh=mesh, in_specs=placed, out_specs=P(("dp", "seq"), "mp"), check_vma=False
    )
```

```python
import functools

import jax
import jax.numpy as jnp
import numpy as np
from jax import lax
from jax.experimental import pallas as pl
from jax.experimental.pallas import tpu as pltpu
from jax.sharding import PartitionSpec as P

HD = 128
NZ, NX, NY, NC = 8, 4, 4, 2
SEG = 256
ROWS = SEG + 16
TOK = 2048
FEAT = 512
COLS = 256
WIDTH = 4096
SCORE = 1.4426950408889634 * HD**-0.5
LOG2E = 1.4426950408889634
LOW = -1e30
VMEM_LIMIT = 20 * 1024 * 1024
F32, BF16 = jnp.float32, jnp.bfloat16


def number(z, x, y, c):
    return ((z % NZ) * NX + x % NX) * (NY * NC) + (y % NY) * NC + c % NC


def everywhere():
    return [(z, x, y, c) for z in range(NZ) for x in range(NX) for y in range(NY) for c in range(NC)]


def way(c):
    return 1 if c == 0 else -1


def move(value, target):
    pairs = [(number(*d), number(*target(*d))) for d in everywhere()]
    return lax.ppermute(value, ("seq", "mp"), pairs)


def swap(value):
    return move(value, lambda z, x, y, c: (z, x, y, 1 - c))


def y_one(value):
    return move(value, lambda z, x, y, c: (z, x, y + way(c), c))


def y_other(value):
    return move(value, lambda z, x, y, c: (z, x, y - way(c), c))


def z_one(value):
    return move(value, lambda z, x, y, c: (z + way(c), x, y, c))


def z_other(value):
    return move(value, lambda z, x, y, c: (z - way(c), x, y, c))


def x_by(value, by):
    return move(value, lambda z, x, y, c: (z, x + by, y, c))


def sources(y, c):
    own = [(y, c), (y - way(c), c), (y + way(c), c), (y + 2, c)]
    o = 1 - c
    other = [(y, o), (y - way(o), o), (y + way(o), o), (y + 2, o)]
    return [((b[0] % NY) * NC + b[1]) for b in own + other]


def mp_exchange(value):
    first = y_one(value)
    second = y_other(value)
    sibling = swap(value)
    far = y_one(first)
    return [value, first, second, far, sibling, swap(first), swap(second), swap(far)]


def device_table():
    rows = []
    for z, x, y, c in everywhere():
        row = [y * NC + c] + sources(y, c)
        row += [x] + [(x - k) % NX for k in (1, 2, 3)]
        for k in (1, 2, 3, 4):
            row += [int((z - way(c) * k) % NZ < z), int((z + way(c) * k) % NZ < z)]
        for o in (c, 1 - c):
            row += [(v % NY) * NC + o for v in (y, y + way(o), y - way(o), y + 2)]
        row += [0] * (32 - len(row))
        rows.append(row)
    return np.asarray(rows, np.int32)


I_MP, I_SRC, I_X, I_OK, I_CUT = 0, 1, 9, 13, 21
SMEM = pl.BlockSpec(memory_space=pltpu.SMEM)
WHOLE = pl.BlockSpec(memory_space=pltpu.VMEM)
FAR = pl.BlockSpec(memory_space=pl.ANY)
DISTANT = pl.BlockSpec(memory_space=pltpu.HBM)


def call(body, outs, ins, flops=0, moved=0, scratch=(), aliases=None, far_in=(), far_out=(), far=FAR):
    return pl.pallas_call(
        body,
        out_shape=outs,
        in_specs=[SMEM] + [far if i in far_in else WHOLE for i in range(1, len(ins))],
        out_specs=[far if i in far_out else WHOLE for i in range(len(outs))],
        scratch_shapes=list(scratch),
        input_output_aliases=aliases or {},
        compiler_params=pltpu.CompilerParams(vmem_limit_bytes=VMEM_LIMIT),
        cost_estimate=pl.CostEstimate(flops=flops, bytes_accessed=moved, transcendentals=0),
    )(*ins)


def gate_kernel(info, *refs):
    pass


def gate(info, values, token):
    ins = [info] + list(values) + [token]
    count = len(values)
    return call(
        gate_kernel,
        [shape(v.shape, v.dtype) for v in values],
        ins,
        aliases={i + 1: i for i in range(count)},
        far_in=range(1, count + 2),
        far_out=range(count),
    )


def shape(dims, dtype):
    return jax.ShapeDtypeStruct(dims, dtype)


def dot(a, b):
    return jnp.dot(a, b, preferred_element_type=F32)


def iota(dims, axis):
    return lax.broadcasted_iota(jnp.int32, dims, axis)


def ones_where(condition):
    return jnp.where(condition, 1.0, 0.0).astype(BF16)


def edge_kernel(info, flags, tokens, ids_out, head_out, tail_out, marks):
    f = flags[...].astype(F32).astype(BF16)
    upto = ones_where(iota((128, 128), 0) <= iota((128, 128), 1))
    inside = dot(f, upto)
    rows = dot(f, jnp.ones((128, 128), BF16)).astype(BF16)
    before = dot(ones_where(iota((16, 16), 1) < iota((16, 16), 0)), rows)
    ids_out[...] = (inside + before - 1.0).astype(jnp.int32)
    wanted = jnp.where(iota((16, 128), 0) < 8, -1, SEG - 1)
    for r in range(16):
        marks[:, r * 128 : (r + 1) * 128] = ones_where(ids_out[r : r + 1, :] == wanted)
    sums = dot(marks[...], tokens[...])
    counts = dot(marks[...], jnp.ones((TOK, 128), BF16))
    head_out[:, :FEAT] = sums[:8]
    head_out[:, FEAT:] = counts[:8]
    tail_out[:, :FEAT] = sums[8:]
    tail_out[:, FEAT:] = counts[8:]


def pool_kernel(info, ids, tokens, sums_out, counts_out, hot):
    segment = iota((SEG, 128), 0)
    for r in range(16):
        hot[:, r * 128 : (r + 1) * 128] = ones_where(ids[r : r + 1, :] == segment)
    sums_out[...] = dot(hot[...], tokens[...])
    counts_out[...] = dot(hot[...], jnp.ones((TOK, 128), BF16))


def wide(column, times):
    return jnp.concatenate([column] * times, axis=1)


def split(value, parts):
    out = []
    for _ in range(parts):
        high = value.astype(BF16).astype(F32)
        out.append(high)
        value = value - high
    return out


def norm_kernel(info, sums, counts, head, above, below, gain, means_out, u_out, bias_out):
    g = gain[pl.ds(info[I_MP], 1), :]
    last = iota((SEG, 128), 0) == SEG - 1
    size = counts[...] + jnp.where(last, above[0:1, FEAT:], 0.0)
    total = sums[...] + jnp.where(iota((SEG, FEAT), 0) == SEG - 1, above[0:1, :FEAT], 0.0)
    size = jnp.maximum(size, 1.0)
    means = total / wide(size, 4)
    means_out[:SEG, :] = means
    u_out[:SEG, :] = (means * g).astype(BF16)
    squares = jnp.sum(means * means, axis=1, keepdims=True)
    squares = jnp.transpose(jnp.broadcast_to(squares, (SEG, 128)))[:16]
    high, low = split(squares, 2)
    extra_size = jnp.maximum(head[0:1, FEAT:] + below[0:1, FEAT:], 1.0)
    extra = (head[0:1, :FEAT] + below[0:1, :FEAT]) / wide(extra_size, 4)
    extra_squares = jnp.broadcast_to(jnp.sum(extra * extra, axis=1, keepdims=True), (16, SEG))
    extra_high, extra_low = split(extra_squares, 2)
    row = iota((16, FEAT), 0)
    means_out[SEG:, :] = jnp.where(row == 0, extra, 0.0)
    tail = jnp.where(row == 0, extra * g, 0.0)
    tail = jnp.where(row == 1, jnp.concatenate([high, low], axis=1), tail)
    tail = jnp.where(row == 2, jnp.concatenate([extra_high, extra_low], axis=1), tail)
    u_out[SEG:, :] = tail.astype(BF16)
    bias = jnp.log(jnp.transpose(size)[:16])
    bias_out[...] = jnp.concatenate([bias, bias], axis=1).astype(BF16)


EARLY = (0, 1, 4, 5)
LATE = (2, 3, 6, 7)


def row_scale(tail):
    squares = tail[:, :SEG] + tail[:, SEG:]
    scale = lax.rsqrt(squares / WIDTH + 1e-05)
    column = jnp.transpose(jnp.broadcast_to(scale[1:2, :], (128, SEG)))
    return scale, wide(column, 2)


def product(acc, blocks, weight, rows):
    for i, u in enumerate(blocks):
        part = dot(u[:rows, :], weight[i])
        acc = part if acc is None else acc + part
    return acc


def early_kernel(info, *refs):
    blocks, weights = refs[:4], refs[4:7]
    sums, kept, early, sems = refs[8:11], refs[11:14], refs[14:17], refs[17]
    copies = {}
    for side, (which, target) in enumerate(((EARLY, early), (LATE, kept))):
        for i in range(4):
            start = pl.multiple_of(info[I_SRC + which[i]] * FEAT, FEAT)
            for n in range(3):
                copies[side, i, n] = pltpu.make_async_copy(
                    weights[n].at[pl.ds(start, FEAT), :], target[n].at[i], sems.at[side, i, n]
                )
                copies[side, i, n].start()
    for i, u in enumerate(blocks):
        for n, rows in enumerate((ROWS, SEG, SEG)):
            copies[0, i, n].wait()
            part = dot(u[:rows, :], early[n][i])
            sums[n][...] = part if i == 0 else sums[n][...] + part
    for i in range(4):
        for n in range(3):
            copies[1, i, n].wait()


def square_rows(blocks):
    tail = jnp.zeros((16, FEAT), F32)
    for u in blocks:
        tail = tail + u[SEG:, :].astype(F32)
    return tail


def key_value_kernel(info, *refs):
    blocks, late = refs[:8], [refs[i] for i in LATE]
    w_key, w_value, keys, values, bias, kv_out = refs[8:]
    _, column = row_scale(square_rows(blocks))
    kv_out[:SEG, :COLS] = (product(keys[...], late, w_key, SEG) * column).astype(BF16)
    kv_out[:SEG, COLS:] = (product(values[...], late, w_value, SEG) * column).astype(BF16)
    kv_out[SEG:, :] = bias[...]


def query_kernel(info, *refs):
    blocks, late = refs[:8], [refs[i] for i in LATE]
    w_query, partial, q_out = refs[8:]
    scale, column = row_scale(square_rows(blocks))
    query = product(partial[...], late, w_query, ROWS)
    q_out[:SEG, :] = (query[:SEG] * column * SCORE).astype(BF16)
    extra = query[SEG:] * scale[2:3, :] * SCORE
    q_out[SEG:, :] = jnp.where(iota((16, COLS), 0) == 0, extra, 0.0).astype(BF16)


def nt_dot(a, b):
    return lax.dot_general(a, b, (((1,), (1,)), ((), ())), preferred_element_type=F32)


def attend(q, k, v, bias, acc_ref, m_ref, j, h, mask=None):
    scores = nt_dot(q[:, h * HD : (h + 1) * HD], k) + bias
    if mask is not None:
        scores = jnp.where(mask, scores, LOW)
    old = m_ref[j, h]
    peak = jnp.maximum(old, jnp.max(scores, axis=1, keepdims=True))
    expo = jnp.exp2(scores - wide(peak, scores.shape[1] // 128))
    if mask is not None:
        expo = jnp.where(mask, expo, 0.0)
    m_ref[j, h] = peak
    acc_ref[j, h] = acc_ref[j, h] * wide(jnp.exp2(old - peak), 2) + dot(expo.astype(BF16), v)


def keys_of(blocks, h):
    return jnp.concatenate([kv[:SEG, h * HD : (h + 1) * HD] for kv in blocks], axis=0)


def values_of(blocks, h):
    lanes = slice(COLS + h * HD, COLS + (h + 1) * HD)
    values = jnp.concatenate([kv[:SEG, lanes] for kv in blocks], axis=0)
    return jnp.concatenate([values, jnp.ones(values.shape, BF16)], axis=1)


def attend_kernel(step, first, final, info, *refs):
    refs = list(refs)
    queries = [refs.pop(0) for _ in range(4)]
    own = refs.pop(0) if first else None
    others = [refs.pop(0) for _ in range(1 if final else 2)]
    if not first:
        state_in = [refs.pop(0) for _ in range(2)]
    if final:
        payloads = [refs.pop(0) for _ in range(4)]
        acc, m = state_in
    else:
        acc, m, done = refs[:3]
        done[...] = jnp.zeros_like(done)
    if first:
        acc[...] = jnp.zeros_like(acc)
        m[...] = jnp.full(m.shape, LOW, F32)
        bias = own[SEG : SEG + 1, :SEG].astype(F32) * LOG2E
        for j in range(4):

            def one(j=j):
                mask = None
                if j == 0:
                    r, k = iota((ROWS, SEG), 0), iota((ROWS, SEG), 1)
                    mask = (k <= r) & (r < SEG)
                for h in range(2):
                    attend(queries[j], keys_of([own], h), values_of([own], h), bias, acc, m, j, h, mask)

            if j == 0:
                one()
            else:
                pl.when(info[I_X] < info[I_X + j])(one)
    ok = [info[I_OK + 2 * (step - 1) + i] for i in range(len(others))]
    some = ok[0] if final else ok[0] + ok[1]

    @pl.when(some > 0)
    def _():
        biases = []
        for kv, good in zip(others, ok):
            row = kv[SEG : SEG + 1, :SEG].astype(F32) * LOG2E
            biases.append(jnp.where(good > 0, row, LOW))
        bias = jnp.concatenate(biases, axis=1)
        for h in range(2):
            k, v = keys_of(others, h), values_of(others, h)
            for j in range(4):
                attend(queries[j], k, v, bias, acc, m, j, h)

    if final:
        row = iota((16, COLS), 0)
        for j in range(4):
            tail = jnp.zeros((16, COLS), F32)
            ends = []
            for h in range(2):
                total = acc[j, h][:, HD:]
                some_keys = total > 0.0
                total = jnp.where(some_keys, total, 1.0)
                out = acc[j, h][:, :HD] / total
                logs = jnp.where(some_keys, m[j, h] + jnp.log2(total), LOW)
                payloads[j][:SEG, h * HD : (h + 1) * HD] = out[:SEG].astype(BF16)
                ends.append(out[SEG:])
                parts = split(jnp.transpose(logs[:SEG])[:16], 3)
                for i, part in enumerate(parts):
                    tail = jnp.where(row == 1 + 3 * h + i, part, tail)
                parts = split(wide(logs[SEG : SEG + 1], 2), 3)
                for i, part in enumerate(parts):
                    tail = jnp.where(row == 7 + 3 * h + i, part, tail)
            tail = jnp.where(row == 0, jnp.concatenate(ends, axis=1), tail)
            payloads[j][SEG:, :] = tail.astype(BF16)


STATE = [shape((4, 2, ROWS, 2 * HD), F32), shape((4, 2, ROWS, HD), F32), shape((8, 128), F32)]


def attend_step(step, info, queries, own, others, state):
    first, final = own is not None, len(others) == 1
    ins = [info] + queries + ([own] if first else []) + others + list(state or [])
    flops = 4 * 1088 * SEG * (len(others) + (1 if first else 0)) * COLS
    body = functools.partial(attend_kernel, step, first, final)
    if final:
        outs = [shape((ROWS, COLS), BF16)] * 4 + STATE[:2]
        aliases = {len(ins) - 2: 4, len(ins) - 1: 5}

        def body(*refs):
            refs = list(refs)
            payloads, state = refs[-6:-2], refs[-2:]
            attend_kernel(step, first, final, *refs[:-8], *state, *payloads)

        return call(body, outs, ins, flops=flops, moved=4 << 20, aliases=aliases)[:4]
    aliases = {} if first else {len(ins) - 2: 0, len(ins) - 1: 1}
    return call(body, STATE, ins, flops=flops, moved=4 << 20, aliases=aliases)


def merge_kernel(info, a, b, c, d, out):
    parts = (a, b, c, d)
    tails = [p[SEG:, :].astype(F32) for p in parts]
    weights, end_weights = [], []
    for h in range(2):
        for base, store in ((1 + 3 * h, weights), (7 + 3 * h, end_weights)):
            logs = [t[base : base + 1] + t[base + 1 : base + 2] + t[base + 2 : base + 3] for t in tails]
            peak = functools.reduce(jnp.maximum, logs)
            expo = [jnp.exp2(v - peak) for v in logs]
            whole = functools.reduce(jnp.add, expo)
            store.append([e / whole for e in expo])
    flat = weights[0] + weights[1]
    columns = jnp.transpose(jnp.concatenate(flat + [jnp.zeros((120, SEG), F32)], axis=0))
    ends = []
    for h in range(2):
        lanes = slice(h * HD, (h + 1) * HD)
        acc = jnp.zeros((SEG, HD), F32)
        end = jnp.zeros((16, HD), F32)
        for j, p in enumerate(parts):
            acc = acc + columns[:, 4 * h + j : 4 * h + j + 1] * p[:SEG, lanes].astype(F32)
            end = end + end_weights[h][j][:, :HD] * tails[j][:, lanes]
        out[:SEG, lanes] = acc.astype(BF16)
        ends.append(end)
    end = jnp.concatenate(ends, axis=1)
    out[SEG:, :] = jnp.where(iota((16, COLS), 0) == 0, end, 0.0).astype(BF16)


BLOCK = 512
TALL = 384
PAIR = (0, 1, 2, 3, 0, 2, 1, 3)


def output_kernel(*refs):
    attended, weights = refs[:8], refs[8:12]
    means, ids, tokens, out, coarse = refs[12:]

    @pl.when(pl.program_id(0) == 0)
    def _():
        acc = means[...]
        for i, a in enumerate(attended):
            acc = acc + dot(a[...], weights[PAIR[i]][i // 4])
        coarse[:ROWS, :] = acc.astype(BF16)
        coarse[ROWS:, :] = jnp.zeros((TALL - ROWS, FEAT), BF16)

    base = pl.multiple_of(pl.program_id(0) * (BLOCK // 128), BLOCK // 128)
    lane = iota((128, 128), 1)
    chunks = []
    for r in range(BLOCK // 128):
        row = ids[pl.ds(base + r, 1), :].astype(F32)
        column = jnp.transpose(jnp.broadcast_to(row, (128, 128))).astype(jnp.int32)
        chunks.append(
            jnp.concatenate(
                [
                    ones_where(column == lane),
                    ones_where(column == lane + 128),
                    ones_where((column == -1) & (lane == 0)),
                ],
                axis=1,
            )
        )
    hot = jnp.concatenate(chunks, axis=0)
    picked = dot(hot, coarse[...])
    out[...] = (tokens[...].astype(F32) + picked).astype(BF16)


def output(attended, weights, means, ids, tokens):
    whole = [WHOLE] * 14
    return pl.pallas_call(
        output_kernel,
        grid=(TOK // BLOCK,),
        out_shape=shape((TOK, FEAT), BF16),
        in_specs=whole + [pl.BlockSpec((BLOCK, FEAT), lambda i: (i, 0))],
        out_specs=pl.BlockSpec((BLOCK, FEAT), lambda i: (i, 0)),
        scratch_shapes=[pltpu.VMEM((TALL, FEAT), BF16)],
        compiler_params=pltpu.CompilerParams(vmem_limit_bytes=VMEM_LIMIT),
        cost_estimate=pl.CostEstimate(flops=2 << 30, bytes_accessed=6 << 20, transcendentals=0),
    )(*attended, *weights, means, ids, tokens)


def cut_kernel(info, w_out, mine, sibling, sems):
    copies = []
    for i in range(4):
        for side, out in enumerate((mine, sibling)):
            start = pl.multiple_of(info[I_CUT + 4 * side + i] * FEAT, FEAT)
            copies.append(pltpu.make_async_copy(w_out.at[:, pl.ds(start, FEAT)], out.at[i], sems.at[side, i]))
            copies[-1].start()
    for copy in copies:
        copy.wait()


def pair_kernel(info, *refs):
    sources, outs, sems = refs[:2], refs[2:6], refs[6]
    copies = []
    for i, out in enumerate(outs):
        for side, source in enumerate(sources):
            copies.append(pltpu.make_async_copy(source.at[i], out.at[side], sems.at[side, i]))
            copies[-1].start()
    for copy in copies:
        copy.wait()


def y_far(value):
    return move(value, lambda z, x, y, c: (z, x, y + 2, c))


def shards(tokens, flags, norm_gain, w_query, w_key, w_value, w_out):
    seq, mp = lax.axis_index("seq"), lax.axis_index("mp")
    info = jnp.asarray(device_table())[seq * (NY * NC) + mp]
    edge = shape((8, FEAT + 128), F32)
    ids, head, tail = call(
        edge_kernel,
        [shape((16, 128), jnp.int32), edge, edge],
        [info, flags.reshape(16, 128), tokens],
        flops=1 << 28,
        moved=2 << 20,
        scratch=[pltpu.VMEM((16, TOK), BF16)],
    )
    count = NZ * NX
    above = lax.ppermute(head, "seq", [(i, i - 1) for i in range(1, count)])
    below = lax.ppermute(tail, "seq", [(i, i + 1) for i in range(count - 1)])
    sums, sizes = call(
        pool_kernel,
        [shape((SEG, FEAT), F32), shape((SEG, 128), F32)],
        [info, ids, tokens],
        flops=1 << 30,
        moved=2 << 20,
        scratch=[pltpu.VMEM((SEG, TOK), BF16)],
    )
    means, u, bias = call(
        norm_kernel,
        [shape((ROWS, FEAT), F32), shape((ROWS, FEAT), BF16), shape((16, FEAT), BF16)],
        [info, sums, sizes, head, above, below, norm_gain.reshape(8, FEAT)],
        moved=2 << 20,
    )
    cut = shape((4, SEG, FEAT), BF16)
    sems = [pltpu.SemaphoreType.DMA((2, 4))]
    mine, theirs = call(
        cut_kernel, [cut, cut], [info, w_out], moved=4 << 20, scratch=sems, far_in=(1,), far_out=(0, 1), far=DISTANT
    )
    first, sibling, second = y_one(u), swap(u), y_other(u)
    part, part_query = shape((SEG, COLS), F32), shape((ROWS, COLS), F32)
    kept = shape((4, FEAT, COLS), BF16)
    across = swap(first)
    queried, keyed, valued, *late = call(
        early_kernel,
        [part_query, part, part] + [kept] * 3,
        [info, u, first, sibling, across, w_query, w_key, w_value, mine],
        flops=ROWS * WIDTH * 3 * COLS,
        moved=8 << 20,
        scratch=[pltpu.VMEM((4, FEAT, COLS), BF16)] * 3 + [pltpu.SemaphoreType.DMA((2, 4, 3))],
        far_in=(5, 6, 7, 8),
    )
    (far,) = gate(info, [y_one(first)], queried)
    theirs = swap(theirs)
    blocks = [u, first, second, far, sibling, across, swap(second), swap(far)]
    (kv,) = call(
        key_value_kernel,
        [shape((ROWS, 2 * COLS), BF16)],
        [info] + blocks + [late[1], late[2], keyed, valued, bias],
        flops=ROWS * WIDTH * 2 * COLS,
        moved=4 << 20,
    )
    (query,) = call(
        query_kernel,
        [shape((ROWS, COLS), BF16)],
        [info] + blocks + [late[0], queried],
        flops=ROWS * WIDTH * COLS,
        moved=2 << 20,
    )
    one, other = z_one(kv), z_other(kv)
    queries = [query] + [x_by(query, k) for k in (1, 2, 3)]
    pair = shape((2, SEG, FEAT), BF16)
    pairs = call(
        pair_kernel,
        [pair] * 4,
        [info, mine, theirs],
        moved=4 << 20,
        scratch=sems,
        far_in=(1, 2),
        far_out=range(4),
        far=DISTANT,
    )
    queries[0], *pairs = gate(info, [query, *pairs], info)
    weights = [pairs[0], y_one(pairs[1]), y_other(pairs[2]), y_far(pairs[3])]
    *state, done = attend_step(1, info, queries, kv, [one, other], None)
    one, other = gate(info, [z_one(one), z_other(other)], done)
    *state, done = attend_step(2, info, queries, None, [one, other], state)
    one, other, weights[1], weights[2] = gate(info, [z_one(one), z_other(other), weights[1], weights[2]], done)
    *state, done = attend_step(3, info, queries, None, [one, other], state)
    one, weights[3] = gate(info, [z_one(one), weights[3]], done)
    partial = attend_step(4, info, queries, None, [one], state)
    partial = [partial[0]] + [x_by(partial[k], -k) for k in (1, 2, 3)]
    (attended,) = call(merge_kernel, [shape((ROWS, COLS), BF16)], [info] + partial, moved=1 << 20)
    return output(mp_exchange(attended), weights, means, ids, tokens)


def solution(mesh):
    placed = (
        P(("dp", "seq"), "mp"),
        P(("dp", "seq")),
        P(),
        P(None, "mp"),
        P(None, "mp"),
        P(None, "mp"),
        P("mp", None),
    )
    return jax.shard_map(
        shards, mesh=mesh, in_specs=placed, out_specs=P(("dp", "seq"), "mp"), check_vma=False
    )
```

```python
import functools

import jax
import jax.numpy as jnp
import numpy as np
from jax import lax
from jax.experimental import pallas as pl
from jax.experimental.pallas import tpu as pltpu
from jax.sharding import PartitionSpec as P

HD = 128
NZ, NX, NY, NC = 8, 4, 4, 2
SEG = 256
ROWS = SEG + 16
TOK = 2048
FEAT = 512
COLS = 256
WIDTH = 4096
SCORE = 1.4426950408889634 * HD**-0.5
LOG2E = 1.4426950408889634
LOW = -1e30
VMEM_LIMIT = 20 * 1024 * 1024
ROOM = 48 * 1024 * 1024
F32, BF16 = jnp.float32, jnp.bfloat16


def number(z, x, y, c):
    return ((z % NZ) * NX + x % NX) * (NY * NC) + (y % NY) * NC + c % NC


def everywhere():
    return [(z, x, y, c) for z in range(NZ) for x in range(NX) for y in range(NY) for c in range(NC)]


def way(c):
    return 1 if c == 0 else -1


def move(value, target):
    pairs = [(number(*d), number(*target(*d))) for d in everywhere()]
    return lax.ppermute(value, ("seq", "mp"), pairs)


def swap(value):
    return move(value, lambda z, x, y, c: (z, x, y, 1 - c))


def y_one(value):
    return move(value, lambda z, x, y, c: (z, x, y + way(c), c))


def y_other(value):
    return move(value, lambda z, x, y, c: (z, x, y - way(c), c))


def z_one(value):
    return move(value, lambda z, x, y, c: (z + way(c), x, y, c))


def z_other(value):
    return move(value, lambda z, x, y, c: (z - way(c), x, y, c))


def x_by(value, by):
    return move(value, lambda z, x, y, c: (z, x + by, y, c))


def sources(y, c):
    own = [(y, c), (y - way(c), c), (y + way(c), c), (y + 2, c)]
    o = 1 - c
    other = [(y, o), (y - way(o), o), (y + way(o), o), (y + 2, o)]
    return [((b[0] % NY) * NC + b[1]) for b in own + other]


def mp_exchange(value):
    first = y_one(value)
    second = y_other(value)
    sibling = swap(value)
    far = y_one(first)
    return [value, first, second, far, sibling, swap(first), swap(second), swap(far)]


def device_table():
    rows = []
    for z, x, y, c in everywhere():
        row = [y * NC + c] + sources(y, c)
        row += [x] + [(x - k) % NX for k in (1, 2, 3)]
        for k in (1, 2, 3, 4):
            row += [int((z - way(c) * k) % NZ < z), int((z + way(c) * k) % NZ < z)]
        for o in (c, 1 - c):
            row += [(v % NY) * NC + o for v in (y, y + way(o), y - way(o), y + 2)]
        row += [0] * (32 - len(row))
        rows.append(row)
    return np.asarray(rows, np.int32)


I_MP, I_SRC, I_X, I_OK, I_CUT = 0, 1, 9, 13, 21
SMEM = pl.BlockSpec(memory_space=pltpu.SMEM)
WHOLE = pl.BlockSpec(memory_space=pltpu.VMEM)
FAR = pl.BlockSpec(memory_space=pl.ANY)
DISTANT = pl.BlockSpec(memory_space=pltpu.HBM)


def call(body, outs, ins, flops=0, moved=0, scratch=(), aliases=None, far_in=(), far_out=(), far=FAR, scalars=0, room=VMEM_LIMIT):
    return pl.pallas_call(
        body,
        out_shape=outs,
        in_specs=[SMEM if i == scalars else far if i in far_in else WHOLE for i in range(len(ins))],
        out_specs=[far if i in far_out else WHOLE for i in range(len(outs))],
        scratch_shapes=list(scratch),
        input_output_aliases=aliases or {},
        compiler_params=pltpu.CompilerParams(vmem_limit_bytes=room),
        cost_estimate=pl.CostEstimate(flops=flops, bytes_accessed=moved, transcendentals=0),
    )(*ins)


def gate_kernel(info, *refs):
    pass


def gate(info, values, token):
    ins = [info] + list(values) + [token]
    count = len(values)
    return call(
        gate_kernel,
        [shape(v.shape, v.dtype) for v in values],
        ins,
        aliases={i + 1: i for i in range(count)},
        far_in=range(1, count + 2),
        far_out=range(count),
    )


def shape(dims, dtype):
    return jax.ShapeDtypeStruct(dims, dtype)


def dot(a, b):
    return jnp.dot(a, b, preferred_element_type=F32)


def iota(dims, axis):
    return lax.broadcasted_iota(jnp.int32, dims, axis)


def ones_where(condition):
    return jnp.where(condition, 1.0, 0.0).astype(BF16)


def edge_kernel(flags, tokens, ids_out, head_out, tail_out, marks):
    f = flags[...].astype(F32).astype(BF16)
    upto = ones_where(iota((128, 128), 0) <= iota((128, 128), 1))
    inside = dot(f, upto)
    rows = dot(f, jnp.ones((128, 128), BF16)).astype(BF16)
    before = dot(ones_where(iota((16, 16), 1) < iota((16, 16), 0)), rows)
    ids_out[...] = (inside + before - 1.0).astype(jnp.int32)
    wanted = jnp.where(iota((16, 128), 0) < 8, -1, SEG - 1)
    for r in range(16):
        marks[:, r * 128 : (r + 1) * 128] = ones_where(ids_out[r : r + 1, :] == wanted)
    sums = dot(marks[...], tokens[...])
    counts = dot(marks[...], jnp.ones((TOK, 128), BF16))
    head_out[:, :FEAT] = sums[:8]
    head_out[:, FEAT:] = counts[:8]
    tail_out[:, :FEAT] = sums[8:]
    tail_out[:, FEAT:] = counts[8:]


def pool_kernel(ids, tokens, sums_out, counts_out, hot):
    segment = iota((SEG, 128), 0)
    for r in range(16):
        hot[:, r * 128 : (r + 1) * 128] = ones_where(ids[r : r + 1, :] == segment)
    sums_out[...] = dot(hot[...], tokens[...])
    counts_out[...] = dot(hot[...], jnp.ones((TOK, 128), BF16))


def wide(column, times):
    return jnp.concatenate([column] * times, axis=1)


def split(value, parts):
    out = []
    for _ in range(parts):
        high = value.astype(BF16).astype(F32)
        out.append(high)
        value = value - high
    return out


def norm_kernel(info, sums, counts, head, above, below, gain, means_out, u_out, bias_out):
    g = gain[pl.ds(info[I_MP], 1), :]
    last = iota((SEG, 128), 0) == SEG - 1
    size = counts[...] + jnp.where(last, above[0:1, FEAT:], 0.0)
    total = sums[...] + jnp.where(iota((SEG, FEAT), 0) == SEG - 1, above[0:1, :FEAT], 0.0)
    size = jnp.maximum(size, 1.0)
    means = total / wide(size, 4)
    means_out[:SEG, :] = means
    u_out[:SEG, :] = (means * g).astype(BF16)
    squares = jnp.sum(means * means, axis=1, keepdims=True)
    squares = jnp.transpose(jnp.broadcast_to(squares, (SEG, 128)))[:16]
    high, low = split(squares, 2)
    extra_size = jnp.maximum(head[0:1, FEAT:] + below[0:1, FEAT:], 1.0)
    extra = (head[0:1, :FEAT] + below[0:1, :FEAT]) / wide(extra_size, 4)
    extra_squares = jnp.broadcast_to(jnp.sum(extra * extra, axis=1, keepdims=True), (16, SEG))
    extra_high, extra_low = split(extra_squares, 2)
    row = iota((16, FEAT), 0)
    means_out[SEG:, :] = jnp.where(row == 0, extra, 0.0)
    tail = jnp.where(row == 0, extra * g, 0.0)
    tail = jnp.where(row == 1, jnp.concatenate([high, low], axis=1), tail)
    tail = jnp.where(row == 2, jnp.concatenate([extra_high, extra_low], axis=1), tail)
    u_out[SEG:, :] = tail.astype(BF16)
    bias = jnp.log(jnp.transpose(size)[:16])
    bias_out[...] = jnp.concatenate([bias, bias], axis=1).astype(BF16)


EARLY = (0, 1, 4, 5)
LATE = (2, 3, 6, 7)


def row_scale(tail):
    squares = tail[:, :SEG] + tail[:, SEG:]
    scale = lax.rsqrt(squares / WIDTH + 1e-05)
    column = jnp.transpose(jnp.broadcast_to(scale[1:2, :], (128, SEG)))
    return scale, wide(column, 2)


def product(acc, blocks, weight, rows):
    for i, u in enumerate(blocks):
        acc = acc + dot(u[:rows, :], weight[i])
    return acc


def early_kernel(info, *refs):
    blocks, weights = refs[:4], refs[4:7]
    sums, kept, early, sems = refs[7:10], refs[10:13], refs[13:16], refs[16]
    copies = {}
    for side, (which, target) in enumerate(((EARLY, early), (LATE, kept))):
        for i in range(4):
            start = pl.multiple_of(info[I_SRC + which[i]] * FEAT, FEAT)
            for n in range(3):
                copies[side, i, n] = pltpu.make_async_copy(
                    weights[n].at[pl.ds(start, FEAT), :], target[n].at[i], sems.at[side, i, n]
                )
                copies[side, i, n].start()
    for i, u in enumerate(blocks):
        for n, rows in enumerate((ROWS, SEG, SEG)):
            copies[0, i, n].wait()
            part = dot(u[:rows, :], early[n][i])
            sums[n][...] = part if i == 0 else sums[n][...] + part
    for i in range(4):
        for n in range(3):
            copies[1, i, n].wait()


def square_rows(blocks):
    tail = jnp.zeros((16, FEAT), F32)
    for u in blocks:
        tail = tail + u[SEG:, :].astype(F32)
    return tail


def key_value_kernel(info, *refs):
    blocks, late = refs[:8], [refs[i] for i in LATE]
    w_key, w_value, keys, values, bias, kv_out = refs[8:]
    _, column = row_scale(square_rows(blocks))
    kv_out[:SEG, :COLS] = (product(keys[...], late, w_key, SEG) * column).astype(BF16)
    kv_out[:SEG, COLS:] = (product(values[...], late, w_value, SEG) * column).astype(BF16)
    kv_out[SEG:, :] = bias[...]


def query_kernel(info, *refs):
    blocks, late = refs[:8], [refs[i] for i in LATE]
    w_query, partial, q_out = refs[8:]
    scale, column = row_scale(square_rows(blocks))
    query = product(partial[...], late, w_query, ROWS)
    q_out[:SEG, :] = (query[:SEG] * column * SCORE).astype(BF16)
    extra = query[SEG:] * scale[2:3, :] * SCORE
    q_out[SEG:, :] = jnp.where(iota((16, COLS), 0) == 0, extra, 0.0).astype(BF16)


def nt_dot(a, b):
    return lax.dot_general(a, b, (((1,), (1,)), ((), ())), preferred_element_type=F32)


def attend(q, k, v, bias, acc_ref, m_ref, j, h, mask=None):
    scores = nt_dot(q[:, h * HD : (h + 1) * HD], k) + bias
    if mask is not None:
        scores = jnp.where(mask, scores, LOW)
    old = m_ref[j, h]
    peak = jnp.maximum(old, jnp.max(scores, axis=1, keepdims=True))
    expo = jnp.exp2(scores - wide(peak, scores.shape[1] // 128))
    if mask is not None:
        expo = jnp.where(mask, expo, 0.0)
    m_ref[j, h] = peak
    acc_ref[j, h] = acc_ref[j, h] * wide(jnp.exp2(old - peak), 2) + dot(expo.astype(BF16), v)


def keys_of(blocks, h):
    return jnp.concatenate([kv[:SEG, h * HD : (h + 1) * HD] for kv in blocks], axis=0)


def values_of(blocks, h):
    lanes = slice(COLS + h * HD, COLS + (h + 1) * HD)
    values = jnp.concatenate([kv[:SEG, lanes] for kv in blocks], axis=0)
    return jnp.concatenate([values, jnp.ones(values.shape, BF16)], axis=1)


def attend_kernel(step, first, final, info, *refs):
    refs = list(refs)
    queries = [refs.pop(0) for _ in range(4)]
    own = refs.pop(0) if first else None
    others = [refs.pop(0) for _ in range(1 if final else 2)]
    if not final:
        refs = refs[1:]
    if not first:
        state_in = [refs.pop(0) for _ in range(2)]
    if final:
        payloads = [refs.pop(0) for _ in range(4)]
        acc, m = state_in
    else:
        acc, m, done = refs[:3]
        done[...] = jnp.zeros_like(done)
    if first:
        acc[...] = jnp.zeros_like(acc)
        m[...] = jnp.full(m.shape, LOW, F32)
        bias = own[SEG : SEG + 1, :SEG].astype(F32) * LOG2E
        for j in range(4):

            def one(j=j):
                mask = None
                if j == 0:
                    r, k = iota((ROWS, SEG), 0), iota((ROWS, SEG), 1)
                    mask = (k <= r) & (r < SEG)
                for h in range(2):
                    attend(queries[j], keys_of([own], h), values_of([own], h), bias, acc, m, j, h, mask)

            if j == 0:
                one()
            else:
                pl.when(info[I_X] < info[I_X + j])(one)
    ok = [info[I_OK + 2 * (step - 1) + i] for i in range(len(others))]
    some = ok[0] if final else ok[0] + ok[1]

    @pl.when(some > 0)
    def _():
        biases = []
        for kv, good in zip(others, ok):
            row = kv[SEG : SEG + 1, :SEG].astype(F32) * LOG2E
            biases.append(jnp.where(good > 0, row, LOW))
        bias = jnp.concatenate(biases, axis=1)
        for h in range(2):
            k, v = keys_of(others, h), values_of(others, h)
            for j in range(4):
                attend(queries[j], k, v, bias, acc, m, j, h)

    if final:
        row = iota((16, COLS), 0)
        for j in range(4):
            tail = jnp.zeros((16, COLS), F32)
            ends = []
            for h in range(2):
                total = acc[j, h][:, HD:]
                some_keys = total > 0.0
                total = jnp.where(some_keys, total, 1.0)
                out = acc[j, h][:, :HD] / total
                logs = jnp.where(some_keys, m[j, h] + jnp.log2(total), LOW)
                payloads[j][:SEG, h * HD : (h + 1) * HD] = out[:SEG].astype(BF16)
                ends.append(out[SEG:])
                parts = split(jnp.transpose(logs[:SEG])[:16], 3)
                for i, part in enumerate(parts):
                    tail = jnp.where(row == 1 + 3 * h + i, part, tail)
                parts = split(wide(logs[SEG : SEG + 1], 2), 3)
                for i, part in enumerate(parts):
                    tail = jnp.where(row == 7 + 3 * h + i, part, tail)
            tail = jnp.where(row == 0, jnp.concatenate(ends, axis=1), tail)
            payloads[j][SEG:, :] = tail.astype(BF16)


STATE = [shape((4, 2, ROWS, 2 * HD), F32), shape((4, 2, ROWS, HD), F32), shape((8, 128), F32)]


def attend_step(step, info, queries, own, others, state, ahead=None):
    first, final = own is not None, len(others) == 1
    ins = [info] + queries + ([own] if first else []) + others + ([] if final else [ahead]) + list(state or [])
    flops = 4 * 1088 * SEG * (len(others) + (1 if first else 0)) * COLS
    body = functools.partial(attend_kernel, step, first, final)
    if final:
        outs = [shape((ROWS, COLS), BF16)] * 4 + STATE[:2]
        aliases = {len(ins) - 2: 4, len(ins) - 1: 5}

        def body(*refs):
            refs = list(refs)
            payloads, state = refs[-6:-2], refs[-2:]
            attend_kernel(step, first, final, *refs[:-8], *state, *payloads)

        return call(body, outs, ins, flops=flops, moved=4 << 20, aliases=aliases)[:4]
    aliases = {} if first else {len(ins) - 2: 0, len(ins) - 1: 1}
    ignored = 5 + len(others) + (1 if first else 0)
    return call(body, STATE, ins, flops=flops, moved=4 << 20, aliases=aliases, far_in=(ignored,))


def merge_kernel(info, a, b, c, d, out):
    parts = (a, b, c, d)
    tails = [p[SEG:, :].astype(F32) for p in parts]
    weights, end_weights = [], []
    for h in range(2):
        for base, store in ((1 + 3 * h, weights), (7 + 3 * h, end_weights)):
            logs = [t[base : base + 1] + t[base + 1 : base + 2] + t[base + 2 : base + 3] for t in tails]
            peak = functools.reduce(jnp.maximum, logs)
            expo = [jnp.exp2(v - peak) for v in logs]
            whole = functools.reduce(jnp.add, expo)
            store.append([e / whole for e in expo])
    flat = weights[0] + weights[1]
    columns = jnp.transpose(jnp.concatenate(flat + [jnp.zeros((120, SEG), F32)], axis=0))
    ends = []
    for h in range(2):
        lanes = slice(h * HD, (h + 1) * HD)
        acc = jnp.zeros((SEG, HD), F32)
        end = jnp.zeros((16, HD), F32)
        for j, p in enumerate(parts):
            acc = acc + columns[:, 4 * h + j : 4 * h + j + 1] * p[:SEG, lanes].astype(F32)
            end = end + end_weights[h][j][:, :HD] * tails[j][:, lanes]
        out[:SEG, lanes] = acc.astype(BF16)
        ends.append(end)
    end = jnp.concatenate(ends, axis=1)
    out[SEG:, :] = jnp.where(iota((16, COLS), 0) == 0, end, 0.0).astype(BF16)


BLOCK = 512
TALL = 384
PAIR = (0, 1, 2, 3, 0, 2, 1, 3)


def output_kernel(*refs):
    attended, weights = refs[:8], refs[8:12]
    means, ids, tokens, out, coarse = refs[12:]

    @pl.when(pl.program_id(0) == 0)
    def _():
        acc = means[...]
        for i, a in enumerate(attended):
            acc = acc + dot(a[...], weights[PAIR[i]][i // 4])
        coarse[:ROWS, :] = acc.astype(BF16)
        coarse[ROWS:, :] = jnp.zeros((TALL - ROWS, FEAT), BF16)

    base = pl.multiple_of(pl.program_id(0) * (BLOCK // 128), BLOCK // 128)
    lane = iota((128, 128), 1)
    chunks = []
    for r in range(BLOCK // 128):
        row = ids[pl.ds(base + r, 1), :].astype(F32)
        column = jnp.transpose(jnp.broadcast_to(row, (128, 128))).astype(jnp.int32)
        chunks.append(
            jnp.concatenate(
                [
                    ones_where(column == lane),
                    ones_where(column == lane + 128),
                    ones_where((column == -1) & (lane == 0)),
                ],
                axis=1,
            )
        )
    hot = jnp.concatenate(chunks, axis=0)
    picked = dot(hot, coarse[...])
    out[...] = (tokens[...].astype(F32) + picked).astype(BF16)


def output(attended, weights, means, ids, tokens):
    whole = [WHOLE] * 14
    return pl.pallas_call(
        output_kernel,
        grid=(TOK // BLOCK,),
        out_shape=shape((TOK, FEAT), BF16),
        in_specs=whole + [pl.BlockSpec((BLOCK, FEAT), lambda i: (i, 0))],
        out_specs=pl.BlockSpec((BLOCK, FEAT), lambda i: (i, 0)),
        scratch_shapes=[pltpu.VMEM((TALL, FEAT), BF16)],
        compiler_params=pltpu.CompilerParams(vmem_limit_bytes=VMEM_LIMIT),
        cost_estimate=pl.CostEstimate(flops=2 << 30, bytes_accessed=6 << 20, transcendentals=0),
    )(*attended, *weights, means, ids, tokens)


def cut_kernel(info, w_out, _, mine, sibling, sems):
    copies = []
    for i in range(4):
        for side, out in enumerate((mine, sibling)):
            start = pl.multiple_of(info[I_CUT + 4 * side + i] * FEAT, FEAT)
            copies.append(pltpu.make_async_copy(w_out.at[:, pl.ds(start, FEAT)], out.at[i], sems.at[side, i]))
            copies[-1].start()
    for copy in copies:
        copy.wait()


def pair_kernel(info, *refs):
    sources, outs, sems = refs[:2], refs[3:7], refs[7]
    copies = []
    for i, out in enumerate(outs):
        for side, source in enumerate(sources):
            copies.append(pltpu.make_async_copy(source.at[i], out.at[side], sems.at[side, i]))
            copies[-1].start()
    for copy in copies:
        copy.wait()


def y_far(value):
    return move(value, lambda z, x, y, c: (z, x, y + 2, c))


def shards(tokens, flags, norm_gain, w_query, w_key, w_value, w_out):
    seq, mp = lax.axis_index("seq"), lax.axis_index("mp")
    info = jnp.asarray(device_table())[seq * (NY * NC) + mp]
    edge = shape((8, FEAT + 128), F32)
    ids, head, tail = call(
        edge_kernel,
        [shape((16, 128), jnp.int32), edge, edge],
        [flags.reshape(16, 128), tokens],
        scalars=None,
        flops=1 << 28,
        moved=2 << 20,
        scratch=[pltpu.VMEM((16, TOK), BF16)],
    )
    count = NZ * NX
    above = lax.ppermute(head, "seq", [(i, i - 1) for i in range(1, count)])
    below = lax.ppermute(tail, "seq", [(i, i + 1) for i in range(count - 1)])
    sums, sizes = call(
        pool_kernel,
        [shape((SEG, FEAT), F32), shape((SEG, 128), F32)],
        [ids, tokens],
        scalars=None,
        flops=1 << 30,
        moved=2 << 20,
        scratch=[pltpu.VMEM((SEG, TOK), BF16)],
    )
    means, u, bias = call(
        norm_kernel,
        [shape((ROWS, FEAT), F32), shape((ROWS, FEAT), BF16), shape((16, FEAT), BF16)],
        [info, sums, sizes, head, above, below, norm_gain.reshape(8, FEAT)],
    )
    first, sibling, second = y_one(u), swap(u), y_other(u)
    across, far = swap(first), y_one(first)
    part, part_query = shape((SEG, COLS), F32), shape((ROWS, COLS), F32)
    kept = shape((4, FEAT, COLS), BF16)
    queried, keyed, valued, *late = call(
        early_kernel,
        [part_query, part, part] + [kept] * 3,
        [info, u, first, sibling, across, w_query, w_key, w_value],
        scratch=[pltpu.VMEM((4, FEAT, COLS), BF16)] * 3 + [pltpu.SemaphoreType.DMA((2, 4, 3))],
        far_in=(5, 6, 7),
        room=ROOM,
    )
    cut = shape((4, SEG, FEAT), BF16)
    sems = [pltpu.SemaphoreType.DMA((2, 4))]
    mine, theirs = call(
        cut_kernel, [cut, cut], [info, w_out, second], scratch=sems, far_in=(1, 2), far_out=(0, 1), room=ROOM
    )
    theirs = swap(theirs)
    blocks = [u, first, second, far, sibling, across, swap(second), swap(far)]
    (kv,) = call(
        key_value_kernel,
        [shape((ROWS, 2 * COLS), BF16)],
        [info] + blocks + [late[1], late[2], keyed, valued, bias],
    )
    (query,) = call(
        query_kernel,
        [shape((ROWS, COLS), BF16)],
        [info] + blocks + [late[0], queried],
    )
    queries = [query] + [x_by(query, k) for k in (1, 2, 3)]
    one, other = z_one(kv), z_other(kv)
    pair = shape((2, SEG, FEAT), BF16)
    pairs = call(
        pair_kernel,
        [pair] * 4,
        [info, mine, theirs, one],
        scratch=sems,
        far_in=(1, 2, 3),
        far_out=range(4),
    )
    weights = [pairs[0], y_one(pairs[1]), y_other(pairs[2]), y_far(pairs[3])]
    one2, other2 = z_one(one), z_other(other)
    one3, other3 = z_one(one2), z_other(other2)
    *state, done = attend_step(1, info, queries, kv, [one, other], None, pairs[0])
    *state, done = attend_step(2, info, queries, None, [one2, other2], state, weights[1])
    one3, other3 = gate(info, [one3, other3], done)
    one4 = z_one(one3)
    *state, done = attend_step(3, info, queries, None, [one3, other3], state, weights[2])
    one4, weights[3] = gate(info, [one4, weights[3]], done)
    partial = attend_step(4, info, queries, None, [one4], state)
    partial = [partial[0]] + [x_by(partial[k], -k) for k in (1, 2, 3)]
    (attended,) = call(merge_kernel, [shape((ROWS, COLS), BF16)], [info] + partial, moved=1 << 20)
    return output(mp_exchange(attended), weights, means, ids, tokens)


def solution(mesh):
    placed = (
        P(("dp", "seq"), "mp"),
        P(("dp", "seq")),
        P(),
        P(None, "mp"),
        P(None, "mp"),
        P(None, "mp"),
        P("mp", None),
    )
    return jax.shard_map(
        shards, mesh=mesh, in_specs=placed, out_specs=P(("dp", "seq"), "mp"), check_vma=False
    )
```

```python
import functools

import jax
import jax.numpy as jnp
import numpy as np
from jax import lax
from jax.experimental import pallas as pl
from jax.experimental.pallas import tpu as pltpu
from jax.sharding import PartitionSpec as P

HD = 128
NZ, NX, NY, NC = 8, 4, 4, 2
SEG = 256
ROWS = SEG + 16
TOK = 2048
FEAT = 512
COLS = 256
WIDTH = 4096
SCORE = 1.4426950408889634 * HD**-0.5
LOG2E = 1.4426950408889634
LOW = -1e30
VMEM_LIMIT = 20 * 1024 * 1024
ROOM = 48 * 1024 * 1024
CUT_ROOM = 52 * 1024 * 1024
F32, BF16 = jnp.float32, jnp.bfloat16


def number(z, x, y, c):
    return ((z % NZ) * NX + x % NX) * (NY * NC) + (y % NY) * NC + c % NC


def everywhere():
    return [(z, x, y, c) for z in range(NZ) for x in range(NX) for y in range(NY) for c in range(NC)]


def way(c):
    return 1 if c == 0 else -1


def move(value, target):
    pairs = [(number(*d), number(*target(*d))) for d in everywhere()]
    return lax.ppermute(value, ("seq", "mp"), pairs)


def swap(value):
    return move(value, lambda z, x, y, c: (z, x, y, 1 - c))


def y_one(value):
    return move(value, lambda z, x, y, c: (z, x, y + way(c), c))


def y_other(value):
    return move(value, lambda z, x, y, c: (z, x, y - way(c), c))


def z_one(value):
    return move(value, lambda z, x, y, c: (z + way(c), x, y, c))


def z_other(value):
    return move(value, lambda z, x, y, c: (z - way(c), x, y, c))


def x_by(value, by):
    return move(value, lambda z, x, y, c: (z, x + by, y, c))


def sources(y, c):
    own = [(y, c), (y - way(c), c), (y + way(c), c), (y + 2, c)]
    o = 1 - c
    other = [(y, o), (y - way(o), o), (y + way(o), o), (y + 2, o)]
    return [((b[0] % NY) * NC + b[1]) for b in own + other]


def mp_exchange(value):
    first = y_one(value)
    second = y_other(value)
    sibling = swap(value)
    far = y_one(first)
    return [value, first, second, far, sibling, swap(first), swap(second), swap(far)]


def device_table():
    rows = []
    for z, x, y, c in everywhere():
        row = [y * NC + c] + sources(y, c)
        row += [x] + [(x - k) % NX for k in (1, 2, 3)]
        for k in (1, 2, 3, 4):
            row += [int((z - way(c) * k) % NZ < z), int((z + way(c) * k) % NZ < z)]
        for o in (c, 1 - c):
            row += [(v % NY) * NC + o for v in (y, y + way(o), y - way(o), y + 2)]
        row += [0] * (32 - len(row))
        rows.append(row)
    return np.asarray(rows, np.int32)


I_MP, I_SRC, I_X, I_OK, I_CUT = 0, 1, 9, 13, 21
SMEM = pl.BlockSpec(memory_space=pltpu.SMEM)
WHOLE = pl.BlockSpec(memory_space=pltpu.VMEM)
FAR = pl.BlockSpec(memory_space=pl.ANY)
DISTANT = pl.BlockSpec(memory_space=pltpu.HBM)


def call(body, outs, ins, flops=0, moved=0, scratch=(), aliases=None, far_in=(), far_out=(), far=FAR, scalars=0, room=VMEM_LIMIT):
    return pl.pallas_call(
        body,
        out_shape=outs,
        in_specs=[SMEM if i == scalars else far if i in far_in else WHOLE for i in range(len(ins))],
        out_specs=[far if i in far_out else WHOLE for i in range(len(outs))],
        scratch_shapes=list(scratch),
        input_output_aliases=aliases or {},
        compiler_params=pltpu.CompilerParams(vmem_limit_bytes=room),
        cost_estimate=pl.CostEstimate(flops=flops, bytes_accessed=moved, transcendentals=0),
    )(*ins)


def gate_kernel(info, *refs):
    pass


def gate(info, values, token):
    ins = [info] + list(values) + [token]
    count = len(values)
    return call(
        gate_kernel,
        [shape(v.shape, v.dtype) for v in values],
        ins,
        aliases={i + 1: i for i in range(count)},
        far_in=range(1, count + 2),
        far_out=range(count),
    )


def shape(dims, dtype):
    return jax.ShapeDtypeStruct(dims, dtype)


def dot(a, b):
    return jnp.dot(a, b, preferred_element_type=F32)


def iota(dims, axis):
    return lax.broadcasted_iota(jnp.int32, dims, axis)


def ones_where(condition):
    return jnp.where(condition, 1.0, 0.0).astype(BF16)


def edge_kernel(flags, tokens, ids_out, head_out, tail_out, marks):
    f = flags[...].astype(F32).astype(BF16)
    upto = ones_where(iota((128, 128), 0) <= iota((128, 128), 1))
    inside = dot(f, upto)
    rows = dot(f, jnp.ones((128, 128), BF16)).astype(BF16)
    before = dot(ones_where(iota((16, 16), 1) < iota((16, 16), 0)), rows)
    ids_out[...] = (inside + before - 1.0).astype(jnp.int32)
    wanted = jnp.where(iota((16, 128), 0) < 8, -1, SEG - 1)
    for r in range(16):
        marks[:, r * 128 : (r + 1) * 128] = ones_where(ids_out[r : r + 1, :] == wanted)
    sums = dot(marks[...], tokens[...])
    counts = dot(marks[...], jnp.ones((TOK, 128), BF16))
    head_out[:, :FEAT] = sums[:8]
    head_out[:, FEAT:] = counts[:8]
    tail_out[:, :FEAT] = sums[8:]
    tail_out[:, FEAT:] = counts[8:]


def pool_kernel(ids, tokens, _, sums_out, counts_out, hot):
    segment = iota((SEG, 128), 0)
    for r in range(16):
        hot[:, r * 128 : (r + 1) * 128] = ones_where(ids[r : r + 1, :] == segment)
    sums_out[...] = dot(hot[...], tokens[...])
    counts_out[...] = dot(hot[...], jnp.ones((TOK, 128), BF16))


def wide(column, times):
    return jnp.concatenate([column] * times, axis=1)


def split(value, parts):
    out = []
    for _ in range(parts):
        high = value.astype(BF16).astype(F32)
        out.append(high)
        value = value - high
    return out


def norm_kernel(info, sums, counts, head, above, below, gain, means_out, u_out, bias_out):
    g = gain[pl.ds(info[I_MP], 1), :]
    last = iota((SEG, 128), 0) == SEG - 1
    size = counts[...] + jnp.where(last, above[0:1, FEAT:], 0.0)
    total = sums[...] + jnp.where(iota((SEG, FEAT), 0) == SEG - 1, above[0:1, :FEAT], 0.0)
    size = jnp.maximum(size, 1.0)
    means = total / wide(size, 4)
    means_out[:SEG, :] = means
    u_out[:SEG, :] = (means * g).astype(BF16)
    squares = jnp.sum(means * means, axis=1, keepdims=True)
    squares = jnp.transpose(jnp.broadcast_to(squares, (SEG, 128)))[:16]
    high, low = split(squares, 2)
    extra_size = jnp.maximum(head[0:1, FEAT:] + below[0:1, FEAT:], 1.0)
    extra = (head[0:1, :FEAT] + below[0:1, :FEAT]) / wide(extra_size, 4)
    extra_squares = jnp.broadcast_to(jnp.sum(extra * extra, axis=1, keepdims=True), (16, SEG))
    extra_high, extra_low = split(extra_squares, 2)
    row = iota((16, FEAT), 0)
    means_out[SEG:, :] = jnp.where(row == 0, extra, 0.0)
    tail = jnp.where(row == 0, extra * g, 0.0)
    tail = jnp.where(row == 1, jnp.concatenate([high, low], axis=1), tail)
    tail = jnp.where(row == 2, jnp.concatenate([extra_high, extra_low], axis=1), tail)
    u_out[SEG:, :] = tail.astype(BF16)
    bias = jnp.log(jnp.transpose(size)[:16])
    bias_out[...] = jnp.concatenate([bias, bias], axis=1).astype(BF16)


EARLY = (0, 1, 2, 4)
LATE = (3, 5, 6, 7)


def row_scale(tail):
    squares = tail[:, :SEG] + tail[:, SEG:]
    scale = lax.rsqrt(squares / WIDTH + 1e-05)
    column = jnp.transpose(jnp.broadcast_to(scale[1:2, :], (128, SEG)))
    return scale, wide(column, 2)


def product(acc, blocks, weight, rows):
    for i, u in enumerate(blocks):
        acc = acc + dot(u[:rows, :], weight[i])
    return acc


def early_kernel(info, *refs):
    blocks, weights = refs[:4], refs[4:7]
    sums, kept, early, sems = refs[7:10], refs[10:13], refs[13:16], refs[16]
    copies = {}
    for side, (which, target) in enumerate(((EARLY, early), (LATE, kept))):
        for i in range(4):
            start = pl.multiple_of(info[I_SRC + which[i]] * FEAT, FEAT)
            for n in range(3):
                copies[side, i, n] = pltpu.make_async_copy(
                    weights[n].at[pl.ds(start, FEAT), :], target[n].at[i], sems.at[side, i, n]
                )
                copies[side, i, n].start()
    for i, u in enumerate(blocks):
        for n, rows in enumerate((ROWS, SEG, SEG)):
            copies[0, i, n].wait()
            part = dot(u[:rows, :], early[n][i])
            sums[n][...] = part if i == 0 else sums[n][...] + part
    for i in range(4):
        for n in range(3):
            copies[1, i, n].wait()


def square_rows(blocks):
    tail = jnp.zeros((16, FEAT), F32)
    for u in blocks:
        tail = tail + u[SEG:, :].astype(F32)
    return tail


def key_value_kernel(info, *refs):
    blocks, late = refs[:8], [refs[i] for i in LATE]
    w_key, w_value, keys, values, bias, kv_out = refs[8:]
    _, column = row_scale(square_rows(blocks))
    kv_out[:SEG, :COLS] = (product(keys[...], late, w_key, SEG) * column).astype(BF16)
    kv_out[:SEG, COLS:] = (product(values[...], late, w_value, SEG) * column).astype(BF16)
    kv_out[SEG:, :] = bias[...]


def query_kernel(info, *refs):
    blocks, late = refs[:8], [refs[i] for i in LATE]
    w_query, partial, _, q_out = refs[8:]
    scale, column = row_scale(square_rows(blocks))
    query = product(partial[...], late, w_query, ROWS)
    q_out[:SEG, :] = (query[:SEG] * column * SCORE).astype(BF16)
    extra = query[SEG:] * scale[2:3, :] * SCORE
    q_out[SEG:, :] = jnp.where(iota((16, COLS), 0) == 0, extra, 0.0).astype(BF16)


def nt_dot(a, b):
    return lax.dot_general(a, b, (((1,), (1,)), ((), ())), preferred_element_type=F32)


def attend(q, k, v, bias, acc_ref, m_ref, j, h, mask=None):
    scores = nt_dot(q[:, h * HD : (h + 1) * HD], k) + bias
    if mask is not None:
        scores = jnp.where(mask, scores, LOW)
    old = m_ref[j, h]
    peak = jnp.maximum(old, jnp.max(scores, axis=1, keepdims=True))
    expo = jnp.exp2(scores - wide(peak, scores.shape[1] // 128))
    if mask is not None:
        expo = jnp.where(mask, expo, 0.0)
    m_ref[j, h] = peak
    acc_ref[j, h] = acc_ref[j, h] * wide(jnp.exp2(old - peak), 2) + dot(expo.astype(BF16), v)


def keys_of(blocks, h):
    return jnp.concatenate([kv[:SEG, h * HD : (h + 1) * HD] for kv in blocks], axis=0)


def values_of(blocks, h):
    lanes = slice(COLS + h * HD, COLS + (h + 1) * HD)
    values = jnp.concatenate([kv[:SEG, lanes] for kv in blocks], axis=0)
    return jnp.concatenate([values, jnp.ones(values.shape, BF16)], axis=1)


def attend_kernel(step, first, final, info, *refs):
    refs = list(refs)
    queries = [refs.pop(0) for _ in range(4)]
    own = refs.pop(0) if first else None
    others = [refs.pop(0) for _ in range(1 if final else 2)]
    if not final:
        refs = refs[1:]
    if not first:
        state_in = [refs.pop(0) for _ in range(2)]
    if final:
        payloads = [refs.pop(0) for _ in range(4)]
        acc, m = state_in
    else:
        acc, m, done = refs[:3]
        done[...] = jnp.zeros_like(done)
    if first:
        acc[...] = jnp.zeros_like(acc)
        m[...] = jnp.full(m.shape, LOW, F32)
        bias = own[SEG : SEG + 1, :SEG].astype(F32) * LOG2E
        for j in range(4):

            def one(j=j):
                mask = None
                if j == 0:
                    r, k = iota((ROWS, SEG), 0), iota((ROWS, SEG), 1)
                    mask = (k <= r) & (r < SEG)
                for h in range(2):
                    attend(queries[j], keys_of([own], h), values_of([own], h), bias, acc, m, j, h, mask)

            if j == 0:
                one()
            else:
                pl.when(info[I_X] < info[I_X + j])(one)
    ok = [info[I_OK + 2 * (step - 1) + i] for i in range(len(others))]
    some = ok[0] if final else ok[0] + ok[1]

    @pl.when(some > 0)
    def _():
        biases = []
        for kv, good in zip(others, ok):
            row = kv[SEG : SEG + 1, :SEG].astype(F32) * LOG2E
            biases.append(jnp.where(good > 0, row, LOW))
        bias = jnp.concatenate(biases, axis=1)
        for h in range(2):
            k, v = keys_of(others, h), values_of(others, h)
            for j in range(4):
                attend(queries[j], k, v, bias, acc, m, j, h)

    if final:
        row = iota((16, COLS), 0)
        for j in range(4):
            tail = jnp.zeros((16, COLS), F32)
            ends = []
            for h in range(2):
                total = acc[j, h][:, HD:]
                some_keys = total > 0.0
                total = jnp.where(some_keys, total, 1.0)
                out = acc[j, h][:, :HD] / total
                logs = jnp.where(some_keys, m[j, h] + jnp.log2(total), LOW)
                payloads[j][:SEG, h * HD : (h + 1) * HD] = out[:SEG].astype(BF16)
                ends.append(out[SEG:])
                parts = split(jnp.transpose(logs[:SEG])[:16], 3)
                for i, part in enumerate(parts):
                    tail = jnp.where(row == 1 + 3 * h + i, part, tail)
                parts = split(wide(logs[SEG : SEG + 1], 2), 3)
                for i, part in enumerate(parts):
                    tail = jnp.where(row == 7 + 3 * h + i, part, tail)
            tail = jnp.where(row == 0, jnp.concatenate(ends, axis=1), tail)
            payloads[j][SEG:, :] = tail.astype(BF16)


STATE = [shape((4, 2, ROWS, 2 * HD), F32), shape((4, 2, ROWS, HD), F32), shape((8, 128), F32)]


def attend_step(step, info, queries, own, others, state, ahead=None):
    first, final = own is not None, len(others) == 1
    ins = [info] + queries + ([own] if first else []) + others + ([] if final else [ahead]) + list(state or [])
    flops = 4 * 1088 * SEG * (len(others) + (1 if first else 0)) * COLS
    body = functools.partial(attend_kernel, step, first, final)
    if final:
        outs = [shape((ROWS, COLS), BF16)] * 4 + STATE[:2]
        aliases = {len(ins) - 2: 4, len(ins) - 1: 5}

        def body(*refs):
            refs = list(refs)
            payloads, state = refs[-6:-2], refs[-2:]
            attend_kernel(step, first, final, *refs[:-8], *state, *payloads)

        return call(body, outs, ins, flops=flops, moved=4 << 20, aliases=aliases)[:4]
    aliases = {} if first else {len(ins) - 2: 0, len(ins) - 1: 1}
    ignored = 5 + len(others) + (1 if first else 0)
    return call(body, STATE, ins, flops=flops, moved=4 << 20, aliases=aliases, far_in=(ignored,))


def merge_kernel(info, a, b, c, d, out):
    parts = (a, b, c, d)
    tails = [p[SEG:, :].astype(F32) for p in parts]
    weights, end_weights = [], []
    for h in range(2):
        for base, store in ((1 + 3 * h, weights), (7 + 3 * h, end_weights)):
            logs = [t[base : base + 1] + t[base + 1 : base + 2] + t[base + 2 : base + 3] for t in tails]
            peak = functools.reduce(jnp.maximum, logs)
            expo = [jnp.exp2(v - peak) for v in logs]
            whole = functools.reduce(jnp.add, expo)
            store.append([e / whole for e in expo])
    flat = weights[0] + weights[1]
    columns = jnp.transpose(jnp.concatenate(flat + [jnp.zeros((120, SEG), F32)], axis=0))
    ends = []
    for h in range(2):
        lanes = slice(h * HD, (h + 1) * HD)
        acc = jnp.zeros((SEG, HD), F32)
        end = jnp.zeros((16, HD), F32)
        for j, p in enumerate(parts):
            acc = acc + columns[:, 4 * h + j : 4 * h + j + 1] * p[:SEG, lanes].astype(F32)
            end = end + end_weights[h][j][:, :HD] * tails[j][:, lanes]
        out[:SEG, lanes] = acc.astype(BF16)
        ends.append(end)
    end = jnp.concatenate(ends, axis=1)
    out[SEG:, :] = jnp.where(iota((16, COLS), 0) == 0, end, 0.0).astype(BF16)


BLOCK = 512
TALL = 384
PAIR = (0, 1, 2, 3, 0, 2, 1, 3)


def output_kernel(*refs):
    attended, weights = refs[:8], refs[8:12]
    means, ids, tokens, out, coarse = refs[12:]

    @pl.when(pl.program_id(0) == 0)
    def _():
        acc = means[...]
        for i, a in enumerate(attended):
            acc = acc + dot(a[...], weights[PAIR[i]][i // 4])
        coarse[:ROWS, :] = acc.astype(BF16)
        coarse[ROWS:, :] = jnp.zeros((TALL - ROWS, FEAT), BF16)

    base = pl.multiple_of(pl.program_id(0) * (BLOCK // 128), BLOCK // 128)
    lane = iota((128, 128), 1)
    chunks = []
    for r in range(BLOCK // 128):
        row = ids[pl.ds(base + r, 1), :].astype(F32)
        column = jnp.transpose(jnp.broadcast_to(row, (128, 128))).astype(jnp.int32)
        chunks.append(
            jnp.concatenate(
                [
                    ones_where(column == lane),
                    ones_where(column == lane + 128),
                    ones_where((column == -1) & (lane == 0)),
                ],
                axis=1,
            )
        )
    hot = jnp.concatenate(chunks, axis=0)
    picked = dot(hot, coarse[...])
    out[...] = (tokens[...].astype(F32) + picked).astype(BF16)


def output(attended, weights, means, ids, tokens):
    whole = [WHOLE] * 14
    return pl.pallas_call(
        output_kernel,
        grid=(TOK // BLOCK,),
        out_shape=shape((TOK, FEAT), BF16),
        in_specs=whole + [pl.BlockSpec((BLOCK, FEAT), lambda i: (i, 0))],
        out_specs=pl.BlockSpec((BLOCK, FEAT), lambda i: (i, 0)),
        scratch_shapes=[pltpu.VMEM((TALL, FEAT), BF16)],
        compiler_params=pltpu.CompilerParams(vmem_limit_bytes=VMEM_LIMIT),
        cost_estimate=pl.CostEstimate(flops=2 << 30, bytes_accessed=6 << 20, transcendentals=0),
    )(*attended, *weights, means, ids, tokens)


def cut_kernel(info, w_out, _, mine, sibling, done, sems):
    copies = []
    for i in range(4):
        for side, out in enumerate((mine, sibling)):
            start = pl.multiple_of(info[I_CUT + 4 * side + i] * FEAT, FEAT)
            copies.append(pltpu.make_async_copy(w_out.at[:, pl.ds(start, FEAT)], out.at[i], sems.at[side, i]))
            copies[-1].start()
    done[...] = jnp.zeros_like(done)
    for copy in copies:
        copy.wait()


def pair_kernel(info, *refs):
    sources, outs, sems = refs[:2], refs[7:11], refs[-1]
    copies = []
    for i, out in enumerate(outs):
        for side, source in enumerate(sources):
            copies.append(pltpu.make_async_copy(source.at[i], out.at[side], sems.at[side, i]))
            copies[-1].start()
    for copy in copies:
        copy.wait()


def y_far(value):
    return move(value, lambda z, x, y, c: (z, x, y + 2, c))


def shards(tokens, flags, norm_gain, w_query, w_key, w_value, w_out):
    seq, mp = lax.axis_index("seq"), lax.axis_index("mp")
    info = jnp.asarray(device_table())[seq * (NY * NC) + mp]
    edge = shape((8, FEAT + 128), F32)
    ids, head, tail = call(
        edge_kernel,
        [shape((16, 128), jnp.int32), edge, edge],
        [flags.reshape(16, 128), tokens],
        scalars=None,
        flops=1 << 28,
        moved=2 << 20,
        scratch=[pltpu.VMEM((16, TOK), BF16)],
    )
    count = NZ * NX
    above = lax.ppermute(head, "seq", [(i, i - 1) for i in range(1, count)])
    below = lax.ppermute(tail, "seq", [(i, i + 1) for i in range(count - 1)])
    cut = shape((4, SEG, FEAT), BF16)
    sems = [pltpu.SemaphoreType.DMA((2, 4))]
    mine, theirs, cut_done = call(
        cut_kernel, [cut, cut, shape((8, 128), F32)], [info, w_out, ids], scratch=sems, far_in=(1, 2), far_out=(0, 1), room=CUT_ROOM
    )
    theirs = swap(theirs)
    sums, sizes = call(
        pool_kernel,
        [shape((SEG, FEAT), F32), shape((SEG, 128), F32)],
        [ids, tokens, cut_done],
        scalars=None,
        far_in=(2,),
        flops=1 << 30,
        moved=2 << 20,
        scratch=[pltpu.VMEM((SEG, TOK), BF16)],
    )
    means, u, bias = call(
        norm_kernel,
        [shape((ROWS, FEAT), F32), shape((ROWS, FEAT), BF16), shape((16, FEAT), BF16)],
        [info, sums, sizes, head, above, below, norm_gain.reshape(8, FEAT)],
    )
    first, sibling, second = y_one(u), swap(u), y_other(u)
    across, far = swap(first), y_one(first)
    part, part_query = shape((SEG, COLS), F32), shape((ROWS, COLS), F32)
    kept = shape((4, FEAT, COLS), BF16)
    queried, keyed, valued, *late = call(
        early_kernel,
        [part_query, part, part] + [kept] * 3,
        [info, u, first, second, sibling, w_query, w_key, w_value],
        scratch=[pltpu.VMEM((4, FEAT, COLS), BF16)] * 3 + [pltpu.SemaphoreType.DMA((2, 4, 3))],
        flops=ROWS * WIDTH * 3 * COLS,
        moved=6 << 20,
        far_in=(5, 6, 7),
        room=ROOM,
    )
    blocks = [u, first, second, far, sibling, across, swap(second), swap(far)]
    (kv,) = call(
        key_value_kernel,
        [shape((ROWS, 2 * COLS), BF16)],
        [info] + blocks + [late[1], late[2], keyed, valued, bias],
    )
    (query,) = call(
        query_kernel,
        [shape((ROWS, COLS), BF16)],
        [info] + blocks + [late[0], queried, kv],
        far_in=(11,),
    )
    queries = [query] + [x_by(query, k) for k in (1, 2, 3)]
    one, other = z_one(kv), z_other(kv)
    pair = shape((2, SEG, FEAT), BF16)
    block = shape(kv.shape, BF16)
    *pairs, one, other = call(
        pair_kernel,
        [pair] * 4 + [block] * 2,
        [info, mine, theirs, one, other] + queries[1:],
        scratch=sems,
        aliases={3: 4, 4: 5},
        far_in=range(1, 8),
        far_out=range(6),
    )
    far_weights = y_far(pairs[3])
    one2, other2 = z_one(one), z_other(other)
    *state, done = attend_step(1, info, queries, kv, [one, other], None, pairs[0])
    one2, other2 = gate(info, [one2, other2], done)
    one3, other3 = z_one(one2), z_other(other2)
    one_weights = y_one(pairs[1])
    *state, done = attend_step(2, info, queries, None, [one2, other2], state, far_weights)
    one3, other3 = gate(info, [one3, other3], done)
    one4 = z_one(one3)
    other_weights = y_other(pairs[2])
    *state, done = attend_step(3, info, queries, None, [one3, other3], state, one_weights)
    one4, other_weights = gate(info, [one4, other_weights], done)
    partial = attend_step(4, info, queries, None, [one4], state)
    weights = [pairs[0], one_weights, other_weights, far_weights]
    partial = [partial[0]] + [x_by(partial[k], -k) for k in (1, 2, 3)]
    (attended,) = call(merge_kernel, [shape((ROWS, COLS), BF16)], [info] + partial, moved=1 << 20)
    return output(mp_exchange(attended), weights, means, ids, tokens)


def solution(mesh):
    placed = (
        P(("dp", "seq"), "mp"),
        P(("dp", "seq")),
        P(),
        P(None, "mp"),
        P(None, "mp"),
        P(None, "mp"),
        P("mp", None),
    )
    return jax.shard_map(
        shards, mesh=mesh, in_specs=placed, out_specs=P(("dp", "seq"), "mp"), check_vma=False
    )
```

```python
import functools

import jax
import jax.numpy as jnp
import numpy as np
from jax import lax
from jax.experimental import pallas as pl
from jax.experimental.pallas import tpu as pltpu
from jax.sharding import PartitionSpec as P

HD = 128
NZ, NX, NY, NC = 8, 4, 4, 2
SEG = 256
ROWS = SEG + 16
TOK = 2048
FEAT = 512
COLS = 256
WIDTH = 4096
SCORE = 1.4426950408889634 * HD**-0.5
LOG2E = 1.4426950408889634
LOW = -1e30
VMEM_LIMIT = 20 * 1024 * 1024
ROOM = 48 * 1024 * 1024
F32, BF16 = jnp.float32, jnp.bfloat16


def number(z, x, y, c):
    return ((z % NZ) * NX + x % NX) * (NY * NC) + (y % NY) * NC + c % NC


def everywhere():
    return [(z, x, y, c) for z in range(NZ) for x in range(NX) for y in range(NY) for c in range(NC)]


def way(c):
    return 1 if c == 0 else -1


def move(value, target):
    pairs = [(number(*d), number(*target(*d))) for d in everywhere()]
    return lax.ppermute(value, ("seq", "mp"), pairs)


def swap(value):
    return move(value, lambda z, x, y, c: (z, x, y, 1 - c))


def y_one(value):
    return move(value, lambda z, x, y, c: (z, x, y + way(c), c))


def y_other(value):
    return move(value, lambda z, x, y, c: (z, x, y - way(c), c))


def z_one(value):
    return move(value, lambda z, x, y, c: (z + way(c), x, y, c))


def z_other(value):
    return move(value, lambda z, x, y, c: (z - way(c), x, y, c))


def x_by(value, by):
    return move(value, lambda z, x, y, c: (z, x + by, y, c))


def sources(y, c):
    own = [(y, c), (y - way(c), c), (y + way(c), c), (y + 2, c)]
    o = 1 - c
    other = [(y, o), (y - way(o), o), (y + way(o), o), (y + 2, o)]
    return [((b[0] % NY) * NC + b[1]) for b in own + other]


def mp_exchange(value):
    first = y_one(value)
    second = y_other(value)
    sibling = swap(value)
    far = y_one(first)
    return [value, first, second, far, sibling, swap(first), swap(second), swap(far)]


def device_table():
    rows = []
    for z, x, y, c in everywhere():
        row = [y * NC + c] + sources(y, c)
        row += [x] + [(x - k) % NX for k in (1, 2, 3)]
        for k in (1, 2, 3, 4):
            row += [int((z - way(c) * k) % NZ < z), int((z + way(c) * k) % NZ < z)]
        for o in (c, 1 - c):
            row += [(v % NY) * NC + o for v in (y, y + way(o), y - way(o), y + 2)]
        row += [0] * (32 - len(row))
        rows.append(row)
    return np.asarray(rows, np.int32)


I_MP, I_SRC, I_X, I_OK, I_CUT = 0, 1, 9, 13, 21
SMEM = pl.BlockSpec(memory_space=pltpu.SMEM)
WHOLE = pl.BlockSpec(memory_space=pltpu.VMEM)
FAR = pl.BlockSpec(memory_space=pl.ANY)
DISTANT = pl.BlockSpec(memory_space=pltpu.HBM)


def call(body, outs, ins, flops=0, moved=0, scratch=(), aliases=None, far_in=(), far_out=(), far=FAR, scalars=0, room=VMEM_LIMIT):
    return pl.pallas_call(
        body,
        out_shape=outs,
        in_specs=[SMEM if i == scalars else far if i in far_in else WHOLE for i in range(len(ins))],
        out_specs=[far if i in far_out else WHOLE for i in range(len(outs))],
        scratch_shapes=list(scratch),
        input_output_aliases=aliases or {},
        compiler_params=pltpu.CompilerParams(vmem_limit_bytes=room),
        cost_estimate=pl.CostEstimate(flops=flops, bytes_accessed=moved, transcendentals=0),
    )(*ins)


def gate_kernel(info, *refs):
    pass


def gate(info, values, token):
    ins = [info] + list(values) + [token]
    count = len(values)
    return call(
        gate_kernel,
        [shape(v.shape, v.dtype) for v in values],
        ins,
        aliases={i + 1: i for i in range(count)},
        far_in=range(1, count + 2),
        far_out=range(count),
    )


def shape(dims, dtype):
    return jax.ShapeDtypeStruct(dims, dtype)


def dot(a, b):
    return jnp.dot(a, b, preferred_element_type=F32)


def iota(dims, axis):
    return lax.broadcasted_iota(jnp.int32, dims, axis)


def ones_where(condition):
    return jnp.where(condition, 1.0, 0.0).astype(BF16)


def edge_kernel(flags, tokens, ids_out, head_out, tail_out, marks):
    f = flags[...].astype(F32).astype(BF16)
    upto = ones_where(iota((128, 128), 0) <= iota((128, 128), 1))
    inside = dot(f, upto)
    rows = dot(f, jnp.ones((128, 128), BF16)).astype(BF16)
    before = dot(ones_where(iota((16, 16), 1) < iota((16, 16), 0)), rows)
    ids_out[...] = (inside + before - 1.0).astype(jnp.int32)
    wanted = jnp.where(iota((16, 128), 0) < 8, -1, SEG - 1)
    for r in range(16):
        marks[:, r * 128 : (r + 1) * 128] = ones_where(ids_out[r : r + 1, :] == wanted)
    sums = dot(marks[...], tokens[...])
    counts = dot(marks[...], jnp.ones((TOK, 128), BF16))
    head_out[:, :FEAT] = sums[:8]
    head_out[:, FEAT:] = counts[:8]
    tail_out[:, :FEAT] = sums[8:]
    tail_out[:, FEAT:] = counts[8:]


def pool_kernel(ids, tokens, sums_out, counts_out, hot):
    segment = iota((SEG, 128), 0)
    for r in range(16):
        hot[:, r * 128 : (r + 1) * 128] = ones_where(ids[r : r + 1, :] == segment)
    sums_out[...] = dot(hot[...], tokens[...])
    counts_out[...] = dot(hot[...], jnp.ones((TOK, 128), BF16))


def wide(column, times):
    return jnp.concatenate([column] * times, axis=1)


def split(value, parts):
    out = []
    for _ in range(parts):
        high = value.astype(BF16).astype(F32)
        out.append(high)
        value = value - high
    return out


def norm_kernel(info, sums, counts, head, above, below, gain, means_out, u_out, bias_out):
    g = gain[pl.ds(info[I_MP], 1), :]
    last = iota((SEG, 128), 0) == SEG - 1
    size = counts[...] + jnp.where(last, above[0:1, FEAT:], 0.0)
    total = sums[...] + jnp.where(iota((SEG, FEAT), 0) == SEG - 1, above[0:1, :FEAT], 0.0)
    size = jnp.maximum(size, 1.0)
    means = total / wide(size, 4)
    means_out[:SEG, :] = means
    u_out[:SEG, :] = (means * g).astype(BF16)
    squares = jnp.sum(means * means, axis=1, keepdims=True)
    squares = jnp.transpose(jnp.broadcast_to(squares, (SEG, 128)))[:16]
    high, low = split(squares, 2)
    extra_size = jnp.maximum(head[0:1, FEAT:] + below[0:1, FEAT:], 1.0)
    extra = (head[0:1, :FEAT] + below[0:1, :FEAT]) / wide(extra_size, 4)
    extra_squares = jnp.broadcast_to(jnp.sum(extra * extra, axis=1, keepdims=True), (16, SEG))
    extra_high, extra_low = split(extra_squares, 2)
    row = iota((16, FEAT), 0)
    means_out[SEG:, :] = jnp.where(row == 0, extra, 0.0)
    tail = jnp.where(row == 0, extra * g, 0.0)
    tail = jnp.where(row == 1, jnp.concatenate([high, low], axis=1), tail)
    tail = jnp.where(row == 2, jnp.concatenate([extra_high, extra_low], axis=1), tail)
    u_out[SEG:, :] = tail.astype(BF16)
    bias = jnp.log(jnp.transpose(size)[:16])
    bias_out[...] = jnp.concatenate([bias, bias], axis=1).astype(BF16)


EARLY = (0, 1, 2, 4)
LATE = (3, 5, 6, 7)


def row_scale(tail):
    squares = tail[:, :SEG] + tail[:, SEG:]
    scale = lax.rsqrt(squares / WIDTH + 1e-05)
    column = jnp.transpose(jnp.broadcast_to(scale[1:2, :], (128, SEG)))
    return scale, wide(column, 2)


def product(acc, blocks, weight, rows):
    for i, u in enumerate(blocks):
        acc = acc + dot(u[:rows, :], weight[i])
    return acc


def early_kernel(info, *refs):
    blocks, weights = refs[:4], refs[4:7]
    sums, kept, early, sems = refs[7:10], refs[10:13], refs[13:16], refs[16]
    copies = {}
    for side, (which, target) in enumerate(((EARLY, early), (LATE, kept))):
        for i in range(4):
            start = pl.multiple_of(info[I_SRC + which[i]] * FEAT, FEAT)
            for n in range(3):
                copies[side, i, n] = pltpu.make_async_copy(
                    weights[n].at[pl.ds(start, FEAT), :], target[n].at[i], sems.at[side, i, n]
                )
                copies[side, i, n].start()
    for i, u in enumerate(blocks):
        for n, rows in enumerate((ROWS, SEG, SEG)):
            copies[0, i, n].wait()
            part = dot(u[:rows, :], early[n][i])
            sums[n][...] = part if i == 0 else sums[n][...] + part
    for i in range(4):
        for n in range(3):
            copies[1, i, n].wait()


def square_rows(blocks):
    tail = jnp.zeros((16, FEAT), F32)
    for u in blocks:
        tail = tail + u[SEG:, :].astype(F32)
    return tail


def key_value_kernel(info, *refs):
    blocks, late = refs[:8], [refs[i] for i in LATE]
    w_key, w_value, keys, values, bias, kv_out = refs[8:]
    _, column = row_scale(square_rows(blocks))
    kv_out[:SEG, :COLS] = (product(keys[...], late, w_key, SEG) * column).astype(BF16)
    kv_out[:SEG, COLS:] = (product(values[...], late, w_value, SEG) * column).astype(BF16)
    kv_out[SEG:, :] = bias[...]


def query_kernel(info, *refs):
    blocks, late = refs[:8], [refs[i] for i in LATE]
    w_query, partial, _, q_out = refs[8:]
    scale, column = row_scale(square_rows(blocks))
    query = product(partial[...], late, w_query, ROWS)
    q_out[:SEG, :] = (query[:SEG] * column * SCORE).astype(BF16)
    extra = query[SEG:] * scale[2:3, :] * SCORE
    q_out[SEG:, :] = jnp.where(iota((16, COLS), 0) == 0, extra, 0.0).astype(BF16)


def nt_dot(a, b):
    return lax.dot_general(a, b, (((1,), (1,)), ((), ())), preferred_element_type=F32)


def attend(q, k, v, bias, acc_ref, m_ref, j, h, mask=None):
    scores = nt_dot(q[:, h * HD : (h + 1) * HD], k) + bias
    if mask is not None:
        scores = jnp.where(mask, scores, LOW)
    old = m_ref[j, h]
    peak = jnp.maximum(old, jnp.max(scores, axis=1, keepdims=True))
    expo = jnp.exp2(scores - wide(peak, scores.shape[1] // 128))
    if mask is not None:
        expo = jnp.where(mask, expo, 0.0)
    m_ref[j, h] = peak
    acc_ref[j, h] = acc_ref[j, h] * wide(jnp.exp2(old - peak), 2) + dot(expo.astype(BF16), v)


def keys_of(blocks, h):
    return jnp.concatenate([kv[:SEG, h * HD : (h + 1) * HD] for kv in blocks], axis=0)


def values_of(blocks, h):
    lanes = slice(COLS + h * HD, COLS + (h + 1) * HD)
    values = jnp.concatenate([kv[:SEG, lanes] for kv in blocks], axis=0)
    return jnp.concatenate([values, jnp.ones(values.shape, BF16)], axis=1)


def attend_kernel(step, first, final, info, *refs):
    refs = list(refs)
    queries = [refs.pop(0) for _ in range(4)]
    own = refs.pop(0) if first else None
    others = [refs.pop(0) for _ in range(1 if final else 2)]
    if not final:
        refs = refs[1:]
    if not first:
        state_in = [refs.pop(0) for _ in range(2)]
    if final:
        payloads = [refs.pop(0) for _ in range(4)]
        acc, m = state_in
    else:
        acc, m, done = refs[:3]
        done[...] = jnp.zeros_like(done)
    if first:
        acc[...] = jnp.zeros_like(acc)
        m[...] = jnp.full(m.shape, LOW, F32)
        bias = own[SEG : SEG + 1, :SEG].astype(F32) * LOG2E
        for j in range(4):

            def one(j=j):
                mask = None
                if j == 0:
                    r, k = iota((ROWS, SEG), 0), iota((ROWS, SEG), 1)
                    mask = (k <= r) & (r < SEG)
                for h in range(2):
                    attend(queries[j], keys_of([own], h), values_of([own], h), bias, acc, m, j, h, mask)

            if j == 0:
                one()
            else:
                pl.when(info[I_X] < info[I_X + j])(one)
    ok = [info[I_OK + 2 * (step - 1) + i] for i in range(len(others))]
    some = ok[0] if final else ok[0] + ok[1]

    @pl.when(some > 0)
    def _():
        biases = []
        for kv, good in zip(others, ok):
            row = kv[SEG : SEG + 1, :SEG].astype(F32) * LOG2E
            biases.append(jnp.where(good > 0, row, LOW))
        bias = jnp.concatenate(biases, axis=1)
        for h in range(2):
            k, v = keys_of(others, h), values_of(others, h)
            for j in range(4):
                attend(queries[j], k, v, bias, acc, m, j, h)

    if final:
        row = iota((16, COLS), 0)
        for j in range(4):
            tail = jnp.zeros((16, COLS), F32)
            ends = []
            for h in range(2):
                total = acc[j, h][:, HD:]
                some_keys = total > 0.0
                total = jnp.where(some_keys, total, 1.0)
                out = acc[j, h][:, :HD] / total
                logs = jnp.where(some_keys, m[j, h] + jnp.log2(total), LOW)
                payloads[j][:SEG, h * HD : (h + 1) * HD] = out[:SEG].astype(BF16)
                ends.append(out[SEG:])
                parts = split(jnp.transpose(logs[:SEG])[:16], 3)
                for i, part in enumerate(parts):
                    tail = jnp.where(row == 1 + 3 * h + i, part, tail)
                parts = split(wide(logs[SEG : SEG + 1], 2), 3)
                for i, part in enumerate(parts):
                    tail = jnp.where(row == 7 + 3 * h + i, part, tail)
            tail = jnp.where(row == 0, jnp.concatenate(ends, axis=1), tail)
            payloads[j][SEG:, :] = tail.astype(BF16)


STATE = [shape((4, 2, ROWS, 2 * HD), F32), shape((4, 2, ROWS, HD), F32), shape((8, 128), F32)]


def attend_step(step, info, queries, own, others, state, ahead=None):
    first, final = own is not None, len(others) == 1
    ins = [info] + queries + ([own] if first else []) + others + ([] if final else [ahead]) + list(state or [])
    flops = 4 * 1088 * SEG * (len(others) + (1 if first else 0)) * COLS
    body = functools.partial(attend_kernel, step, first, final)
    if final:
        outs = [shape((ROWS, COLS), BF16)] * 4 + STATE[:2]
        aliases = {len(ins) - 2: 4, len(ins) - 1: 5}

        def body(*refs):
            refs = list(refs)
            payloads, state = refs[-6:-2], refs[-2:]
            attend_kernel(step, first, final, *refs[:-8], *state, *payloads)

        return call(body, outs, ins, flops=flops, moved=4 << 20, aliases=aliases)[:4]
    aliases = {} if first else {len(ins) - 2: 0, len(ins) - 1: 1}
    ignored = 5 + len(others) + (1 if first else 0)
    return call(body, STATE, ins, flops=flops, moved=4 << 20, aliases=aliases, far_in=(ignored,))


def merge_kernel(info, a, b, c, d, _, out):
    parts = (a, b, c, d)
    tails = [p[SEG:, :].astype(F32) for p in parts]
    weights, end_weights = [], []
    for h in range(2):
        for base, store in ((1 + 3 * h, weights), (7 + 3 * h, end_weights)):
            logs = [t[base : base + 1] + t[base + 1 : base + 2] + t[base + 2 : base + 3] for t in tails]
            peak = functools.reduce(jnp.maximum, logs)
            expo = [jnp.exp2(v - peak) for v in logs]
            whole = functools.reduce(jnp.add, expo)
            store.append([e / whole for e in expo])
    flat = weights[0] + weights[1]
    columns = jnp.transpose(jnp.concatenate(flat + [jnp.zeros((120, SEG), F32)], axis=0))
    ends = []
    for h in range(2):
        lanes = slice(h * HD, (h + 1) * HD)
        acc = jnp.zeros((SEG, HD), F32)
        end = jnp.zeros((16, HD), F32)
        for j, p in enumerate(parts):
            acc = acc + columns[:, 4 * h + j : 4 * h + j + 1] * p[:SEG, lanes].astype(F32)
            end = end + end_weights[h][j][:, :HD] * tails[j][:, lanes]
        out[:SEG, lanes] = acc.astype(BF16)
        ends.append(end)
    end = jnp.concatenate(ends, axis=1)
    out[SEG:, :] = jnp.where(iota((16, COLS), 0) == 0, end, 0.0).astype(BF16)


BLOCK = 512
TALL = 384
PAIR = (0, 1, 2, 3, 0, 2, 1, 3)


def output_kernel(*refs):
    attended, weights = refs[:8], refs[8:12]
    means, ids, tokens, out, coarse = refs[12:]

    @pl.when(pl.program_id(0) == 0)
    def _():
        acc = means[...]
        for i, a in enumerate(attended):
            acc = acc + dot(a[...], weights[PAIR[i]][i // 4])
        coarse[:ROWS, :] = acc.astype(BF16)
        coarse[ROWS:, :] = jnp.zeros((TALL - ROWS, FEAT), BF16)

    base = pl.multiple_of(pl.program_id(0) * (BLOCK // 128), BLOCK // 128)
    lane = iota((128, 128), 1)
    chunks = []
    for r in range(BLOCK // 128):
        row = ids[pl.ds(base + r, 1), :].astype(F32)
        column = jnp.transpose(jnp.broadcast_to(row, (128, 128))).astype(jnp.int32)
        chunks.append(
            jnp.concatenate(
                [
                    ones_where(column == lane),
                    ones_where(column == lane + 128),
                    ones_where((column == -1) & (lane == 0)),
                ],
                axis=1,
            )
        )
    hot = jnp.concatenate(chunks, axis=0)
    picked = dot(hot, coarse[...])
    out[...] = (tokens[...].astype(F32) + picked).astype(BF16)


def output(attended, weights, means, ids, tokens):
    whole = [WHOLE] * 14
    return pl.pallas_call(
        output_kernel,
        grid=(TOK // BLOCK,),
        out_shape=shape((TOK, FEAT), BF16),
        in_specs=whole + [pl.BlockSpec((BLOCK, FEAT), lambda i: (i, 0))],
        out_specs=pl.BlockSpec((BLOCK, FEAT), lambda i: (i, 0)),
        scratch_shapes=[pltpu.VMEM((TALL, FEAT), BF16)],
        compiler_params=pltpu.CompilerParams(vmem_limit_bytes=VMEM_LIMIT),
        cost_estimate=pl.CostEstimate(flops=2 << 30, bytes_accessed=6 << 20, transcendentals=0),
    )(*attended, *weights, means, ids, tokens)


def cut_kernel(info, w_out, _, mine, sibling, sems):
    copies = []
    for i in range(4):
        for side, out in enumerate((mine, sibling)):
            start = pl.multiple_of(info[I_CUT + 4 * side + i] * FEAT, FEAT)
            copies.append(pltpu.make_async_copy(w_out.at[:, pl.ds(start, FEAT)], out.at[i], sems.at[side, i]))
            copies[-1].start()
    for copy in copies:
        copy.wait()


def pair_kernel(info, *refs):
    sources, outs, sems = refs[:2], refs[3:7], refs[7]
    copies = []
    for i, out in enumerate(outs):
        for side, source in enumerate(sources):
            copies.append(pltpu.make_async_copy(source.at[i], out.at[side], sems.at[side, i]))
            copies[-1].start()
    for copy in copies:
        copy.wait()


def y_far(value):
    return move(value, lambda z, x, y, c: (z, x, y + 2, c))


def shards(tokens, flags, norm_gain, w_query, w_key, w_value, w_out):
    seq, mp = lax.axis_index("seq"), lax.axis_index("mp")
    info = jnp.asarray(device_table())[seq * (NY * NC) + mp]
    edge = shape((8, FEAT + 128), F32)
    ids, head, tail = call(
        edge_kernel,
        [shape((16, 128), jnp.int32), edge, edge],
        [flags.reshape(16, 128), tokens],
        scalars=None,
        flops=1 << 28,
        moved=2 << 20,
        scratch=[pltpu.VMEM((16, TOK), BF16)],
    )
    count = NZ * NX
    above = lax.ppermute(head, "seq", [(i, i - 1) for i in range(1, count)])
    below = lax.ppermute(tail, "seq", [(i, i + 1) for i in range(count - 1)])
    sums, sizes = call(
        pool_kernel,
        [shape((SEG, FEAT), F32), shape((SEG, 128), F32)],
        [ids, tokens],
        scalars=None,
        flops=1 << 30,
        moved=2 << 20,
        scratch=[pltpu.VMEM((SEG, TOK), BF16)],
    )
    means, u, bias = call(
        norm_kernel,
        [shape((ROWS, FEAT), F32), shape((ROWS, FEAT), BF16), shape((16, FEAT), BF16)],
        [info, sums, sizes, head, above, below, norm_gain.reshape(8, FEAT)],
    )
    first, sibling, second = y_one(u), swap(u), y_other(u)
    across = swap(first)
    part, part_query = shape((SEG, COLS), F32), shape((ROWS, COLS), F32)
    kept = shape((4, FEAT, COLS), BF16)
    queried, keyed, valued, *late = call(
        early_kernel,
        [part_query, part, part] + [kept] * 3,
        [info, u, first, second, sibling, w_query, w_key, w_value],
        scratch=[pltpu.VMEM((4, FEAT, COLS), BF16)] * 3 + [pltpu.SemaphoreType.DMA((2, 4, 3))],
        flops=ROWS * WIDTH * 3 * COLS,
        moved=6 << 20,
        far_in=(5, 6, 7),
        room=ROOM,
    )
    (far,) = gate(info, [y_one(first)], queried)
    blocks = [u, first, second, far, sibling, across, swap(second), swap(far)]
    (kv,) = call(
        key_value_kernel,
        [shape((ROWS, 2 * COLS), BF16)],
        [info] + blocks + [late[1], late[2], keyed, valued, bias],
    )
    (query,) = call(
        query_kernel,
        [shape((ROWS, COLS), BF16)],
        [info] + blocks + [late[0], queried, kv],
        far_in=(11,),
    )
    queries = [query] + [x_by(query, k) for k in (1, 2, 3)]
    one, other = z_one(kv), z_other(kv)
    cut = shape((4, SEG, FEAT), BF16)
    sems = [pltpu.SemaphoreType.DMA((2, 4))]
    mine, theirs = call(
        cut_kernel, [cut, cut], [info, w_out, kv], scratch=sems, far_in=(1, 2), far_out=(0, 1)
    )
    theirs = swap(theirs)
    one2, other2 = z_one(one), z_other(other)
    *state, done = attend_step(1, info, queries, kv, [one, other], None, kv)
    pair = shape((2, SEG, FEAT), BF16)
    pairs = call(
        pair_kernel,
        [pair] * 4,
        [info, mine, theirs, done],
        scratch=sems,
        far_in=range(1, 4),
        far_out=range(4),
    )
    far_weights = y_far(pairs[3])
    one2, other2 = gate(info, [one2, other2], done)
    one3, other3 = z_one(one2), z_other(other2)
    one_weights = y_one(pairs[1])
    *state, done = attend_step(2, info, queries, None, [one2, other2], state, pairs[0])
    one3, other3 = gate(info, [one3, other3], done)
    one4 = z_one(one3)
    other_weights = y_other(pairs[2])
    *state, done = attend_step(3, info, queries, None, [one3, other3], state, far_weights)
    one4, one_weights = gate(info, [one4, one_weights], done)
    partial = attend_step(4, info, queries, None, [one4], state)
    weights = [pairs[0], one_weights, other_weights, far_weights]
    partial = [partial[0]] + [x_by(partial[k], -k) for k in (1, 2, 3)]
    (attended,) = call(
        merge_kernel, [shape((ROWS, COLS), BF16)], [info] + partial + [other_weights], moved=1 << 20, far_in=(5,)
    )
    return output(mp_exchange(attended), weights, means, ids, tokens)


def solution(mesh):
    placed = (
        P(("dp", "seq"), "mp"),
        P(("dp", "seq")),
        P(),
        P(None, "mp"),
        P(None, "mp"),
        P(None, "mp"),
        P("mp", None),
    )
    return jax.shard_map(
        shards, mesh=mesh, in_specs=placed, out_specs=P(("dp", "seq"), "mp"), check_vma=False
    )
```

```python
import functools

import jax
import jax.numpy as jnp
import numpy as np
from jax import lax
from jax.experimental import pallas as pl
from jax.experimental.pallas import tpu as pltpu
from jax.sharding import PartitionSpec as P

HD = 128
NZ, NX, NY, NC = 8, 4, 4, 2
SEG = 256
ROWS = SEG + 16
TOK = 2048
FEAT = 512
COLS = 256
WIDTH = 4096
SCORE = 1.4426950408889634 * HD**-0.5
LOG2E = 1.4426950408889634
LOW = -1e30
VMEM_LIMIT = 20 * 1024 * 1024
ROOM = 48 * 1024 * 1024
F32, BF16 = jnp.float32, jnp.bfloat16


def number(z, x, y, c):
    return ((z % NZ) * NX + x % NX) * (NY * NC) + (y % NY) * NC + c % NC


def everywhere():
    return [(z, x, y, c) for z in range(NZ) for x in range(NX) for y in range(NY) for c in range(NC)]


def way(c):
    return 1 if c == 0 else -1


def move(value, target):
    pairs = [(number(*d), number(*target(*d))) for d in everywhere()]
    return lax.ppermute(value, ("seq", "mp"), pairs)


def swap(value):
    return move(value, lambda z, x, y, c: (z, x, y, 1 - c))


def y_one(value):
    return move(value, lambda z, x, y, c: (z, x, y + way(c), c))


def y_other(value):
    return move(value, lambda z, x, y, c: (z, x, y - way(c), c))


def z_one(value):
    return move(value, lambda z, x, y, c: (z + way(c), x, y, c))


def z_other(value):
    return move(value, lambda z, x, y, c: (z - way(c), x, y, c))


def x_by(value, by):
    return move(value, lambda z, x, y, c: (z, x + by, y, c))


def sources(y, c):
    own = [(y, c), (y - way(c), c), (y + way(c), c), (y + 2, c)]
    o = 1 - c
    other = [(y, o), (y - way(o), o), (y + way(o), o), (y + 2, o)]
    return [((b[0] % NY) * NC + b[1]) for b in own + other]


def mp_exchange(value):
    first = y_one(value)
    second = y_other(value)
    sibling = swap(value)
    far = y_one(first)
    return [value, first, second, far, sibling, swap(first), swap(second), swap(far)]


def device_table():
    rows = []
    for z, x, y, c in everywhere():
        row = [y * NC + c] + sources(y, c)
        row += [x] + [(x - k) % NX for k in (1, 2, 3)]
        for k in (1, 2, 3, 4):
            row += [int((z - way(c) * k) % NZ < z), int((z + way(c) * k) % NZ < z)]
        for o in (c, 1 - c):
            row += [(v % NY) * NC + o for v in (y, y + way(o), y - way(o), y + 2)]
        row += [0] * (32 - len(row))
        rows.append(row)
    return np.asarray(rows, np.int32)


I_MP, I_SRC, I_X, I_OK, I_CUT = 0, 1, 9, 13, 21
SMEM = pl.BlockSpec(memory_space=pltpu.SMEM)
WHOLE = pl.BlockSpec(memory_space=pltpu.VMEM)
FAR = pl.BlockSpec(memory_space=pl.ANY)
DISTANT = pl.BlockSpec(memory_space=pltpu.HBM)


def call(body, outs, ins, flops=0, moved=0, scratch=(), aliases=None, far_in=(), far_out=(), far=FAR, scalars=0, room=VMEM_LIMIT):
    return pl.pallas_call(
        body,
        out_shape=outs,
        in_specs=[SMEM if i == scalars else far if i in far_in else WHOLE for i in range(len(ins))],
        out_specs=[far if i in far_out else WHOLE for i in range(len(outs))],
        scratch_shapes=list(scratch),
        input_output_aliases=aliases or {},
        compiler_params=pltpu.CompilerParams(vmem_limit_bytes=room),
        cost_estimate=pl.CostEstimate(flops=flops, bytes_accessed=moved, transcendentals=0),
    )(*ins)


def gate_kernel(info, *refs):
    pass


def gate(info, values, token):
    ins = [info] + list(values) + [token]
    count = len(values)
    return call(
        gate_kernel,
        [shape(v.shape, v.dtype) for v in values],
        ins,
        aliases={i + 1: i for i in range(count)},
        far_in=range(1, count + 2),
        far_out=range(count),
    )


def shape(dims, dtype):
    return jax.ShapeDtypeStruct(dims, dtype)


def dot(a, b):
    return jnp.dot(a, b, preferred_element_type=F32)


def iota(dims, axis):
    return lax.broadcasted_iota(jnp.int32, dims, axis)


def ones_where(condition):
    return jnp.where(condition, 1.0, 0.0).astype(BF16)


def edge_kernel(flags, tokens, ids_out, head_out, tail_out, marks):
    f = flags[...].astype(F32).astype(BF16)
    upto = ones_where(iota((128, 128), 0) <= iota((128, 128), 1))
    inside = dot(f, upto)
    rows = dot(f, jnp.ones((128, 128), BF16)).astype(BF16)
    before = dot(ones_where(iota((16, 16), 1) < iota((16, 16), 0)), rows)
    ids_out[...] = (inside + before - 1.0).astype(jnp.int32)
    wanted = jnp.where(iota((16, 128), 0) < 8, -1, SEG - 1)
    for r in range(16):
        marks[:, r * 128 : (r + 1) * 128] = ones_where(ids_out[r : r + 1, :] == wanted)
    sums = dot(marks[...], tokens[...])
    counts = dot(marks[...], jnp.ones((TOK, 128), BF16))
    head_out[:, :FEAT] = sums[:8]
    head_out[:, FEAT:] = counts[:8]
    tail_out[:, :FEAT] = sums[8:]
    tail_out[:, FEAT:] = counts[8:]


def pool_kernel(ids, tokens, sums_out, counts_out, hot):
    segment = iota((SEG, 128), 0)
    for r in range(16):
        hot[:, r * 128 : (r + 1) * 128] = ones_where(ids[r : r + 1, :] == segment)
    sums_out[...] = dot(hot[...], tokens[...])
    counts_out[...] = dot(hot[...], jnp.ones((TOK, 128), BF16))


def wide(column, times):
    return jnp.concatenate([column] * times, axis=1)


def split(value, parts):
    out = []
    for _ in range(parts):
        high = value.astype(BF16).astype(F32)
        out.append(high)
        value = value - high
    return out


def norm_kernel(info, sums, counts, head, above, below, gain, means_out, u_out, bias_out):
    g = gain[pl.ds(info[I_MP], 1), :]
    last = iota((SEG, 128), 0) == SEG - 1
    size = counts[...] + jnp.where(last, above[0:1, FEAT:], 0.0)
    total = sums[...] + jnp.where(iota((SEG, FEAT), 0) == SEG - 1, above[0:1, :FEAT], 0.0)
    size = jnp.maximum(size, 1.0)
    means = total / wide(size, 4)
    means_out[:SEG, :] = means
    u_out[:SEG, :] = (means * g).astype(BF16)
    squares = jnp.sum(means * means, axis=1, keepdims=True)
    squares = jnp.transpose(jnp.broadcast_to(squares, (SEG, 128)))[:16]
    high, low = split(squares, 2)
    extra_size = jnp.maximum(head[0:1, FEAT:] + below[0:1, FEAT:], 1.0)
    extra = (head[0:1, :FEAT] + below[0:1, :FEAT]) / wide(extra_size, 4)
    extra_squares = jnp.broadcast_to(jnp.sum(extra * extra, axis=1, keepdims=True), (16, SEG))
    extra_high, extra_low = split(extra_squares, 2)
    row = iota((16, FEAT), 0)
    means_out[SEG:, :] = jnp.where(row == 0, extra, 0.0)
    tail = jnp.where(row == 0, extra * g, 0.0)
    tail = jnp.where(row == 1, jnp.concatenate([high, low], axis=1), tail)
    tail = jnp.where(row == 2, jnp.concatenate([extra_high, extra_low], axis=1), tail)
    u_out[SEG:, :] = tail.astype(BF16)
    bias = jnp.log(jnp.transpose(size)[:16])
    bias_out[...] = jnp.concatenate([bias, bias], axis=1).astype(BF16)


EARLY = (0, 1, 2, 4)
LATE = (3, 5, 6, 7)


def row_scale(tail):
    squares = tail[:, :SEG] + tail[:, SEG:]
    scale = lax.rsqrt(squares / WIDTH + 1e-05)
    column = jnp.transpose(jnp.broadcast_to(scale[1:2, :], (128, SEG)))
    return scale, wide(column, 2)


def product(acc, blocks, weight, rows):
    for i, u in enumerate(blocks):
        acc = acc + dot(u[:rows, :], weight[i])
    return acc


def early_kernel(info, *refs):
    blocks, weights = refs[:4], refs[4:7]
    sums, kept, early, sems = refs[7:10], refs[10:13], refs[13:16], refs[16]
    copies = {}
    for side, (which, target) in enumerate(((EARLY, early), (LATE, kept))):
        for i in range(4):
            start = pl.multiple_of(info[I_SRC + which[i]] * FEAT, FEAT)
            for n in range(3):
                copies[side, i, n] = pltpu.make_async_copy(
                    weights[n].at[pl.ds(start, FEAT), :], target[n].at[i], sems.at[side, i, n]
                )
                copies[side, i, n].start()
    for i, u in enumerate(blocks):
        for n, rows in enumerate((ROWS, SEG, SEG)):
            copies[0, i, n].wait()
            part = dot(u[:rows, :], early[n][i])
            sums[n][...] = part if i == 0 else sums[n][...] + part
    for i in range(4):
        for n in range(3):
            copies[1, i, n].wait()


def square_rows(blocks):
    tail = jnp.zeros((16, FEAT), F32)
    for u in blocks:
        tail = tail + u[SEG:, :].astype(F32)
    return tail


def key_value_kernel(info, *refs):
    blocks, late = refs[:8], [refs[i] for i in LATE]
    w_key, w_value, keys, values, bias, kv_out = refs[8:]
    _, column = row_scale(square_rows(blocks))
    kv_out[:SEG, :COLS] = (product(keys[...], late, w_key, SEG) * column).astype(BF16)
    kv_out[:SEG, COLS:] = (product(values[...], late, w_value, SEG) * column).astype(BF16)
    kv_out[SEG:, :] = bias[...]


def query_kernel(info, *refs):
    blocks, late = refs[:8], [refs[i] for i in LATE]
    w_query, partial, _, q_out = refs[8:]
    scale, column = row_scale(square_rows(blocks))
    query = product(partial[...], late, w_query, ROWS)
    q_out[:SEG, :] = (query[:SEG] * column * SCORE).astype(BF16)
    extra = query[SEG:] * scale[2:3, :] * SCORE
    q_out[SEG:, :] = jnp.where(iota((16, COLS), 0) == 0, extra, 0.0).astype(BF16)


def nt_dot(a, b):
    return lax.dot_general(a, b, (((1,), (1,)), ((), ())), preferred_element_type=F32)


def attend(q, k, v, bias, acc_ref, m_ref, j, h, mask=None):
    scores = nt_dot(q[:, h * HD : (h + 1) * HD], k) + bias
    if mask is not None:
        scores = jnp.where(mask, scores, LOW)
    old = m_ref[j, h]
    peak = jnp.maximum(old, jnp.max(scores, axis=1, keepdims=True))
    expo = jnp.exp2(scores - wide(peak, scores.shape[1] // 128))
    if mask is not None:
        expo = jnp.where(mask, expo, 0.0)
    m_ref[j, h] = peak
    acc_ref[j, h] = acc_ref[j, h] * wide(jnp.exp2(old - peak), 2) + dot(expo.astype(BF16), v)


def keys_of(blocks, h):
    return jnp.concatenate([kv[:SEG, h * HD : (h + 1) * HD] for kv in blocks], axis=0)


def values_of(blocks, h):
    lanes = slice(COLS + h * HD, COLS + (h + 1) * HD)
    values = jnp.concatenate([kv[:SEG, lanes] for kv in blocks], axis=0)
    return jnp.concatenate([values, jnp.ones(values.shape, BF16)], axis=1)


def attend_kernel(step, first, final, info, *refs):
    refs = list(refs)
    queries = [refs.pop(0) for _ in range(4)]
    own = refs.pop(0) if first else None
    others = [refs.pop(0) for _ in range(1 if final else 2)]
    if not first:
        state_in = [refs.pop(0) for _ in range(2)]
    if final:
        payloads = [refs.pop(0) for _ in range(4)]
        acc, m = state_in
    else:
        acc, m, done = refs[:3]
        done[...] = jnp.zeros_like(done)
    if first:
        acc[...] = jnp.zeros_like(acc)
        m[...] = jnp.full(m.shape, LOW, F32)
        bias = own[SEG : SEG + 1, :SEG].astype(F32) * LOG2E
        for j in range(4):

            def one(j=j):
                mask = None
                if j == 0:
                    r, k = iota((ROWS, SEG), 0), iota((ROWS, SEG), 1)
                    mask = (k <= r) & (r < SEG)
                for h in range(2):
                    attend(queries[j], keys_of([own], h), values_of([own], h), bias, acc, m, j, h, mask)

            if j == 0:
                one()
            else:
                pl.when(info[I_X] < info[I_X + j])(one)
    ok = [info[I_OK + 2 * (step - 1) + i] for i in range(len(others))]
    some = ok[0] if final else ok[0] + ok[1]

    @pl.when(some > 0)
    def _():
        biases = []
        for kv, good in zip(others, ok):
            row = kv[SEG : SEG + 1, :SEG].astype(F32) * LOG2E
            biases.append(jnp.where(good > 0, row, LOW))
        bias = jnp.concatenate(biases, axis=1)
        for h in range(2):
            k, v = keys_of(others, h), values_of(others, h)
            for j in range(4):
                attend(queries[j], k, v, bias, acc, m, j, h)

    if final:
        row = iota((16, COLS), 0)
        for j in range(4):
            tail = jnp.zeros((16, COLS), F32)
            ends = []
            for h in range(2):
                total = acc[j, h][:, HD:]
                some_keys = total > 0.0
                total = jnp.where(some_keys, total, 1.0)
                out = acc[j, h][:, :HD] / total
                logs = jnp.where(some_keys, m[j, h] + jnp.log2(total), LOW)
                payloads[j][:SEG, h * HD : (h + 1) * HD] = out[:SEG].astype(BF16)
                ends.append(out[SEG:])
                parts = split(jnp.transpose(logs[:SEG])[:16], 3)
                for i, part in enumerate(parts):
                    tail = jnp.where(row == 1 + 3 * h + i, part, tail)
                parts = split(wide(logs[SEG : SEG + 1], 2), 3)
                for i, part in enumerate(parts):
                    tail = jnp.where(row == 7 + 3 * h + i, part, tail)
            tail = jnp.where(row == 0, jnp.concatenate(ends, axis=1), tail)
            payloads[j][SEG:, :] = tail.astype(BF16)


STATE = [shape((4, 2, ROWS, 2 * HD), F32), shape((4, 2, ROWS, HD), F32), shape((8, 128), F32)]


def attend_step(step, info, queries, own, others, state):
    first, final = own is not None, len(others) == 1
    ins = [info] + queries + ([own] if first else []) + others + list(state or [])
    flops = 4 * 1088 * SEG * (len(others) + (1 if first else 0)) * COLS
    body = functools.partial(attend_kernel, step, first, final)
    if final:
        outs = [shape((ROWS, COLS), BF16)] * 4 + STATE[:2]
        aliases = {len(ins) - 2: 4, len(ins) - 1: 5}

        def body(*refs):
            refs = list(refs)
            payloads, state = refs[-6:-2], refs[-2:]
            attend_kernel(step, first, final, *refs[:-8], *state, *payloads)

        return call(body, outs, ins, flops=flops, moved=4 << 20, aliases=aliases)[:4]
    aliases = {} if first else {len(ins) - 2: 0, len(ins) - 1: 1}
    return call(body, STATE, ins, flops=flops, moved=4 << 20, aliases=aliases)


def merge_kernel(info, a, b, c, d, out):
    parts = (a, b, c, d)
    tails = [p[SEG:, :].astype(F32) for p in parts]
    weights, end_weights = [], []
    for h in range(2):
        for base, store in ((1 + 3 * h, weights), (7 + 3 * h, end_weights)):
            logs = [t[base : base + 1] + t[base + 1 : base + 2] + t[base + 2 : base + 3] for t in tails]
            peak = functools.reduce(jnp.maximum, logs)
            expo = [jnp.exp2(v - peak) for v in logs]
            whole = functools.reduce(jnp.add, expo)
            store.append([e / whole for e in expo])
    flat = weights[0] + weights[1]
    columns = jnp.transpose(jnp.concatenate(flat + [jnp.zeros((120, SEG), F32)], axis=0))
    ends = []
    for h in range(2):
        lanes = slice(h * HD, (h + 1) * HD)
        acc = jnp.zeros((SEG, HD), F32)
        end = jnp.zeros((16, HD), F32)
        for j, p in enumerate(parts):
            acc = acc + columns[:, 4 * h + j : 4 * h + j + 1] * p[:SEG, lanes].astype(F32)
            end = end + end_weights[h][j][:, :HD] * tails[j][:, lanes]
        out[:SEG, lanes] = acc.astype(BF16)
        ends.append(end)
    end = jnp.concatenate(ends, axis=1)
    out[SEG:, :] = jnp.where(iota((16, COLS), 0) == 0, end, 0.0).astype(BF16)


BLOCK = 512
TALL = 384


def mark_kernel(ids, out):
    lane = iota((128, 128), 1)
    for r in range(TOK // 128):
        row = ids[r : r + 1, :].astype(F32)
        column = jnp.transpose(jnp.broadcast_to(row, (128, 128))).astype(jnp.int32)
        rows = slice(r * 128, (r + 1) * 128)
        out[rows, :128] = ones_where(column == lane)
        out[rows, 128:256] = ones_where(column == lane + 128)
        out[rows, 256:] = ones_where((column == -1) & (lane == 0))


def output_kernel(own, first, second, third, hot, tokens, out, coarse):
    @pl.when(pl.program_id(0) == 0)
    def _():
        total = own[...] + first[...].astype(F32) + second[...].astype(F32) + third[...].astype(F32)
        coarse[:ROWS, :] = total.astype(BF16)
        coarse[ROWS:, :] = jnp.zeros((TALL - ROWS, FEAT), BF16)

    picked = dot(hot[...], coarse[...])
    out[...] = (tokens[...].astype(F32) + picked).astype(BF16)


def output(products, hot, tokens):
    return pl.pallas_call(
        output_kernel,
        grid=(TOK // BLOCK,),
        out_shape=shape((TOK, FEAT), BF16),
        in_specs=[WHOLE] * 4
        + [pl.BlockSpec((BLOCK, TALL), lambda i: (i, 0)), pl.BlockSpec((BLOCK, FEAT), lambda i: (i, 0))],
        out_specs=pl.BlockSpec((BLOCK, FEAT), lambda i: (i, 0)),
        scratch_shapes=[pltpu.VMEM((TALL, FEAT), BF16)],
        compiler_params=pltpu.CompilerParams(vmem_limit_bytes=VMEM_LIMIT),
        cost_estimate=pl.CostEstimate(flops=2 << 30, bytes_accessed=6 << 20, transcendentals=0),
    )(*products, hot, tokens)


def cut_kernel(info, w_out, sibling, sems):
    copies = []
    for i in range(4):
        start = pl.multiple_of(info[I_CUT + 4 + i] * FEAT, FEAT)
        copies.append(pltpu.make_async_copy(w_out.at[:, pl.ds(start, FEAT)], sibling.at[i], sems.at[i]))
        copies[-1].start()
    for copy in copies:
        copy.wait()


def product_kernel(info, attended, other, w_out, theirs, means, own_out, *outs):
    for i in range(4):
        start = pl.multiple_of(info[I_CUT + i] * FEAT, FEAT)
        part = dot(attended[...], w_out[:, pl.ds(start, FEAT)]) + dot(other[...], theirs[i])
        if i == 0:
            own_out[...] = part + means[...]
        else:
            outs[i - 1][...] = part.astype(BF16)


def y_far(value):
    return move(value, lambda z, x, y, c: (z, x, y + 2, c))


def shards(tokens, flags, norm_gain, w_query, w_key, w_value, w_out):
    seq, mp = lax.axis_index("seq"), lax.axis_index("mp")
    info = jnp.asarray(device_table())[seq * (NY * NC) + mp]
    edge = shape((8, FEAT + 128), F32)
    ids, head, tail = call(
        edge_kernel,
        [shape((16, 128), jnp.int32), edge, edge],
        [flags.reshape(16, 128), tokens],
        scalars=None,
        flops=1 << 28,
        moved=2 << 20,
        scratch=[pltpu.VMEM((16, TOK), BF16)],
    )
    count = NZ * NX
    above = lax.ppermute(head, "seq", [(i, i - 1) for i in range(1, count)])
    below = lax.ppermute(tail, "seq", [(i, i + 1) for i in range(count - 1)])
    sums, sizes = call(
        pool_kernel,
        [shape((SEG, FEAT), F32), shape((SEG, 128), F32)],
        [ids, tokens],
        scalars=None,
        flops=1 << 30,
        moved=2 << 20,
        scratch=[pltpu.VMEM((SEG, TOK), BF16)],
    )
    means, u, bias = call(
        norm_kernel,
        [shape((ROWS, FEAT), F32), shape((ROWS, FEAT), BF16), shape((16, FEAT), BF16)],
        [info, sums, sizes, head, above, below, norm_gain.reshape(8, FEAT)],
    )
    first, sibling, second = y_one(u), swap(u), y_other(u)
    across = swap(first)
    part, part_query = shape((SEG, COLS), F32), shape((ROWS, COLS), F32)
    kept = shape((4, FEAT, COLS), BF16)
    queried, keyed, valued, *late = call(
        early_kernel,
        [part_query, part, part] + [kept] * 3,
        [info, u, first, second, sibling, w_query, w_key, w_value],
        scratch=[pltpu.VMEM((4, FEAT, COLS), BF16)] * 3 + [pltpu.SemaphoreType.DMA((2, 4, 3))],
        flops=ROWS * WIDTH * 3 * COLS,
        moved=6 << 20,
        far_in=(5, 6, 7),
        room=ROOM,
    )
    (far,) = gate(info, [y_one(first)], queried)
    blocks = [u, first, second, far, sibling, across, swap(second), swap(far)]
    (kv,) = call(
        key_value_kernel,
        [shape((ROWS, 2 * COLS), BF16)],
        [info] + blocks + [late[1], late[2], keyed, valued, bias],
    )
    (query,) = call(
        query_kernel,
        [shape((ROWS, COLS), BF16)],
        [info] + blocks + [late[0], queried, kv],
        far_in=(11,),
    )
    queries = [query] + [x_by(query, k) for k in (1, 2, 3)]
    one, other = z_one(kv), z_other(kv)
    (theirs,) = call(
        cut_kernel,
        [shape((4, SEG, FEAT), BF16)],
        [info, w_out],
        scratch=[pltpu.SemaphoreType.DMA((4,))],
        far_in=(1,),
        far_out=(0,),
    )
    theirs = swap(theirs)
    one2, other2 = z_one(one), z_other(other)
    *state, done = attend_step(1, info, queries, kv, [one, other], None)
    one3, other3 = z_one(one2), z_other(other2)
    *state, done = attend_step(2, info, queries, None, [one2, other2], state)
    one3, other3 = gate(info, [one3, other3], done)
    one4 = z_one(one3)
    *state, done = attend_step(3, info, queries, None, [one3, other3], state)
    partial = attend_step(4, info, queries, None, [one4], state)
    partial = [partial[0]] + [x_by(partial[k], -k) for k in (1, 2, 3)]
    (attended,) = call(merge_kernel, [shape((ROWS, COLS), BF16)], [info] + partial, moved=1 << 20)
    block = shape((ROWS, FEAT), BF16)
    own, first, second, third = call(
        product_kernel,
        [shape((ROWS, FEAT), F32)] + [block] * 3,
        [info, attended, swap(attended), w_out, theirs, means],
        flops=2 * ROWS * 2 * COLS * 4 * FEAT,
        moved=4 << 20,
    )
    (hot,) = call(mark_kernel, [shape((TOK, TALL), BF16)], [ids], flops=1 << 29, moved=3 << 20, scalars=None)
    return output([own, y_one(first), y_other(second), y_far(third)], hot, tokens)


def solution(mesh):
    placed = (
        P(("dp", "seq"), "mp"),
        P(("dp", "seq")),
        P(),
        P(None, "mp"),
        P(None, "mp"),
        P(None, "mp"),
        P("mp", None),
    )
    return jax.shard_map(
        shards, mesh=mesh, in_specs=placed, out_specs=P(("dp", "seq"), "mp"), check_vma=False
    )
```

```python
import functools

import jax
import jax.numpy as jnp
import numpy as np
from jax import lax
from jax.experimental import pallas as pl
from jax.experimental.pallas import tpu as pltpu
from jax.sharding import PartitionSpec as P

HD = 128
NZ, NX, NY, NC = 8, 4, 4, 2
SEG = 256
ROWS = SEG + 16
TOK = 2048
FEAT = 512
COLS = 256
WIDTH = 4096
SCORE = 1.4426950408889634 * HD**-0.5
LOG2E = 1.4426950408889634
LOW = -1e30
VMEM_LIMIT = 20 * 1024 * 1024
ROOM = 48 * 1024 * 1024
F32, BF16 = jnp.float32, jnp.bfloat16


def number(z, x, y, c):
    return ((z % NZ) * NX + x % NX) * (NY * NC) + (y % NY) * NC + c % NC


def everywhere():
    return [(z, x, y, c) for z in range(NZ) for x in range(NX) for y in range(NY) for c in range(NC)]


def way(c):
    return 1 if c == 0 else -1


def move(value, target):
    pairs = [(number(*d), number(*target(*d))) for d in everywhere()]
    return lax.ppermute(value, ("seq", "mp"), pairs)


def swap(value):
    return move(value, lambda z, x, y, c: (z, x, y, 1 - c))


def y_one(value):
    return move(value, lambda z, x, y, c: (z, x, y + way(c), c))


def y_other(value):
    return move(value, lambda z, x, y, c: (z, x, y - way(c), c))


def z_one(value):
    return move(value, lambda z, x, y, c: (z + way(c), x, y, c))


def z_other(value):
    return move(value, lambda z, x, y, c: (z - way(c), x, y, c))


def x_by(value, by):
    return move(value, lambda z, x, y, c: (z, x + by, y, c))


def sources(y, c):
    own = [(y, c), (y - way(c), c), (y + way(c), c), (y + 2, c)]
    o = 1 - c
    other = [(y, o), (y - way(o), o), (y + way(o), o), (y + 2, o)]
    return [((b[0] % NY) * NC + b[1]) for b in own + other]


def mp_exchange(value):
    first = y_one(value)
    second = y_other(value)
    sibling = swap(value)
    far = y_one(first)
    return [value, first, second, far, sibling, swap(first), swap(second), swap(far)]


def device_table():
    rows = []
    for z, x, y, c in everywhere():
        row = [y * NC + c] + sources(y, c)
        row += [x] + [(x - k) % NX for k in (1, 2, 3)]
        for k in (1, 2, 3, 4):
            row += [int((z - way(c) * k) % NZ < z), int((z + way(c) * k) % NZ < z)]
        for o in (c, 1 - c):
            row += [(v % NY) * NC + o for v in (y, y + way(o), y - way(o), y + 2)]
        row += [0] * (32 - len(row))
        rows.append(row)
    return np.asarray(rows, np.int32)


I_MP, I_SRC, I_X, I_OK, I_CUT = 0, 1, 9, 13, 21
SMEM = pl.BlockSpec(memory_space=pltpu.SMEM)
WHOLE = pl.BlockSpec(memory_space=pltpu.VMEM)
FAR = pl.BlockSpec(memory_space=pl.ANY)
DISTANT = pl.BlockSpec(memory_space=pltpu.HBM)


def call(body, outs, ins, flops=0, moved=0, scratch=(), aliases=None, far_in=(), far_out=(), far=FAR, scalars=0, room=VMEM_LIMIT):
    return pl.pallas_call(
        body,
        out_shape=outs,
        in_specs=[SMEM if i == scalars else far if i in far_in else WHOLE for i in range(len(ins))],
        out_specs=[far if i in far_out else WHOLE for i in range(len(outs))],
        scratch_shapes=list(scratch),
        input_output_aliases=aliases or {},
        compiler_params=pltpu.CompilerParams(vmem_limit_bytes=room),
        cost_estimate=pl.CostEstimate(flops=flops, bytes_accessed=moved, transcendentals=0),
    )(*ins)


def gate_kernel(info, *refs):
    pass


def gate(info, values, token):
    ins = [info] + list(values) + [token]
    count = len(values)
    return call(
        gate_kernel,
        [shape(v.shape, v.dtype) for v in values],
        ins,
        aliases={i + 1: i for i in range(count)},
        far_in=range(1, count + 2),
        far_out=range(count),
    )


def shape(dims, dtype):
    return jax.ShapeDtypeStruct(dims, dtype)


def dot(a, b):
    return jnp.dot(a, b, preferred_element_type=F32)


def iota(dims, axis):
    return lax.broadcasted_iota(jnp.int32, dims, axis)


def ones_where(condition):
    return jnp.where(condition, 1.0, 0.0).astype(BF16)


def edge_kernel(flags, tokens, ids_out, head_out, tail_out, marks):
    f = flags[...].astype(F32).astype(BF16)
    upto = ones_where(iota((128, 128), 0) <= iota((128, 128), 1))
    inside = dot(f, upto)
    rows = dot(f, jnp.ones((128, 128), BF16)).astype(BF16)
    before = dot(ones_where(iota((16, 16), 1) < iota((16, 16), 0)), rows)
    ids_out[...] = (inside + before - 1.0).astype(jnp.int32)
    wanted = jnp.where(iota((16, 128), 0) < 8, -1, SEG - 1)
    for r in range(16):
        marks[:, r * 128 : (r + 1) * 128] = ones_where(ids_out[r : r + 1, :] == wanted)
    sums = dot(marks[...], tokens[...])
    counts = dot(marks[...], jnp.ones((TOK, 128), BF16))
    head_out[:, :FEAT] = sums[:8]
    head_out[:, FEAT:] = counts[:8]
    tail_out[:, :FEAT] = sums[8:]
    tail_out[:, FEAT:] = counts[8:]


def pool_kernel(ids, tokens, sums_out, counts_out, hot):
    segment = iota((SEG, 128), 0)
    for r in range(16):
        hot[:, r * 128 : (r + 1) * 128] = ones_where(ids[r : r + 1, :] == segment)
    sums_out[...] = dot(hot[...], tokens[...])
    counts_out[...] = dot(hot[...], jnp.ones((TOK, 128), BF16))


def wide(column, times):
    return jnp.concatenate([column] * times, axis=1)


def split(value, parts):
    out = []
    for _ in range(parts):
        high = value.astype(BF16).astype(F32)
        out.append(high)
        value = value - high
    return out


def norm_kernel(info, sums, counts, head, above, below, gain, means_out, u_out, bias_out):
    g = gain[pl.ds(info[I_MP], 1), :]
    last = iota((SEG, 128), 0) == SEG - 1
    size = counts[...] + jnp.where(last, above[0:1, FEAT:], 0.0)
    total = sums[...] + jnp.where(iota((SEG, FEAT), 0) == SEG - 1, above[0:1, :FEAT], 0.0)
    size = jnp.maximum(size, 1.0)
    means = total / wide(size, 4)
    means_out[:SEG, :] = means
    u_out[:SEG, :] = (means * g).astype(BF16)
    squares = jnp.sum(means * means, axis=1, keepdims=True)
    squares = jnp.transpose(jnp.broadcast_to(squares, (SEG, 128)))[:16]
    high, low = split(squares, 2)
    extra_size = jnp.maximum(head[0:1, FEAT:] + below[0:1, FEAT:], 1.0)
    extra = (head[0:1, :FEAT] + below[0:1, :FEAT]) / wide(extra_size, 4)
    extra_squares = jnp.broadcast_to(jnp.sum(extra * extra, axis=1, keepdims=True), (16, SEG))
    extra_high, extra_low = split(extra_squares, 2)
    row = iota((16, FEAT), 0)
    means_out[SEG:, :] = jnp.where(row == 0, extra, 0.0)
    tail = jnp.where(row == 0, extra * g, 0.0)
    tail = jnp.where(row == 1, jnp.concatenate([high, low], axis=1), tail)
    tail = jnp.where(row == 2, jnp.concatenate([extra_high, extra_low], axis=1), tail)
    u_out[SEG:, :] = tail.astype(BF16)
    bias = jnp.log(jnp.transpose(size)[:16])
    bias_out[...] = jnp.concatenate([bias, bias], axis=1).astype(BF16)


EARLY = (0, 1, 2, 4)
LATE = (3, 5, 6, 7)


def row_scale(tail):
    squares = tail[:, :SEG] + tail[:, SEG:]
    scale = lax.rsqrt(squares / WIDTH + 1e-05)
    column = jnp.transpose(jnp.broadcast_to(scale[1:2, :], (128, SEG)))
    return scale, wide(column, 2)


def product(acc, blocks, weight, rows):
    for i, u in enumerate(blocks):
        acc = acc + dot(u[:rows, :], weight[i])
    return acc


def early_kernel(info, *refs):
    blocks, weights = refs[:4], refs[4:7]
    sums, kept, early, sems = refs[7:10], refs[10:13], refs[13:16], refs[16]
    copies = {}
    for side, (which, target) in enumerate(((EARLY, early), (LATE, kept))):
        for i in range(4):
            start = pl.multiple_of(info[I_SRC + which[i]] * FEAT, FEAT)
            for n in range(3):
                copies[side, i, n] = pltpu.make_async_copy(
                    weights[n].at[pl.ds(start, FEAT), :], target[n].at[i], sems.at[side, i, n]
                )
                copies[side, i, n].start()
    for i, u in enumerate(blocks):
        for n, rows in enumerate((ROWS, SEG, SEG)):
            copies[0, i, n].wait()
            part = dot(u[:rows, :], early[n][i])
            sums[n][...] = part if i == 0 else sums[n][...] + part
    for i in range(4):
        for n in range(3):
            copies[1, i, n].wait()


def square_rows(blocks):
    tail = jnp.zeros((16, FEAT), F32)
    for u in blocks:
        tail = tail + u[SEG:, :].astype(F32)
    return tail


def key_value_kernel(info, *refs):
    blocks, late = refs[:8], [refs[i] for i in LATE]
    w_key, w_value, keys, values, bias, kv_out = refs[8:]
    _, column = row_scale(square_rows(blocks))
    kv_out[:SEG, :COLS] = (product(keys[...], late, w_key, SEG) * column).astype(BF16)
    kv_out[:SEG, COLS:] = (product(values[...], late, w_value, SEG) * column).astype(BF16)
    kv_out[SEG:, :] = bias[...]


def query_kernel(info, *refs):
    blocks, late = refs[:8], [refs[i] for i in LATE]
    w_query, partial, _, q_out = refs[8:]
    scale, column = row_scale(square_rows(blocks))
    query = product(partial[...], late, w_query, ROWS)
    q_out[:SEG, :] = (query[:SEG] * column * SCORE).astype(BF16)
    extra = query[SEG:] * scale[2:3, :] * SCORE
    q_out[SEG:, :] = jnp.where(iota((16, COLS), 0) == 0, extra, 0.0).astype(BF16)


def nt_dot(a, b):
    return lax.dot_general(a, b, (((1,), (1,)), ((), ())), preferred_element_type=F32)


def attend(q, k, v, bias, acc_ref, m_ref, j, h, mask=None):
    scores = nt_dot(q[:, h * HD : (h + 1) * HD], k) + bias
    if mask is not None:
        scores = jnp.where(mask, scores, LOW)
    old = m_ref[j, h]
    peak = jnp.maximum(old, jnp.max(scores, axis=1, keepdims=True))
    expo = jnp.exp2(scores - wide(peak, scores.shape[1] // 128))
    if mask is not None:
        expo = jnp.where(mask, expo, 0.0)
    m_ref[j, h] = peak
    acc_ref[j, h] = acc_ref[j, h] * wide(jnp.exp2(old - peak), 2) + dot(expo.astype(BF16), v)


def keys_of(blocks, h):
    return jnp.concatenate([kv[:SEG, h * HD : (h + 1) * HD] for kv in blocks], axis=0)


def values_of(blocks, h):
    lanes = slice(COLS + h * HD, COLS + (h + 1) * HD)
    values = jnp.concatenate([kv[:SEG, lanes] for kv in blocks], axis=0)
    return jnp.concatenate([values, jnp.ones(values.shape, BF16)], axis=1)


def attend_kernel(step, first, final, info, *refs):
    refs = list(refs)
    queries = [refs.pop(0) for _ in range(4)]
    own = refs.pop(0) if first else None
    others = [refs.pop(0) for _ in range(1 if final else 2)]
    if not first:
        state_in = [refs.pop(0) for _ in range(2)]
    if final:
        payloads = [refs.pop(0) for _ in range(4)]
        acc, m = state_in
    else:
        acc, m, done = refs[:3]
        done[...] = jnp.zeros_like(done)
    if first:
        acc[...] = jnp.zeros_like(acc)
        m[...] = jnp.full(m.shape, LOW, F32)
        bias = own[SEG : SEG + 1, :SEG].astype(F32) * LOG2E
        for j in range(4):

            def one(j=j):
                mask = None
                if j == 0:
                    r, k = iota((ROWS, SEG), 0), iota((ROWS, SEG), 1)
                    mask = (k <= r) & (r < SEG)
                for h in range(2):
                    attend(queries[j], keys_of([own], h), values_of([own], h), bias, acc, m, j, h, mask)

            if j == 0:
                one()
            else:
                pl.when(info[I_X] < info[I_X + j])(one)
    ok = [info[I_OK + 2 * (step - 1) + i] for i in range(len(others))]
    some = ok[0] if final else ok[0] + ok[1]

    @pl.when(some > 0)
    def _():
        biases = []
        for kv, good in zip(others, ok):
            row = kv[SEG : SEG + 1, :SEG].astype(F32) * LOG2E
            biases.append(jnp.where(good > 0, row, LOW))
        bias = jnp.concatenate(biases, axis=1)
        for h in range(2):
            k, v = keys_of(others, h), values_of(others, h)
            for j in range(4):
                attend(queries[j], k, v, bias, acc, m, j, h)

    if final:
        row = iota((16, COLS), 0)
        for j in range(4):
            tail = jnp.zeros((16, COLS), F32)
            ends = []
            for h in range(2):
                total = acc[j, h][:, HD:]
                some_keys = total > 0.0
                total = jnp.where(some_keys, total, 1.0)
                out = acc[j, h][:, :HD] / total
                logs = jnp.where(some_keys, m[j, h] + jnp.log2(total), LOW)
                payloads[j][:SEG, h * HD : (h + 1) * HD] = out[:SEG].astype(BF16)
                ends.append(out[SEG:])
                parts = split(jnp.transpose(logs[:SEG])[:16], 3)
                for i, part in enumerate(parts):
                    tail = jnp.where(row == 1 + 3 * h + i, part, tail)
                parts = split(wide(logs[SEG : SEG + 1], 2), 3)
                for i, part in enumerate(parts):
                    tail = jnp.where(row == 7 + 3 * h + i, part, tail)
            tail = jnp.where(row == 0, jnp.concatenate(ends, axis=1), tail)
            payloads[j][SEG:, :] = tail.astype(BF16)


STATE = [shape((4, 2, ROWS, 2 * HD), F32), shape((4, 2, ROWS, HD), F32), shape((8, 128), F32)]


def attend_step(step, info, queries, own, others, state):
    first, final = own is not None, len(others) == 1
    ins = [info] + queries + ([own] if first else []) + others + list(state or [])
    flops = 4 * 1088 * SEG * (len(others) + (1 if first else 0)) * COLS
    body = functools.partial(attend_kernel, step, first, final)
    if final:
        outs = [shape((ROWS, COLS), BF16)] * 4 + STATE[:2]
        aliases = {len(ins) - 2: 4, len(ins) - 1: 5}

        def body(*refs):
            refs = list(refs)
            payloads, state = refs[-6:-2], refs[-2:]
            attend_kernel(step, first, final, *refs[:-8], *state, *payloads)

        return call(body, outs, ins, flops=flops, moved=4 << 20, aliases=aliases)[:4]
    aliases = {} if first else {len(ins) - 2: 0, len(ins) - 1: 1}
    return call(body, STATE, ins, flops=flops, moved=4 << 20, aliases=aliases)


def merge_kernel(info, a, b, c, d, out):
    parts = (a, b, c, d)
    tails = [p[SEG:, :].astype(F32) for p in parts]
    weights, end_weights = [], []
    for h in range(2):
        for base, store in ((1 + 3 * h, weights), (7 + 3 * h, end_weights)):
            logs = [t[base : base + 1] + t[base + 1 : base + 2] + t[base + 2 : base + 3] for t in tails]
            peak = functools.reduce(jnp.maximum, logs)
            expo = [jnp.exp2(v - peak) for v in logs]
            whole = functools.reduce(jnp.add, expo)
            store.append([e / whole for e in expo])
    flat = weights[0] + weights[1]
    columns = jnp.transpose(jnp.concatenate(flat + [jnp.zeros((120, SEG), F32)], axis=0))
    ends = []
    for h in range(2):
        lanes = slice(h * HD, (h + 1) * HD)
        acc = jnp.zeros((SEG, HD), F32)
        end = jnp.zeros((16, HD), F32)
        for j, p in enumerate(parts):
            acc = acc + columns[:, 4 * h + j : 4 * h + j + 1] * p[:SEG, lanes].astype(F32)
            end = end + end_weights[h][j][:, :HD] * tails[j][:, lanes]
        out[:SEG, lanes] = acc.astype(BF16)
        ends.append(end)
    end = jnp.concatenate(ends, axis=1)
    out[SEG:, :] = jnp.where(iota((16, COLS), 0) == 0, end, 0.0).astype(BF16)


BLOCK = 512
TALL = 384


def mark_kernel(ids, out):
    lane = iota((128, 128), 1)
    for r in range(TOK // 128):
        row = ids[r : r + 1, :].astype(F32)
        column = jnp.transpose(jnp.broadcast_to(row, (128, 128))).astype(jnp.int32)
        rows = slice(r * 128, (r + 1) * 128)
        out[rows, :128] = ones_where(column == lane)
        out[rows, 128:256] = ones_where(column == lane + 128)
        out[rows, 256:] = ones_where((column == -1) & (lane == 0))


def output_kernel(own, first, second, hot, tokens, out, coarse):
    @pl.when(pl.program_id(0) == 0)
    def _():
        total = own[...] + first[...].astype(F32) + second[...].astype(F32)
        coarse[:ROWS, :] = total.astype(BF16)
        coarse[ROWS:, :] = jnp.zeros((TALL - ROWS, FEAT), BF16)

    picked = dot(hot[...], coarse[...])
    out[...] = (tokens[...].astype(F32) + picked).astype(BF16)


def output(products, hot, tokens):
    return pl.pallas_call(
        output_kernel,
        grid=(TOK // BLOCK,),
        out_shape=shape((TOK, FEAT), BF16),
        in_specs=[WHOLE] * 3
        + [pl.BlockSpec((BLOCK, TALL), lambda i: (i, 0)), pl.BlockSpec((BLOCK, FEAT), lambda i: (i, 0))],
        out_specs=pl.BlockSpec((BLOCK, FEAT), lambda i: (i, 0)),
        scratch_shapes=[pltpu.VMEM((TALL, FEAT), BF16)],
        compiler_params=pltpu.CompilerParams(vmem_limit_bytes=VMEM_LIMIT),
        cost_estimate=pl.CostEstimate(flops=2 << 30, bytes_accessed=6 << 20, transcendentals=0),
    )(*products, hot, tokens)


def cut_kernel(info, w_out, _, sibling, sems):
    copies = []
    for i in range(4):
        start = pl.multiple_of(info[I_CUT + 4 + i] * FEAT, FEAT)
        copies.append(pltpu.make_async_copy(w_out.at[:, pl.ds(start, FEAT)], sibling.at[i], sems.at[i]))
        copies[-1].start()
    for copy in copies:
        copy.wait()


def product_kernel(info, attended, other, w_out, theirs, means, own_out, *outs):
    for i in range(4):
        start = pl.multiple_of(info[I_CUT + i] * FEAT, FEAT)
        part = dot(attended[...], w_out[:, pl.ds(start, FEAT)]) + dot(other[...], theirs[i])
        if i == 0:
            own_out[...] = part + means[...]
        else:
            outs[i - 1][...] = part.astype(outs[i - 1].dtype)


def add_kernel(a, b, out):
    out[...] = (a[...] + b[...].astype(F32)).astype(BF16)


def shards(tokens, flags, norm_gain, w_query, w_key, w_value, w_out):
    seq, mp = lax.axis_index("seq"), lax.axis_index("mp")
    info = jnp.asarray(device_table())[seq * (NY * NC) + mp]
    edge = shape((8, FEAT + 128), F32)
    ids, head, tail = call(
        edge_kernel,
        [shape((16, 128), jnp.int32), edge, edge],
        [flags.reshape(16, 128), tokens],
        scalars=None,
        flops=1 << 28,
        moved=2 << 20,
        scratch=[pltpu.VMEM((16, TOK), BF16)],
    )
    count = NZ * NX
    above = lax.ppermute(head, "seq", [(i, i - 1) for i in range(1, count)])
    below = lax.ppermute(tail, "seq", [(i, i + 1) for i in range(count - 1)])
    sums, sizes = call(
        pool_kernel,
        [shape((SEG, FEAT), F32), shape((SEG, 128), F32)],
        [ids, tokens],
        scalars=None,
        flops=1 << 30,
        moved=2 << 20,
        scratch=[pltpu.VMEM((SEG, TOK), BF16)],
    )
    means, u, bias = call(
        norm_kernel,
        [shape((ROWS, FEAT), F32), shape((ROWS, FEAT), BF16), shape((16, FEAT), BF16)],
        [info, sums, sizes, head, above, below, norm_gain.reshape(8, FEAT)],
    )
    first, sibling, second = y_one(u), swap(u), y_other(u)
    across = swap(first)
    part, part_query = shape((SEG, COLS), F32), shape((ROWS, COLS), F32)
    kept = shape((4, FEAT, COLS), BF16)
    queried, keyed, valued, *late = call(
        early_kernel,
        [part_query, part, part] + [kept] * 3,
        [info, u, first, second, sibling, w_query, w_key, w_value],
        scratch=[pltpu.VMEM((4, FEAT, COLS), BF16)] * 3 + [pltpu.SemaphoreType.DMA((2, 4, 3))],
        flops=ROWS * WIDTH * 3 * COLS,
        moved=6 << 20,
        far_in=(5, 6, 7),
        room=ROOM,
    )
    (far,) = gate(info, [y_one(first)], queried)
    blocks = [u, first, second, far, sibling, across, swap(second), swap(far)]
    (kv,) = call(
        key_value_kernel,
        [shape((ROWS, 2 * COLS), BF16)],
        [info] + blocks + [late[1], late[2], keyed, valued, bias],
    )
    (query,) = call(
        query_kernel,
        [shape((ROWS, COLS), BF16)],
        [info] + blocks + [late[0], queried, kv],
        far_in=(11,),
    )
    queries = [query] + [x_by(query, k) for k in (1, 2, 3)]
    one, other = z_one(kv), z_other(kv)
    one2, other2 = z_one(one), z_other(other)
    *state, done = attend_step(1, info, queries, kv, [one, other], None)
    (theirs,) = call(
        cut_kernel,
        [shape((4, SEG, FEAT), BF16)],
        [info, w_out, done],
        scratch=[pltpu.SemaphoreType.DMA((4,))],
        far_in=(1, 2),
        far_out=(0,),
    )
    theirs = swap(theirs)
    one2, other2 = gate(info, [one2, other2], done)
    one3, other3 = z_one(one2), z_other(other2)
    *state, done = attend_step(2, info, queries, None, [one2, other2], state)
    one4 = z_one(one3)
    *state, done = attend_step(3, info, queries, None, [one3, other3], state)
    partial = attend_step(4, info, queries, None, [one4], state)
    partial = [partial[0]] + [x_by(partial[k], -k) for k in (1, 2, 3)]
    (attended,) = call(merge_kernel, [shape((ROWS, COLS), BF16)], [info] + partial, moved=1 << 20)
    block = shape((ROWS, FEAT), BF16)
    own, first, second, third = call(
        product_kernel,
        [shape((ROWS, FEAT), F32)] * 2 + [block] * 2,
        [info, attended, swap(attended), w_out, theirs, means],
        flops=2 * ROWS * 2 * COLS * 4 * FEAT,
        moved=4 << 20,
    )
    (hot,) = call(mark_kernel, [shape((TOK, TALL), BF16)], [ids], flops=1 << 29, moved=3 << 20, scalars=None)
    (first,) = call(add_kernel, [block], [first, y_one(third)], scalars=None)
    return output([own, y_one(first), y_other(second)], hot, tokens)


def solution(mesh):
    placed = (
        P(("dp", "seq"), "mp"),
        P(("dp", "seq")),
        P(),
        P(None, "mp"),
        P(None, "mp"),
        P(None, "mp"),
        P("mp", None),
    )
    return jax.shard_map(
        shards, mesh=mesh, in_specs=placed, out_specs=P(("dp", "seq"), "mp"), check_vma=False
    )
```

```python
import functools

import jax
import jax.numpy as jnp
import numpy as np
from jax import lax
from jax.experimental import pallas as pl
from jax.experimental.pallas import tpu as pltpu
from jax.sharding import PartitionSpec as P

HD = 128
NZ, NX, NY, NC = 8, 4, 4, 2
SEG = 256
ROWS = SEG + 16
TOK = 2048
FEAT = 512
COLS = 256
WIDTH = 4096
SCORE = 1.4426950408889634 * HD**-0.5
LOG2E = 1.4426950408889634
LOW = -1e30
VMEM_LIMIT = 20 * 1024 * 1024
ROOM = 47 * 1024 * 1024
F32, BF16 = jnp.float32, jnp.bfloat16


def number(z, x, y, c):
    return ((z % NZ) * NX + x % NX) * (NY * NC) + (y % NY) * NC + c % NC


def everywhere():
    return [(z, x, y, c) for z in range(NZ) for x in range(NX) for y in range(NY) for c in range(NC)]


def way(c):
    return 1 if c == 0 else -1


def move(value, target):
    pairs = [(number(*d), number(*target(*d))) for d in everywhere()]
    return lax.ppermute(value, ("seq", "mp"), pairs)


def swap(value):
    return move(value, lambda z, x, y, c: (z, x, y, 1 - c))


def y_one(value):
    return move(value, lambda z, x, y, c: (z, x, y + way(c), c))


def y_other(value):
    return move(value, lambda z, x, y, c: (z, x, y - way(c), c))


def z_one(value):
    return move(value, lambda z, x, y, c: (z + way(c), x, y, c))


def z_other(value):
    return move(value, lambda z, x, y, c: (z - way(c), x, y, c))


def x_by(value, by):
    return move(value, lambda z, x, y, c: (z, x + by, y, c))


def sources(y, c):
    own = [(y, c), (y - way(c), c), (y + way(c), c), (y + 2, c)]
    o = 1 - c
    other = [(y, o), (y - way(o), o), (y + way(o), o), (y + 2, o)]
    return [((b[0] % NY) * NC + b[1]) for b in own + other]


def mp_exchange(value):
    first = y_one(value)
    second = y_other(value)
    sibling = swap(value)
    far = y_one(first)
    return [value, first, second, far, sibling, swap(first), swap(second), swap(far)]


def device_table():
    rows = []
    for z, x, y, c in everywhere():
        row = [y * NC + c] + sources(y, c)
        row += [x] + [(x - k) % NX for k in (1, 2, 3)]
        for k in (1, 2, 3, 4):
            row += [int((z - way(c) * k) % NZ < z), int((z + way(c) * k) % NZ < z)]
        for o in (c, 1 - c):
            row += [(v % NY) * NC + o for v in (y, y + way(o), y - way(o), y + 2)]
        row += [0] * (32 - len(row))
        rows.append(row)
    return np.asarray(rows, np.int32)


I_MP, I_SRC, I_X, I_OK, I_CUT = 0, 1, 9, 13, 21
SMEM = pl.BlockSpec(memory_space=pltpu.SMEM)
WHOLE = pl.BlockSpec(memory_space=pltpu.VMEM)
FAR = pl.BlockSpec(memory_space=pl.ANY)
DISTANT = pl.BlockSpec(memory_space=pltpu.HBM)


def call(body, outs, ins, flops=0, moved=0, scratch=(), aliases=None, far_in=(), far_out=(), far=FAR, scalars=0, room=VMEM_LIMIT):
    return pl.pallas_call(
        body,
        out_shape=outs,
        in_specs=[SMEM if i == scalars else far if i in far_in else WHOLE for i in range(len(ins))],
        out_specs=[far if i in far_out else WHOLE for i in range(len(outs))],
        scratch_shapes=list(scratch),
        input_output_aliases=aliases or {},
        compiler_params=pltpu.CompilerParams(vmem_limit_bytes=room),
        cost_estimate=pl.CostEstimate(flops=flops, bytes_accessed=moved, transcendentals=0),
    )(*ins)


def gate_kernel(info, *refs):
    pass


def gate(info, values, token):
    ins = [info] + list(values) + [token]
    count = len(values)
    return call(
        gate_kernel,
        [shape(v.shape, v.dtype) for v in values],
        ins,
        aliases={i + 1: i for i in range(count)},
        far_in=range(1, count + 2),
        far_out=range(count),
    )


def shape(dims, dtype):
    return jax.ShapeDtypeStruct(dims, dtype)


def dot(a, b):
    return jnp.dot(a, b, preferred_element_type=F32)


def iota(dims, axis):
    return lax.broadcasted_iota(jnp.int32, dims, axis)


def ones_where(condition):
    return jnp.where(condition, 1.0, 0.0).astype(BF16)


def edge_kernel(flags, tokens, ids_out, head_out, tail_out, marks):
    f = flags[...].astype(F32).astype(BF16)
    upto = ones_where(iota((128, 128), 0) <= iota((128, 128), 1))
    inside = dot(f, upto)
    rows = dot(f, jnp.ones((128, 128), BF16)).astype(BF16)
    before = dot(ones_where(iota((16, 16), 1) < iota((16, 16), 0)), rows)
    ids_out[...] = (inside + before - 1.0).astype(jnp.int32)
    wanted = jnp.where(iota((16, 128), 0) < 8, -1, SEG - 1)
    for r in range(16):
        marks[:, r * 128 : (r + 1) * 128] = ones_where(ids_out[r : r + 1, :] == wanted)
    sums = dot(marks[...], tokens[...])
    counts = dot(marks[...], jnp.ones((TOK, 128), BF16))
    head_out[:, :FEAT] = sums[:8]
    head_out[:, FEAT:] = counts[:8]
    tail_out[:, :FEAT] = sums[8:]
    tail_out[:, FEAT:] = counts[8:]


def pool_kernel(ids, tokens, sums_out, counts_out, hot):
    segment = iota((SEG, 128), 0)
    for r in range(16):
        hot[:, r * 128 : (r + 1) * 128] = ones_where(ids[r : r + 1, :] == segment)
    sums_out[...] = dot(hot[...], tokens[...])
    counts_out[...] = dot(hot[...], jnp.ones((TOK, 128), BF16))


def wide(column, times):
    return jnp.concatenate([column] * times, axis=1)


def split(value, parts):
    out = []
    for _ in range(parts):
        high = value.astype(BF16).astype(F32)
        out.append(high)
        value = value - high
    return out


def norm_kernel(info, sums, counts, head, above, below, gain, _, means_out, u_out, bias_out):
    g = gain[pl.ds(info[I_MP], 1), :]
    last = iota((SEG, 128), 0) == SEG - 1
    size = counts[...] + jnp.where(last, above[0:1, FEAT:], 0.0)
    total = sums[...] + jnp.where(iota((SEG, FEAT), 0) == SEG - 1, above[0:1, :FEAT], 0.0)
    size = jnp.maximum(size, 1.0)
    means = total / wide(size, 4)
    means_out[:SEG, :] = means
    u_out[:SEG, :] = (means * g).astype(BF16)
    squares = jnp.sum(means * means, axis=1, keepdims=True)
    squares = jnp.transpose(jnp.broadcast_to(squares, (SEG, 128)))[:16]
    high, low = split(squares, 2)
    extra_size = jnp.maximum(head[0:1, FEAT:] + below[0:1, FEAT:], 1.0)
    extra = (head[0:1, :FEAT] + below[0:1, :FEAT]) / wide(extra_size, 4)
    extra_squares = jnp.broadcast_to(jnp.sum(extra * extra, axis=1, keepdims=True), (16, SEG))
    extra_high, extra_low = split(extra_squares, 2)
    row = iota((16, FEAT), 0)
    means_out[SEG:, :] = jnp.where(row == 0, extra, 0.0)
    tail = jnp.where(row == 0, extra * g, 0.0)
    tail = jnp.where(row == 1, jnp.concatenate([high, low], axis=1), tail)
    tail = jnp.where(row == 2, jnp.concatenate([extra_high, extra_low], axis=1), tail)
    u_out[SEG:, :] = tail.astype(BF16)
    bias = jnp.log(jnp.transpose(size)[:16])
    bias_out[...] = jnp.concatenate([bias, bias], axis=1).astype(BF16)


EARLY = (0, 1, 2, 4)
LATE = (3, 5, 6, 7)


def row_scale(tail):
    squares = tail[:, :SEG] + tail[:, SEG:]
    scale = lax.rsqrt(squares / WIDTH + 1e-05)
    column = jnp.transpose(jnp.broadcast_to(scale[1:2, :], (128, SEG)))
    return scale, wide(column, 2)


def load_kernel(_, *refs):
    sources, outs, done, sems = refs[:3], refs[3:6], refs[6], refs[7]
    copies = []
    for n in range(3):
        for i in range(4):
            rows = pl.ds(i * (WIDTH // 4), WIDTH // 4)
            copies.append(pltpu.make_async_copy(sources[n].at[rows, :], outs[n].at[rows, :], sems.at[n, i]))
            copies[-1].start()
    done[...] = jnp.zeros_like(done)
    for copy in copies:
        copy.wait()


def product(info, acc, blocks, which, weight, rows):
    for i, u in zip(which, blocks):
        start = pl.multiple_of(info[I_SRC + i] * FEAT, FEAT)
        part = dot(u[:rows, :], weight[pl.ds(start, FEAT), :])
        acc = part if acc is None else acc + part
    return acc


def early_kernel(info, *refs):
    blocks, weights, sums = refs[:4], refs[4:7], refs[7:]
    for n, rows in enumerate((ROWS, SEG, SEG)):
        sums[n][...] = product(info, None, blocks, EARLY, weights[n], rows)


def square_rows(blocks):
    tail = jnp.zeros((16, FEAT), F32)
    for u in blocks:
        tail = tail + u[SEG:, :].astype(F32)
    return tail


def key_value_kernel(info, *refs):
    blocks, late = refs[:8], [refs[i] for i in LATE]
    w_key, w_value, keys, values, bias, kv_out = refs[8:]
    _, column = row_scale(square_rows(blocks))
    kv_out[:SEG, :COLS] = (product(info, keys[...], late, LATE, w_key, SEG) * column).astype(BF16)
    kv_out[:SEG, COLS:] = (product(info, values[...], late, LATE, w_value, SEG) * column).astype(BF16)
    kv_out[SEG:, :] = bias[...]


def query_kernel(info, *refs):
    blocks, late = refs[:8], [refs[i] for i in LATE]
    w_query, partial, _, q_out = refs[8:]
    scale, column = row_scale(square_rows(blocks))
    query = product(info, partial[...], late, LATE, w_query, ROWS)
    q_out[:SEG, :] = (query[:SEG] * column * SCORE).astype(BF16)
    extra = query[SEG:] * scale[2:3, :] * SCORE
    q_out[SEG:, :] = jnp.where(iota((16, COLS), 0) == 0, extra, 0.0).astype(BF16)


def nt_dot(a, b):
    return lax.dot_general(a, b, (((1,), (1,)), ((), ())), preferred_element_type=F32)


def attend(q, k, v, bias, acc_ref, m_ref, j, h, mask=None):
    scores = nt_dot(q[:, h * HD : (h + 1) * HD], k) + bias
    if mask is not None:
        scores = jnp.where(mask, scores, LOW)
    old = m_ref[j, h]
    peak = jnp.maximum(old, jnp.max(scores, axis=1, keepdims=True))
    expo = jnp.exp2(scores - wide(peak, scores.shape[1] // 128))
    if mask is not None:
        expo = jnp.where(mask, expo, 0.0)
    m_ref[j, h] = peak
    acc_ref[j, h] = acc_ref[j, h] * wide(jnp.exp2(old - peak), 2) + dot(expo.astype(BF16), v)


def keys_of(blocks, h):
    return jnp.concatenate([kv[:SEG, h * HD : (h + 1) * HD] for kv in blocks], axis=0)


def values_of(blocks, h):
    lanes = slice(COLS + h * HD, COLS + (h + 1) * HD)
    values = jnp.concatenate([kv[:SEG, lanes] for kv in blocks], axis=0)
    return jnp.concatenate([values, jnp.ones(values.shape, BF16)], axis=1)


def attend_kernel(step, first, final, info, *refs):
    refs = list(refs)
    queries = [refs.pop(0) for _ in range(4)]
    own = refs.pop(0) if first else None
    others = [refs.pop(0) for _ in range(1 if final else 2)]
    if not first:
        state_in = [refs.pop(0) for _ in range(2)]
    if final:
        payloads = [refs.pop(0) for _ in range(4)]
        acc, m = state_in
    else:
        acc, m, done = refs[:3]
        done[...] = jnp.zeros_like(done)
    if first:
        acc[...] = jnp.zeros_like(acc)
        m[...] = jnp.full(m.shape, LOW, F32)
        bias = own[SEG : SEG + 1, :SEG].astype(F32) * LOG2E
        for j in range(4):

            def one(j=j):
                mask = None
                if j == 0:
                    r, k = iota((ROWS, SEG), 0), iota((ROWS, SEG), 1)
                    mask = (k <= r) & (r < SEG)
                for h in range(2):
                    attend(queries[j], keys_of([own], h), values_of([own], h), bias, acc, m, j, h, mask)

            if j == 0:
                one()
            else:
                pl.when(info[I_X] < info[I_X + j])(one)
    ok = [info[I_OK + 2 * (step - 1) + i] for i in range(len(others))]
    some = ok[0] if final else ok[0] + ok[1]

    @pl.when(some > 0)
    def _():
        biases = []
        for kv, good in zip(others, ok):
            row = kv[SEG : SEG + 1, :SEG].astype(F32) * LOG2E
            biases.append(jnp.where(good > 0, row, LOW))
        bias = jnp.concatenate(biases, axis=1)
        for h in range(2):
            k, v = keys_of(others, h), values_of(others, h)
            for j in range(4):
                attend(queries[j], k, v, bias, acc, m, j, h)

    if final:
        row = iota((16, COLS), 0)
        for j in range(4):
            tail = jnp.zeros((16, COLS), F32)
            ends = []
            for h in range(2):
                total = acc[j, h][:, HD:]
                some_keys = total > 0.0
                total = jnp.where(some_keys, total, 1.0)
                out = acc[j, h][:, :HD] / total
                logs = jnp.where(some_keys, m[j, h] + jnp.log2(total), LOW)
                payloads[j][:SEG, h * HD : (h + 1) * HD] = out[:SEG].astype(BF16)
                ends.append(out[SEG:])
                parts = split(jnp.transpose(logs[:SEG])[:16], 3)
                for i, part in enumerate(parts):
                    tail = jnp.where(row == 1 + 3 * h + i, part, tail)
                parts = split(wide(logs[SEG : SEG + 1], 2), 3)
                for i, part in enumerate(parts):
                    tail = jnp.where(row == 7 + 3 * h + i, part, tail)
            tail = jnp.where(row == 0, jnp.concatenate(ends, axis=1), tail)
            payloads[j][SEG:, :] = tail.astype(BF16)


STATE = [shape((4, 2, ROWS, 2 * HD), F32), shape((4, 2, ROWS, HD), F32), shape((8, 128), F32)]


def attend_step(step, info, queries, own, others, state):
    first, final = own is not None, len(others) == 1
    ins = [info] + queries + ([own] if first else []) + others + list(state or [])
    flops = 4 * 1088 * SEG * (len(others) + (1 if first else 0)) * COLS
    body = functools.partial(attend_kernel, step, first, final)
    if final:
        outs = [shape((ROWS, COLS), BF16)] * 4 + STATE[:2]
        aliases = {len(ins) - 2: 4, len(ins) - 1: 5}

        def body(*refs):
            refs = list(refs)
            payloads, state = refs[-6:-2], refs[-2:]
            attend_kernel(step, first, final, *refs[:-8], *state, *payloads)

        return call(body, outs, ins, flops=flops, moved=4 << 20, aliases=aliases)[:4]
    aliases = {} if first else {len(ins) - 2: 0, len(ins) - 1: 1}
    return call(body, STATE, ins, flops=flops, moved=4 << 20, aliases=aliases)


def merge_kernel(info, a, b, c, d, out):
    parts = (a, b, c, d)
    tails = [p[SEG:, :].astype(F32) for p in parts]
    weights, end_weights = [], []
    for h in range(2):
        for base, store in ((1 + 3 * h, weights), (7 + 3 * h, end_weights)):
            logs = [t[base : base + 1] + t[base + 1 : base + 2] + t[base + 2 : base + 3] for t in tails]
            peak = functools.reduce(jnp.maximum, logs)
            expo = [jnp.exp2(v - peak) for v in logs]
            whole = functools.reduce(jnp.add, expo)
            store.append([e / whole for e in expo])
    flat = weights[0] + weights[1]
    columns = jnp.transpose(jnp.concatenate(flat + [jnp.zeros((120, SEG), F32)], axis=0))
    ends = []
    for h in range(2):
        lanes = slice(h * HD, (h + 1) * HD)
        acc = jnp.zeros((SEG, HD), F32)
        end = jnp.zeros((16, HD), F32)
        for j, p in enumerate(parts):
            acc = acc + columns[:, 4 * h + j : 4 * h + j + 1] * p[:SEG, lanes].astype(F32)
            end = end + end_weights[h][j][:, :HD] * tails[j][:, lanes]
        out[:SEG, lanes] = acc.astype(BF16)
        ends.append(end)
    end = jnp.concatenate(ends, axis=1)
    out[SEG:, :] = jnp.where(iota((16, COLS), 0) == 0, end, 0.0).astype(BF16)


BLOCK = 256
TALL = 384


def mark_kernel(ids, out):
    lane = iota((128, 128), 1)
    for r in range(TOK // 128):
        row = ids[r : r + 1, :].astype(F32)
        column = jnp.transpose(jnp.broadcast_to(row, (128, 128))).astype(jnp.int32)
        rows = slice(r * 128, (r + 1) * 128)
        out[rows, :128] = ones_where(column == lane)
        out[rows, 128:256] = ones_where(column == lane + 128)
        out[rows, 256:] = ones_where((column == -1) & (lane == 0))


def output_kernel(own, first, second, hot, tokens, out, coarse):
    @pl.when(pl.program_id(0) == 0)
    def _():
        total = own[...] + first[...].astype(F32) + second[...].astype(F32)
        coarse[:ROWS, :] = total.astype(BF16)
        coarse[ROWS:, :] = jnp.zeros((TALL - ROWS, FEAT), BF16)

    picked = dot(hot[...], coarse[...])
    out[...] = (tokens[...].astype(F32) + picked).astype(BF16)


def output(products, hot, tokens):
    return pl.pallas_call(
        output_kernel,
        grid=(TOK // BLOCK,),
        out_shape=shape((TOK, FEAT), BF16),
        in_specs=[WHOLE] * 3
        + [pl.BlockSpec((BLOCK, TALL), lambda i: (i, 0)), pl.BlockSpec((BLOCK, FEAT), lambda i: (i, 0))],
        out_specs=pl.BlockSpec((BLOCK, FEAT), lambda i: (i, 0)),
        scratch_shapes=[pltpu.VMEM((TALL, FEAT), BF16)],
        compiler_params=pltpu.CompilerParams(vmem_limit_bytes=VMEM_LIMIT),
        cost_estimate=pl.CostEstimate(flops=2 << 30, bytes_accessed=6 << 20, transcendentals=0),
    )(*products, hot, tokens)


def cut_kernel(info, w_out, _, sibling, sems):
    copies = []
    for i in range(4):
        start = pl.multiple_of(info[I_CUT + 4 + i] * FEAT, FEAT)
        copies.append(pltpu.make_async_copy(w_out.at[:, pl.ds(start, FEAT)], sibling.at[i], sems.at[i]))
        copies[-1].start()
    for copy in copies:
        copy.wait()


def product_kernel(info, attended, other, w_out, theirs, means, own_out, *outs):
    for i in range(4):
        start = pl.multiple_of(info[I_CUT + i] * FEAT, FEAT)
        part = dot(attended[...], w_out[:, pl.ds(start, FEAT)]) + dot(other[...], theirs[i])
        if i == 0:
            own_out[...] = part + means[...]
        else:
            outs[i - 1][...] = part.astype(outs[i - 1].dtype)


def add_kernel(a, b, out):
    out[...] = (a[...] + b[...].astype(F32)).astype(BF16)


def shards(tokens, flags, norm_gain, w_query, w_key, w_value, w_out):
    seq, mp = lax.axis_index("seq"), lax.axis_index("mp")
    info = jnp.asarray(device_table())[seq * (NY * NC) + mp]
    edge = shape((8, FEAT + 128), F32)
    ids, head, tail = call(
        edge_kernel,
        [shape((16, 128), jnp.int32), edge, edge],
        [flags.reshape(16, 128), tokens],
        scalars=None,
        flops=1 << 28,
        moved=2 << 20,
        scratch=[pltpu.VMEM((16, TOK), BF16)],
    )
    count = NZ * NX
    above = lax.ppermute(head, "seq", [(i, i - 1) for i in range(1, count)])
    below = lax.ppermute(tail, "seq", [(i, i + 1) for i in range(count - 1)])
    *weights, loaded = call(
        load_kernel,
        [shape((WIDTH, COLS), BF16)] * 3 + [shape((8, 128), F32)],
        [tail, w_query, w_key, w_value],
        scalars=None,
        moved=12 << 20,
        scratch=[pltpu.SemaphoreType.DMA((3, 4))],
        far_in=range(4),
        room=ROOM,
    )
    sums, sizes = call(
        pool_kernel,
        [shape((SEG, FEAT), F32), shape((SEG, 128), F32)],
        [ids, tokens],
        scalars=None,
        flops=1 << 30,
        moved=2 << 20,
        scratch=[pltpu.VMEM((SEG, TOK), BF16)],
    )
    means, u, bias = call(
        norm_kernel,
        [shape((ROWS, FEAT), F32), shape((ROWS, FEAT), BF16), shape((16, FEAT), BF16)],
        [info, sums, sizes, head, above, below, norm_gain.reshape(8, FEAT), loaded],
    )
    first, sibling, second = y_one(u), swap(u), y_other(u)
    across = swap(first)
    part, part_query = shape((SEG, COLS), F32), shape((ROWS, COLS), F32)
    queried, keyed, valued = call(
        early_kernel,
        [part_query, part, part],
        [info, u, first, second, sibling, *weights],
        flops=ROWS * WIDTH * 3 * COLS,
        moved=3 << 20,
    )
    far = y_one(first)
    blocks = [u, first, second, far, sibling, across, swap(second), swap(far)]
    (kv,) = call(
        key_value_kernel,
        [shape((ROWS, 2 * COLS), BF16)],
        [info] + blocks + [weights[1], weights[2], keyed, valued, bias],
    )
    (query,) = call(
        query_kernel,
        [shape((ROWS, COLS), BF16)],
        [info] + blocks + [weights[0], queried, kv],
        far_in=(11,),
    )
    queries = [query] + [x_by(query, k) for k in (1, 2, 3)]
    one, other = z_one(kv), z_other(kv)
    one2, other2 = z_one(one), z_other(other)
    *state, done = attend_step(1, info, queries, kv, [one, other], None)
    (theirs,) = call(
        cut_kernel,
        [shape((4, SEG, FEAT), BF16)],
        [info, w_out, done],
        scratch=[pltpu.SemaphoreType.DMA((4,))],
        far_in=(1, 2),
        far_out=(0,),
    )
    theirs = swap(theirs)
    one2, other2 = gate(info, [one2, other2], done)
    one3, other3 = z_one(one2), z_other(other2)
    *state, done = attend_step(2, info, queries, None, [one2, other2], state)
    one4 = z_one(one3)
    *state, done = attend_step(3, info, queries, None, [one3, other3], state)
    partial = attend_step(4, info, queries, None, [one4], state)
    partial = [partial[0]] + [x_by(partial[k], -k) for k in (1, 2, 3)]
    (attended,) = call(merge_kernel, [shape((ROWS, COLS), BF16)], [info] + partial, moved=1 << 20)
    block = shape((ROWS, FEAT), BF16)
    own, first, second, third = call(
        product_kernel,
        [shape((ROWS, FEAT), F32)] * 2 + [block] * 2,
        [info, attended, swap(attended), w_out, theirs, means],
        flops=2 * ROWS * 2 * COLS * 4 * FEAT,
        moved=4 << 20,
    )
    (hot,) = call(mark_kernel, [shape((TOK, TALL), BF16)], [ids], flops=1 << 29, moved=3 << 20, scalars=None)
    (first,) = call(add_kernel, [block], [first, y_one(third)], scalars=None)
    return output([own, y_one(first), y_other(second)], hot, tokens)


def solution(mesh):
    placed = (
        P(("dp", "seq"), "mp"),
        P(("dp", "seq")),
        P(),
        P(None, "mp"),
        P(None, "mp"),
        P(None, "mp"),
        P("mp", None),
    )
    return jax.shard_map(
        shards, mesh=mesh, in_specs=placed, out_specs=P(("dp", "seq"), "mp"), check_vma=False
    )
```

```python
import functools

import jax
import jax.numpy as jnp
import numpy as np
from jax import lax
from jax.experimental import pallas as pl
from jax.experimental.pallas import tpu as pltpu
from jax.sharding import PartitionSpec as P

HD = 128
NZ, NX, NY, NC = 8, 4, 4, 2
SEG = 256
ROWS = SEG + 16
TOK = 2048
FEAT = 512
COLS = 256
WIDTH = 4096
SCORE = 1.4426950408889634 * HD**-0.5
LOG2E = 1.4426950408889634
LOW = -1e30
VMEM_LIMIT = 20 * 1024 * 1024
ROOM = 47 * 1024 * 1024
F32, BF16 = jnp.float32, jnp.bfloat16


def number(z, x, y, c):
    return ((z % NZ) * NX + x % NX) * (NY * NC) + (y % NY) * NC + c % NC


def everywhere():
    return [(z, x, y, c) for z in range(NZ) for x in range(NX) for y in range(NY) for c in range(NC)]


def way(c):
    return 1 if c == 0 else -1


def move(value, target):
    pairs = [(number(*d), number(*target(*d))) for d in everywhere()]
    return lax.ppermute(value, ("seq", "mp"), pairs)


def swap(value):
    return move(value, lambda z, x, y, c: (z, x, y, 1 - c))


def y_one(value):
    return move(value, lambda z, x, y, c: (z, x, y + way(c), c))


def y_other(value):
    return move(value, lambda z, x, y, c: (z, x, y - way(c), c))


def z_one(value):
    return move(value, lambda z, x, y, c: (z + way(c), x, y, c))


def z_other(value):
    return move(value, lambda z, x, y, c: (z - way(c), x, y, c))


def x_by(value, by):
    return move(value, lambda z, x, y, c: (z, x + by, y, c))


def sources(y, c):
    own = [(y, c), (y - way(c), c), (y + way(c), c), (y + 2, c)]
    o = 1 - c
    other = [(y, o), (y - way(o), o), (y + way(o), o), (y + 2, o)]
    return [((b[0] % NY) * NC + b[1]) for b in own + other]


def mp_exchange(value):
    first = y_one(value)
    second = y_other(value)
    sibling = swap(value)
    far = y_one(first)
    return [value, first, second, far, sibling, swap(first), swap(second), swap(far)]


def device_table():
    rows = []
    for z, x, y, c in everywhere():
        row = [y * NC + c] + sources(y, c)
        row += [x] + [(x - k) % NX for k in (1, 2, 3)]
        for k in (1, 2, 3, 4):
            row += [int((z - way(c) * k) % NZ < z), int((z + way(c) * k) % NZ < z)]
        for o in (c, 1 - c):
            row += [(v % NY) * NC + o for v in (y, y + way(o), y - way(o), y + 2)]
        row += [0] * (32 - len(row))
        rows.append(row)
    return np.asarray(rows, np.int32)


I_MP, I_SRC, I_X, I_OK, I_CUT = 0, 1, 9, 13, 21
SMEM = pl.BlockSpec(memory_space=pltpu.SMEM)
WHOLE = pl.BlockSpec(memory_space=pltpu.VMEM)
FAR = pl.BlockSpec(memory_space=pl.ANY)
DISTANT = pl.BlockSpec(memory_space=pltpu.HBM)


def call(body, outs, ins, flops=0, moved=0, scratch=(), aliases=None, far_in=(), far_out=(), far=FAR, scalars=0, room=VMEM_LIMIT):
    return pl.pallas_call(
        body,
        out_shape=outs,
        in_specs=[SMEM if i == scalars else far if i in far_in else WHOLE for i in range(len(ins))],
        out_specs=[far if i in far_out else WHOLE for i in range(len(outs))],
        scratch_shapes=list(scratch),
        input_output_aliases=aliases or {},
        compiler_params=pltpu.CompilerParams(vmem_limit_bytes=room),
        cost_estimate=pl.CostEstimate(flops=flops, bytes_accessed=moved, transcendentals=0),
    )(*ins)


def gate_kernel(info, *refs):
    pass


def gate(info, values, token):
    ins = [info] + list(values) + [token]
    count = len(values)
    return call(
        gate_kernel,
        [shape(v.shape, v.dtype) for v in values],
        ins,
        aliases={i + 1: i for i in range(count)},
        far_in=range(1, count + 2),
        far_out=range(count),
    )


def shape(dims, dtype):
    return jax.ShapeDtypeStruct(dims, dtype)


def dot(a, b):
    return jnp.dot(a, b, preferred_element_type=F32)


def iota(dims, axis):
    return lax.broadcasted_iota(jnp.int32, dims, axis)


def ones_where(condition):
    return jnp.where(condition, 1.0, 0.0).astype(BF16)


def edge_kernel(flags, tokens, ids_out, head_out, tail_out, marks):
    f = flags[...].astype(F32).astype(BF16)
    upto = ones_where(iota((128, 128), 0) <= iota((128, 128), 1))
    inside = dot(f, upto)
    rows = dot(f, jnp.ones((128, 128), BF16)).astype(BF16)
    before = dot(ones_where(iota((16, 16), 1) < iota((16, 16), 0)), rows)
    ids_out[...] = (inside + before - 1.0).astype(jnp.int32)
    wanted = jnp.where(iota((16, 128), 0) < 8, -1, SEG - 1)
    for r in range(16):
        marks[:, r * 128 : (r + 1) * 128] = ones_where(ids_out[r : r + 1, :] == wanted)
    sums = dot(marks[...], tokens[...])
    counts = dot(marks[...], jnp.ones((TOK, 128), BF16))
    head_out[:, :FEAT] = sums[:8]
    head_out[:, FEAT:] = counts[:8]
    tail_out[:, :FEAT] = sums[8:]
    tail_out[:, FEAT:] = counts[8:]


def pool_kernel(ids, tokens, sums_out, counts_out, hot):
    segment = iota((SEG, 128), 0)
    for r in range(16):
        hot[:, r * 128 : (r + 1) * 128] = ones_where(ids[r : r + 1, :] == segment)
    sums_out[...] = dot(hot[...], tokens[...])
    counts_out[...] = dot(hot[...], jnp.ones((TOK, 128), BF16))


def wide(column, times):
    return jnp.concatenate([column] * times, axis=1)


def split(value, parts):
    out = []
    for _ in range(parts):
        high = value.astype(BF16).astype(F32)
        out.append(high)
        value = value - high
    return out


def norm_kernel(info, sums, counts, head, above, below, gain, _, means_out, u_out, bias_out):
    g = gain[pl.ds(info[I_MP], 1), :]
    last = iota((SEG, 128), 0) == SEG - 1
    size = counts[...] + jnp.where(last, above[0:1, FEAT:], 0.0)
    total = sums[...] + jnp.where(iota((SEG, FEAT), 0) == SEG - 1, above[0:1, :FEAT], 0.0)
    size = jnp.maximum(size, 1.0)
    means = total / wide(size, 4)
    means_out[:SEG, :] = means
    u_out[:SEG, :] = (means * g).astype(BF16)
    squares = jnp.sum(means * means, axis=1, keepdims=True)
    squares = jnp.transpose(jnp.broadcast_to(squares, (SEG, 128)))[:16]
    high, low = split(squares, 2)
    extra_size = jnp.maximum(head[0:1, FEAT:] + below[0:1, FEAT:], 1.0)
    extra = (head[0:1, :FEAT] + below[0:1, :FEAT]) / wide(extra_size, 4)
    extra_squares = jnp.broadcast_to(jnp.sum(extra * extra, axis=1, keepdims=True), (16, SEG))
    extra_high, extra_low = split(extra_squares, 2)
    row = iota((16, FEAT), 0)
    means_out[SEG:, :] = jnp.where(row == 0, extra, 0.0)
    tail = jnp.where(row == 0, extra * g, 0.0)
    tail = jnp.where(row == 1, jnp.concatenate([high, low], axis=1), tail)
    tail = jnp.where(row == 2, jnp.concatenate([extra_high, extra_low], axis=1), tail)
    u_out[SEG:, :] = tail.astype(BF16)
    bias = jnp.log(jnp.transpose(size)[:16])
    bias_out[...] = jnp.concatenate([bias, bias], axis=1).astype(BF16)


EARLY = (0, 1, 2, 4)
LATE = (3, 5, 6, 7)


def row_scale(tail):
    squares = tail[:, :SEG] + tail[:, SEG:]
    scale = lax.rsqrt(squares / WIDTH + 1e-05)
    column = jnp.transpose(jnp.broadcast_to(scale[1:2, :], (128, SEG)))
    return scale, wide(column, 2)


def load_kernel(_, *refs):
    sources, outs, done, sems = refs[:3], refs[3:6], refs[6], refs[7]
    copies = []
    for n in range(3):
        for i in range(4):
            rows = pl.ds(i * (WIDTH // 4), WIDTH // 4)
            copies.append(pltpu.make_async_copy(sources[n].at[rows, :], outs[n].at[rows, :], sems.at[n, i]))
            copies[-1].start()
    done[...] = jnp.zeros_like(done)
    for copy in copies:
        copy.wait()


def product(info, acc, blocks, which, weight, rows):
    for i, u in zip(which, blocks):
        start = pl.multiple_of(info[I_SRC + i] * FEAT, FEAT)
        part = dot(u[:rows, :], weight[pl.ds(start, FEAT), :])
        acc = part if acc is None else acc + part
    return acc


def early_kernel(info, *refs):
    blocks, weights, sums = refs[:4], refs[4:7], refs[7:]
    for n, rows in enumerate((ROWS, SEG, SEG)):
        sums[n][...] = product(info, None, blocks, EARLY, weights[n], rows)


def square_rows(blocks):
    tail = jnp.zeros((16, FEAT), F32)
    for u in blocks:
        tail = tail + u[SEG:, :].astype(F32)
    return tail


def key_value_kernel(info, *refs):
    blocks, late = refs[:8], [refs[i] for i in LATE]
    w_key, w_value, keys, values, bias, kv_out = refs[8:]
    _, column = row_scale(square_rows(blocks))
    kv_out[:SEG, :COLS] = (product(info, keys[...], late, LATE, w_key, SEG) * column).astype(BF16)
    kv_out[:SEG, COLS:] = (product(info, values[...], late, LATE, w_value, SEG) * column).astype(BF16)
    kv_out[SEG:, :] = bias[...]


def query_kernel(info, *refs):
    blocks, late = refs[:8], [refs[i] for i in LATE]
    w_query, partial, _, q_out = refs[8:]
    scale, column = row_scale(square_rows(blocks))
    query = product(info, partial[...], late, LATE, w_query, ROWS)
    q_out[:SEG, :] = (query[:SEG] * column * SCORE).astype(BF16)
    extra = query[SEG:] * scale[2:3, :] * SCORE
    q_out[SEG:, :] = jnp.where(iota((16, COLS), 0) == 0, extra, 0.0).astype(BF16)


def nt_dot(a, b):
    return lax.dot_general(a, b, (((1,), (1,)), ((), ())), preferred_element_type=F32)


def attend(q, k, v, bias, acc_ref, m_ref, j, h, mask=None):
    scores = nt_dot(q[:, h * HD : (h + 1) * HD], k) + bias
    if mask is not None:
        scores = jnp.where(mask, scores, LOW)
    old = m_ref[j, h]
    peak = jnp.maximum(old, jnp.max(scores, axis=1, keepdims=True))
    expo = jnp.exp2(scores - wide(peak, scores.shape[1] // 128))
    if mask is not None:
        expo = jnp.where(mask, expo, 0.0)
    m_ref[j, h] = peak
    acc_ref[j, h] = acc_ref[j, h] * wide(jnp.exp2(old - peak), 2) + dot(expo.astype(BF16), v)


def keys_of(blocks, h):
    return jnp.concatenate([kv[:SEG, h * HD : (h + 1) * HD] for kv in blocks], axis=0)


def values_of(blocks, h):
    lanes = slice(COLS + h * HD, COLS + (h + 1) * HD)
    values = jnp.concatenate([kv[:SEG, lanes] for kv in blocks], axis=0)
    return jnp.concatenate([values, jnp.ones(values.shape, BF16)], axis=1)


def attend_kernel(step, has_own, info, *refs):
    first, final = step == 1, step == 4
    refs = list(refs)
    queries = [refs.pop(0) for _ in range(4)]
    own = refs.pop(0) if has_own else None
    others = [refs.pop(0) for _ in range(1 if final else 2)]
    if not first:
        state_in = [refs.pop(0) for _ in range(2)]
    if final:
        payloads = [refs.pop(0) for _ in range(4)]
        acc, m = state_in
    else:
        acc, m, done = refs[:3]
        done[...] = jnp.zeros_like(done)
    if first:
        acc[...] = jnp.zeros_like(acc)
        m[...] = jnp.full(m.shape, LOW, F32)
    if has_own:
        bias = own[SEG : SEG + 1, :SEG].astype(F32) * LOG2E
        for j in range(4):

            def one(j=j):
                mask = None
                if j == 0:
                    r, k = iota((ROWS, SEG), 0), iota((ROWS, SEG), 1)
                    mask = (k <= r) & (r < SEG)
                for h in range(2):
                    attend(queries[j], keys_of([own], h), values_of([own], h), bias, acc, m, j, h, mask)

            if j == 0:
                one()
            else:
                pl.when(info[I_X] < info[I_X + j])(one)
    ok = [info[I_OK + 2 * (step - 1) + i] for i in range(len(others))]
    some = ok[0] if final else ok[0] + ok[1]

    @pl.when(some > 0)
    def _():
        biases = []
        for kv, good in zip(others, ok):
            row = kv[SEG : SEG + 1, :SEG].astype(F32) * LOG2E
            biases.append(jnp.where(good > 0, row, LOW))
        bias = jnp.concatenate(biases, axis=1)
        for h in range(2):
            k, v = keys_of(others, h), values_of(others, h)
            for j in range(4):
                attend(queries[j], k, v, bias, acc, m, j, h)

    if final:
        row = iota((16, COLS), 0)
        for j in range(4):
            tail = jnp.zeros((16, COLS), F32)
            ends = []
            for h in range(2):
                total = acc[j, h][:, HD:]
                some_keys = total > 0.0
                total = jnp.where(some_keys, total, 1.0)
                out = acc[j, h][:, :HD] / total
                logs = jnp.where(some_keys, m[j, h] + jnp.log2(total), LOW)
                payloads[j][:SEG, h * HD : (h + 1) * HD] = out[:SEG].astype(BF16)
                ends.append(out[SEG:])
                parts = split(jnp.transpose(logs[:SEG])[:16], 3)
                for i, part in enumerate(parts):
                    tail = jnp.where(row == 1 + 3 * h + i, part, tail)
                parts = split(wide(logs[SEG : SEG + 1], 2), 3)
                for i, part in enumerate(parts):
                    tail = jnp.where(row == 7 + 3 * h + i, part, tail)
            tail = jnp.where(row == 0, jnp.concatenate(ends, axis=1), tail)
            payloads[j][SEG:, :] = tail.astype(BF16)


STATE = [shape((4, 2, ROWS, 2 * HD), F32), shape((4, 2, ROWS, HD), F32), shape((8, 128), F32)]


def attend_step(step, info, queries, own, others, state):
    first, final, has_own = step == 1, step == 4, own is not None
    ins = [info] + queries + ([own] if has_own else []) + others + list(state or [])
    flops = 4 * 1088 * SEG * (len(others) + 1) * COLS
    body = functools.partial(attend_kernel, step, has_own)
    if final:
        outs = [shape((ROWS, COLS), BF16)] * 4 + STATE[:2]
        aliases = {len(ins) - 2: 4, len(ins) - 1: 5}

        def body(*refs):
            refs = list(refs)
            payloads, state = refs[-6:-2], refs[-2:]
            attend_kernel(step, has_own, *refs[:-8], *state, *payloads)

        return call(body, outs, ins, flops=flops, moved=4 << 20, aliases=aliases)[:4]
    aliases = {} if first else {len(ins) - 2: 0, len(ins) - 1: 1}
    return call(body, STATE, ins, flops=flops, moved=4 << 20, aliases=aliases)


def merge_kernel(info, a, b, c, d, out):
    parts = (a, b, c, d)
    tails = [p[SEG:, :].astype(F32) for p in parts]
    weights, end_weights = [], []
    for h in range(2):
        for base, store in ((1 + 3 * h, weights), (7 + 3 * h, end_weights)):
            logs = [t[base : base + 1] + t[base + 1 : base + 2] + t[base + 2 : base + 3] for t in tails]
            peak = functools.reduce(jnp.maximum, logs)
            expo = [jnp.exp2(v - peak) for v in logs]
            whole = functools.reduce(jnp.add, expo)
            store.append([e / whole for e in expo])
    flat = weights[0] + weights[1]
    columns = jnp.transpose(jnp.concatenate(flat + [jnp.zeros((120, SEG), F32)], axis=0))
    ends = []
    for h in range(2):
        lanes = slice(h * HD, (h + 1) * HD)
        acc = jnp.zeros((SEG, HD), F32)
        end = jnp.zeros((16, HD), F32)
        for j, p in enumerate(parts):
            acc = acc + columns[:, 4 * h + j : 4 * h + j + 1] * p[:SEG, lanes].astype(F32)
            end = end + end_weights[h][j][:, :HD] * tails[j][:, lanes]
        out[:SEG, lanes] = acc.astype(BF16)
        ends.append(end)
    end = jnp.concatenate(ends, axis=1)
    out[SEG:, :] = jnp.where(iota((16, COLS), 0) == 0, end, 0.0).astype(BF16)


BLOCK = 512
TALL = 384


def mark_kernel(ids, out):
    lane = iota((128, 128), 1)
    for r in range(TOK // 128):
        row = ids[r : r + 1, :].astype(F32)
        column = jnp.transpose(jnp.broadcast_to(row, (128, 128))).astype(jnp.int32)
        rows = slice(r * 128, (r + 1) * 128)
        out[rows, :128] = ones_where(column == lane)
        out[rows, 128:256] = ones_where(column == lane + 128)
        out[rows, 256:] = ones_where((column == -1) & (lane == 0))


def output_kernel(own, first, second, hot, tokens, out, coarse):
    @pl.when(pl.program_id(0) == 0)
    def _():
        total = own[...] + first[...].astype(F32) + second[...].astype(F32)
        coarse[:ROWS, :] = total.astype(BF16)
        coarse[ROWS:, :] = jnp.zeros((TALL - ROWS, FEAT), BF16)

    picked = dot(hot[...], coarse[...])
    out[...] = (tokens[...].astype(F32) + picked).astype(BF16)


def output(products, hot, tokens):
    return pl.pallas_call(
        output_kernel,
        grid=(TOK // BLOCK,),
        out_shape=shape((TOK, FEAT), BF16),
        in_specs=[WHOLE] * 3
        + [pl.BlockSpec((BLOCK, TALL), lambda i: (i, 0)), pl.BlockSpec((BLOCK, FEAT), lambda i: (i, 0))],
        out_specs=pl.BlockSpec((BLOCK, FEAT), lambda i: (i, 0)),
        scratch_shapes=[pltpu.VMEM((TALL, FEAT), BF16)],
        compiler_params=pltpu.CompilerParams(vmem_limit_bytes=VMEM_LIMIT),
        cost_estimate=pl.CostEstimate(flops=2 << 30, bytes_accessed=6 << 20, transcendentals=0),
    )(*products, hot, tokens)


def cut_kernel(info, w_out, _, sibling, sems):
    copies = []
    for i in range(4):
        start = pl.multiple_of(info[I_CUT + 4 + i] * FEAT, FEAT)
        copies.append(pltpu.make_async_copy(w_out.at[:, pl.ds(start, FEAT)], sibling.at[i], sems.at[i]))
        copies[-1].start()
    for copy in copies:
        copy.wait()


def product_kernel(info, attended, other, w_out, theirs, means, own_out, *outs):
    for i in range(4):
        start = pl.multiple_of(info[I_CUT + i] * FEAT, FEAT)
        part = dot(attended[...], w_out[:, pl.ds(start, FEAT)]) + dot(other[...], theirs[i])
        if i == 0:
            own_out[...] = part + means[...]
        else:
            outs[i - 1][...] = part.astype(outs[i - 1].dtype)


def add_kernel(a, b, out):
    out[...] = (a[...] + b[...].astype(F32)).astype(BF16)


def shards(tokens, flags, norm_gain, w_query, w_key, w_value, w_out):
    seq, mp = lax.axis_index("seq"), lax.axis_index("mp")
    info = jnp.asarray(device_table())[seq * (NY * NC) + mp]
    edge = shape((8, FEAT + 128), F32)
    ids, head, tail = call(
        edge_kernel,
        [shape((16, 128), jnp.int32), edge, edge],
        [flags.reshape(16, 128), tokens],
        scalars=None,
        flops=1 << 28,
        moved=2 << 20,
        scratch=[pltpu.VMEM((16, TOK), BF16)],
    )
    count = NZ * NX
    above = lax.ppermute(head, "seq", [(i, i - 1) for i in range(1, count)])
    below = lax.ppermute(tail, "seq", [(i, i + 1) for i in range(count - 1)])
    *weights, loaded = call(
        load_kernel,
        [shape((WIDTH, COLS), BF16)] * 3 + [shape((8, 128), F32)],
        [tail, w_query, w_key, w_value],
        scalars=None,
        moved=12 << 20,
        scratch=[pltpu.SemaphoreType.DMA((3, 4))],
        far_in=range(4),
        room=ROOM,
    )
    sums, sizes = call(
        pool_kernel,
        [shape((SEG, FEAT), F32), shape((SEG, 128), F32)],
        [ids, tokens],
        scalars=None,
        flops=1 << 30,
        moved=2 << 20,
        scratch=[pltpu.VMEM((SEG, TOK), BF16)],
    )
    means, u, bias = call(
        norm_kernel,
        [shape((ROWS, FEAT), F32), shape((ROWS, FEAT), BF16), shape((16, FEAT), BF16)],
        [info, sums, sizes, head, above, below, norm_gain.reshape(8, FEAT), loaded],
    )
    first, sibling, second = y_one(u), swap(u), y_other(u)
    across = swap(first)
    part, part_query = shape((SEG, COLS), F32), shape((ROWS, COLS), F32)
    queried, keyed, valued = call(
        early_kernel,
        [part_query, part, part],
        [info, u, first, second, sibling, *weights],
        flops=ROWS * WIDTH * 3 * COLS,
        moved=3 << 20,
    )
    far = y_one(first)
    blocks = [u, first, second, far, sibling, across, swap(second), swap(far)]
    (kv,) = call(
        key_value_kernel,
        [shape((ROWS, 2 * COLS), BF16)],
        [info] + blocks + [weights[1], weights[2], keyed, valued, bias],
    )
    (query,) = call(
        query_kernel,
        [shape((ROWS, COLS), BF16)],
        [info] + blocks + [weights[0], queried, kv],
        far_in=(11,),
    )
    queries = [query] + [x_by(query, k) for k in (1, 2, 3)]
    one, other = z_one(kv), z_other(kv)
    one2, other2 = z_one(one), z_other(other)
    *state, done = attend_step(1, info, queries, None, [one, other], None)
    (theirs,) = call(
        cut_kernel,
        [shape((4, SEG, FEAT), BF16)],
        [info, w_out, done],
        scratch=[pltpu.SemaphoreType.DMA((4,))],
        far_in=(1, 2),
        far_out=(0,),
    )
    theirs = swap(theirs)
    one2, other2 = gate(info, [one2, other2], done)
    one3, other3 = z_one(one2), z_other(other2)
    *state, done = attend_step(2, info, queries, kv, [one2, other2], state)
    (one3_sent,) = gate(info, [one3], done)
    one4 = z_one(one3_sent)
    *state, done = attend_step(3, info, queries, None, [one3_sent, other3], state)
    partial = attend_step(4, info, queries, None, [one4], state)
    partial = [partial[0]] + [x_by(partial[k], -k) for k in (1, 2, 3)]
    (attended,) = call(merge_kernel, [shape((ROWS, COLS), BF16)], [info] + partial, moved=1 << 20)
    block = shape((ROWS, FEAT), BF16)
    own, first, second, third = call(
        product_kernel,
        [shape((ROWS, FEAT), F32)] * 2 + [block] * 2,
        [info, attended, swap(attended), w_out, theirs, means],
        flops=2 * ROWS * 2 * COLS * 4 * FEAT,
        moved=4 << 20,
    )
    (hot,) = call(mark_kernel, [shape((TOK, TALL), BF16)], [ids], flops=1 << 29, moved=3 << 20, scalars=None)
    (first,) = call(add_kernel, [block], [first, y_one(third)], scalars=None)
    return output([own, y_one(first), y_other(second)], hot, tokens)


def solution(mesh):
    placed = (
        P(("dp", "seq"), "mp"),
        P(("dp", "seq")),
        P(),
        P(None, "mp"),
        P(None, "mp"),
        P(None, "mp"),
        P("mp", None),
    )
    return jax.shard_map(
        shards, mesh=mesh, in_specs=placed, out_specs=P(("dp", "seq"), "mp"), check_vma=False
    )
```

```python
import functools

import jax
import jax.numpy as jnp
import numpy as np
from jax import lax
from jax.experimental import pallas as pl
from jax.experimental.pallas import tpu as pltpu
from jax.sharding import PartitionSpec as P

HD = 128
NZ, NX, NY, NC = 8, 4, 4, 2
SEG = 256
ROWS = SEG + 16
TOK = 2048
FEAT = 512
COLS = 256
WIDTH = 4096
SCORE = 1.4426950408889634 * HD**-0.5
LOG2E = 1.4426950408889634
LOW = -1e30
VMEM_LIMIT = 20 * 1024 * 1024
ROOM = 47 * 1024 * 1024
EDGE_ROOM = 51 * 1024 * 1024
PIECES = 8
F32, BF16 = jnp.float32, jnp.bfloat16


def number(z, x, y, c):
    return ((z % NZ) * NX + x % NX) * (NY * NC) + (y % NY) * NC + c % NC


def everywhere():
    return [(z, x, y, c) for z in range(NZ) for x in range(NX) for y in range(NY) for c in range(NC)]


def way(c):
    return 1 if c == 0 else -1


def move(value, target):
    pairs = [(number(*d), number(*target(*d))) for d in everywhere()]
    return lax.ppermute(value, ("seq", "mp"), pairs)


def swap(value):
    return move(value, lambda z, x, y, c: (z, x, y, 1 - c))


def y_one(value):
    return move(value, lambda z, x, y, c: (z, x, y + way(c), c))


def y_other(value):
    return move(value, lambda z, x, y, c: (z, x, y - way(c), c))


def z_one(value):
    return move(value, lambda z, x, y, c: (z + way(c), x, y, c))


def z_other(value):
    return move(value, lambda z, x, y, c: (z - way(c), x, y, c))


def x_by(value, by):
    return move(value, lambda z, x, y, c: (z, x + by, y, c))


def sources(y, c):
    own = [(y, c), (y - way(c), c), (y + way(c), c), (y + 2, c)]
    o = 1 - c
    other = [(y, o), (y - way(o), o), (y + way(o), o), (y + 2, o)]
    return [((b[0] % NY) * NC + b[1]) for b in own + other]


def mp_exchange(value):
    first = y_one(value)
    second = y_other(value)
    sibling = swap(value)
    far = y_one(first)
    return [value, first, second, far, sibling, swap(first), swap(second), swap(far)]


def device_table():
    rows = []
    for z, x, y, c in everywhere():
        row = [y * NC + c] + sources(y, c)
        row += [x] + [(x - k) % NX for k in (1, 2, 3)]
        for k in (1, 2, 3, 4):
            row += [int((z - way(c) * k) % NZ < z), int((z + way(c) * k) % NZ < z)]
        for o in (c, 1 - c):
            row += [(v % NY) * NC + o for v in (y, y + way(o), y - way(o), y + 2)]
        row += [0] * (32 - len(row))
        rows.append(row)
    return np.asarray(rows, np.int32)


I_MP, I_SRC, I_X, I_OK, I_CUT = 0, 1, 9, 13, 21
SMEM = pl.BlockSpec(memory_space=pltpu.SMEM)
WHOLE = pl.BlockSpec(memory_space=pltpu.VMEM)
FAR = pl.BlockSpec(memory_space=pl.ANY)
DISTANT = pl.BlockSpec(memory_space=pltpu.HBM)


def call(body, outs, ins, flops=0, moved=0, scratch=(), aliases=None, far_in=(), far_out=(), far=FAR, scalars=0, room=VMEM_LIMIT):
    return pl.pallas_call(
        body,
        out_shape=outs,
        in_specs=[SMEM if i == scalars else far if i in far_in else WHOLE for i in range(len(ins))],
        out_specs=[far if i in far_out else WHOLE for i in range(len(outs))],
        scratch_shapes=list(scratch),
        input_output_aliases=aliases or {},
        compiler_params=pltpu.CompilerParams(vmem_limit_bytes=room),
        cost_estimate=pl.CostEstimate(flops=flops, bytes_accessed=moved, transcendentals=0),
    )(*ins)


def gate_kernel(info, *refs):
    pass


def gate(info, values, token):
    ins = [info] + list(values) + [token]
    count = len(values)
    return call(
        gate_kernel,
        [shape(v.shape, v.dtype) for v in values],
        ins,
        aliases={i + 1: i for i in range(count)},
        far_in=range(1, count + 2),
        far_out=range(count),
    )


def shape(dims, dtype):
    return jax.ShapeDtypeStruct(dims, dtype)


def dot(a, b):
    return jnp.dot(a, b, preferred_element_type=F32)


def iota(dims, axis):
    return lax.broadcasted_iota(jnp.int32, dims, axis)


def ones_where(condition):
    return jnp.where(condition, 1.0, 0.0).astype(BF16)


def edge_kernel(flags_in, tokens_in, tokens, ids_out, head_out, tail_out, marks, flags, sems):
    copies = [pltpu.make_async_copy(flags_in, flags, sems.at[PIECES])]
    for i in range(PIECES):
        rows = pl.ds(i * (TOK // PIECES), TOK // PIECES)
        copies.append(pltpu.make_async_copy(tokens_in.at[rows, :], tokens.at[rows, :], sems.at[i]))
    for copy in copies:
        copy.start()
    copies[0].wait()
    f = flags[...].astype(F32).astype(BF16)
    upto = ones_where(iota((128, 128), 0) <= iota((128, 128), 1))
    inside = dot(f, upto)
    rows = dot(f, jnp.ones((128, 128), BF16)).astype(BF16)
    before = dot(ones_where(iota((16, 16), 1) < iota((16, 16), 0)), rows)
    ids_out[...] = (inside + before - 1.0).astype(jnp.int32)
    wanted = jnp.where(iota((16, 128), 0) < 8, -1, SEG - 1)
    for r in range(16):
        marks[:, r * 128 : (r + 1) * 128] = ones_where(ids_out[r : r + 1, :] == wanted)
    for copy in copies[1:]:
        copy.wait()
    sums = dot(marks[...], tokens[...])
    counts = dot(marks[...], jnp.ones((TOK, 128), BF16))
    head_out[:, :FEAT] = sums[:8]
    head_out[:, FEAT:] = counts[:8]
    tail_out[:, :FEAT] = sums[8:]
    tail_out[:, FEAT:] = counts[8:]


def pool_kernel(ids, tokens, sums_out, counts_out, hot):
    segment = iota((SEG, 128), 0)
    for r in range(16):
        hot[:, r * 128 : (r + 1) * 128] = ones_where(ids[r : r + 1, :] == segment)
    sums_out[...] = dot(hot[...], tokens[...])
    counts_out[...] = dot(hot[...], jnp.ones((TOK, 128), BF16))


def wide(column, times):
    return jnp.concatenate([column] * times, axis=1)


def split(value, parts):
    out = []
    for _ in range(parts):
        high = value.astype(BF16).astype(F32)
        out.append(high)
        value = value - high
    return out


def norm_kernel(info, sums, counts, head, above, below, gain, _, means_out, u_out, bias_out):
    g = gain[pl.ds(info[I_MP], 1), :]
    last = iota((SEG, 128), 0) == SEG - 1
    size = counts[...] + jnp.where(last, above[0:1, FEAT:], 0.0)
    total = sums[...] + jnp.where(iota((SEG, FEAT), 0) == SEG - 1, above[0:1, :FEAT], 0.0)
    size = jnp.maximum(size, 1.0)
    means = total / wide(size, 4)
    means_out[:SEG, :] = means
    u_out[:SEG, :] = (means * g).astype(BF16)
    squares = jnp.sum(means * means, axis=1, keepdims=True)
    squares = jnp.transpose(jnp.broadcast_to(squares, (SEG, 128)))[:16]
    high, low = split(squares, 2)
    extra_size = jnp.maximum(head[0:1, FEAT:] + below[0:1, FEAT:], 1.0)
    extra = (head[0:1, :FEAT] + below[0:1, :FEAT]) / wide(extra_size, 4)
    extra_squares = jnp.broadcast_to(jnp.sum(extra * extra, axis=1, keepdims=True), (16, SEG))
    extra_high, extra_low = split(extra_squares, 2)
    row = iota((16, FEAT), 0)
    means_out[SEG:, :] = jnp.where(row == 0, extra, 0.0)
    tail = jnp.where(row == 0, extra * g, 0.0)
    tail = jnp.where(row == 1, jnp.concatenate([high, low], axis=1), tail)
    tail = jnp.where(row == 2, jnp.concatenate([extra_high, extra_low], axis=1), tail)
    u_out[SEG:, :] = tail.astype(BF16)
    bias = jnp.log(jnp.transpose(size)[:16])
    bias_out[...] = jnp.concatenate([bias, bias], axis=1).astype(BF16)


EARLY = (0, 1, 2, 4)
LATE = (3, 5, 6, 7)


def row_scale(tail):
    squares = tail[:, :SEG] + tail[:, SEG:]
    scale = lax.rsqrt(squares / WIDTH + 1e-05)
    column = jnp.transpose(jnp.broadcast_to(scale[1:2, :], (128, SEG)))
    return scale, wide(column, 2)


def load_kernel(_, *refs):
    sources, outs, done, sems = refs[:3], refs[3:6], refs[6], refs[7]
    copies = []
    for n in range(3):
        for i in range(4):
            rows = pl.ds(i * (WIDTH // 4), WIDTH // 4)
            copies.append(pltpu.make_async_copy(sources[n].at[rows, :], outs[n].at[rows, :], sems.at[n, i]))
            copies[-1].start()
    done[...] = jnp.zeros_like(done)
    for copy in copies:
        copy.wait()


def product(info, acc, blocks, which, weight, rows):
    for i, u in zip(which, blocks):
        start = pl.multiple_of(info[I_SRC + i] * FEAT, FEAT)
        part = dot(u[:rows, :], weight[pl.ds(start, FEAT), :])
        acc = part if acc is None else acc + part
    return acc


def early_kernel(info, *refs):
    blocks, weights, sums = refs[:4], refs[4:7], refs[7:]
    for n, rows in enumerate((ROWS, SEG, SEG)):
        sums[n][...] = product(info, None, blocks, EARLY, weights[n], rows)


def square_rows(blocks):
    tail = jnp.zeros((16, FEAT), F32)
    for u in blocks:
        tail = tail + u[SEG:, :].astype(F32)
    return tail


def key_value_kernel(info, *refs):
    blocks, late = refs[:8], [refs[i] for i in LATE]
    w_key, w_value, keys, values, bias, kv_out = refs[8:]
    _, column = row_scale(square_rows(blocks))
    kv_out[:SEG, :COLS] = (product(info, keys[...], late, LATE, w_key, SEG) * column).astype(BF16)
    kv_out[:SEG, COLS:] = (product(info, values[...], late, LATE, w_value, SEG) * column).astype(BF16)
    kv_out[SEG:, :] = bias[...]


def query_kernel(info, *refs):
    blocks, late = refs[:8], [refs[i] for i in LATE]
    w_query, partial, _, q_out = refs[8:]
    scale, column = row_scale(square_rows(blocks))
    query = product(info, partial[...], late, LATE, w_query, ROWS)
    q_out[:SEG, :] = (query[:SEG] * column * SCORE).astype(BF16)
    extra = query[SEG:] * scale[2:3, :] * SCORE
    q_out[SEG:, :] = jnp.where(iota((16, COLS), 0) == 0, extra, 0.0).astype(BF16)


def nt_dot(a, b):
    return lax.dot_general(a, b, (((1,), (1,)), ((), ())), preferred_element_type=F32)


def attend(q, k, v, bias, acc_ref, m_ref, j, h, mask=None):
    scores = nt_dot(q[:, h * HD : (h + 1) * HD], k) + bias
    if mask is not None:
        scores = jnp.where(mask, scores, LOW)
    old = m_ref[j, h]
    peak = jnp.maximum(old, jnp.max(scores, axis=1, keepdims=True))
    expo = jnp.exp2(scores - wide(peak, scores.shape[1] // 128))
    if mask is not None:
        expo = jnp.where(mask, expo, 0.0)
    m_ref[j, h] = peak
    acc_ref[j, h] = acc_ref[j, h] * wide(jnp.exp2(old - peak), 2) + dot(expo.astype(BF16), v)


def keys_of(blocks, h):
    return jnp.concatenate([kv[:SEG, h * HD : (h + 1) * HD] for kv in blocks], axis=0)


def values_of(blocks, h):
    lanes = slice(COLS + h * HD, COLS + (h + 1) * HD)
    values = jnp.concatenate([kv[:SEG, lanes] for kv in blocks], axis=0)
    return jnp.concatenate([values, jnp.ones(values.shape, BF16)], axis=1)


def attend_kernel(step, has_own, info, *refs):
    first, final = step == 1, step == 4
    refs = list(refs)
    queries = [refs.pop(0) for _ in range(4)]
    own = refs.pop(0) if has_own else None
    others = [refs.pop(0) for _ in range(1 if final else 2)]
    if not first:
        state_in = [refs.pop(0) for _ in range(2)]
    if final:
        payloads = [refs.pop(0) for _ in range(4)]
        acc, m = state_in
    else:
        acc, m, done = refs[:3]
        done[...] = jnp.zeros_like(done)
    if first:
        acc[...] = jnp.zeros_like(acc)
        m[...] = jnp.full(m.shape, LOW, F32)
    if has_own:
        bias = own[SEG : SEG + 1, :SEG].astype(F32) * LOG2E
        for j in range(4):

            def one(j=j):
                mask = None
                if j == 0:
                    r, k = iota((ROWS, SEG), 0), iota((ROWS, SEG), 1)
                    mask = (k <= r) & (r < SEG)
                for h in range(2):
                    attend(queries[j], keys_of([own], h), values_of([own], h), bias, acc, m, j, h, mask)

            if j == 0:
                one()
            else:
                pl.when(info[I_X] < info[I_X + j])(one)
    ok = [info[I_OK + 2 * (step - 1) + i] for i in range(len(others))]
    some = ok[0] if final else ok[0] + ok[1]

    @pl.when(some > 0)
    def _():
        biases = []
        for kv, good in zip(others, ok):
            row = kv[SEG : SEG + 1, :SEG].astype(F32) * LOG2E
            biases.append(jnp.where(good > 0, row, LOW))
        bias = jnp.concatenate(biases, axis=1)
        for h in range(2):
            k, v = keys_of(others, h), values_of(others, h)
            for j in range(4):
                attend(queries[j], k, v, bias, acc, m, j, h)

    if final:
        row = iota((16, COLS), 0)
        for j in range(4):
            tail = jnp.zeros((16, COLS), F32)
            ends = []
            for h in range(2):
                total = acc[j, h][:, HD:]
                some_keys = total > 0.0
                total = jnp.where(some_keys, total, 1.0)
                out = acc[j, h][:, :HD] / total
                logs = jnp.where(some_keys, m[j, h] + jnp.log2(total), LOW)
                payloads[j][:SEG, h * HD : (h + 1) * HD] = out[:SEG].astype(BF16)
                ends.append(out[SEG:])
                parts = split(jnp.transpose(logs[:SEG])[:16], 3)
                for i, part in enumerate(parts):
                    tail = jnp.where(row == 1 + 3 * h + i, part, tail)
                parts = split(wide(logs[SEG : SEG + 1], 2), 3)
                for i, part in enumerate(parts):
                    tail = jnp.where(row == 7 + 3 * h + i, part, tail)
            tail = jnp.where(row == 0, jnp.concatenate(ends, axis=1), tail)
            payloads[j][SEG:, :] = tail.astype(BF16)


STATE = [shape((4, 2, ROWS, 2 * HD), F32), shape((4, 2, ROWS, HD), F32), shape((8, 128), F32)]


def attend_step(step, info, queries, own, others, state):
    first, final, has_own = step == 1, step == 4, own is not None
    ins = [info] + queries + ([own] if has_own else []) + others + list(state or [])
    flops = 4 * 1088 * SEG * (len(others) + 1) * COLS
    body = functools.partial(attend_kernel, step, has_own)
    if final:
        outs = [shape((ROWS, COLS), BF16)] * 4 + STATE[:2]
        aliases = {len(ins) - 2: 4, len(ins) - 1: 5}

        def body(*refs):
            refs = list(refs)
            payloads, state = refs[-6:-2], refs[-2:]
            attend_kernel(step, has_own, *refs[:-8], *state, *payloads)

        return call(body, outs, ins, flops=flops, moved=4 << 20, aliases=aliases)[:4]
    aliases = {} if first else {len(ins) - 2: 0, len(ins) - 1: 1}
    return call(body, STATE, ins, flops=flops, moved=4 << 20, aliases=aliases)


def merge_kernel(info, a, b, c, d, out):
    parts = (a, b, c, d)
    tails = [p[SEG:, :].astype(F32) for p in parts]
    weights, end_weights = [], []
    for h in range(2):
        for base, store in ((1 + 3 * h, weights), (7 + 3 * h, end_weights)):
            logs = [t[base : base + 1] + t[base + 1 : base + 2] + t[base + 2 : base + 3] for t in tails]
            peak = functools.reduce(jnp.maximum, logs)
            expo = [jnp.exp2(v - peak) for v in logs]
            whole = functools.reduce(jnp.add, expo)
            store.append([e / whole for e in expo])
    flat = weights[0] + weights[1]
    columns = jnp.transpose(jnp.concatenate(flat + [jnp.zeros((120, SEG), F32)], axis=0))
    ends = []
    for h in range(2):
        lanes = slice(h * HD, (h + 1) * HD)
        acc = jnp.zeros((SEG, HD), F32)
        end = jnp.zeros((16, HD), F32)
        for j, p in enumerate(parts):
            acc = acc + columns[:, 4 * h + j : 4 * h + j + 1] * p[:SEG, lanes].astype(F32)
            end = end + end_weights[h][j][:, :HD] * tails[j][:, lanes]
        out[:SEG, lanes] = acc.astype(BF16)
        ends.append(end)
    end = jnp.concatenate(ends, axis=1)
    out[SEG:, :] = jnp.where(iota((16, COLS), 0) == 0, end, 0.0).astype(BF16)


BLOCK = 512
TALL = 384


def mark_kernel(ids, out):
    lane = iota((128, 128), 1)
    for r in range(TOK // 128):
        row = ids[r : r + 1, :].astype(F32)
        column = jnp.transpose(jnp.broadcast_to(row, (128, 128))).astype(jnp.int32)
        rows = slice(r * 128, (r + 1) * 128)
        out[rows, :128] = ones_where(column == lane)
        out[rows, 128:256] = ones_where(column == lane + 128)
        out[rows, 256:] = ones_where((column == -1) & (lane == 0))


def output_kernel(own, first, second, hot, tokens, out, coarse):
    @pl.when(pl.program_id(0) == 0)
    def _():
        total = own[...] + first[...].astype(F32) + second[...].astype(F32)
        coarse[:ROWS, :] = total.astype(BF16)
        coarse[ROWS:, :] = jnp.zeros((TALL - ROWS, FEAT), BF16)

    picked = dot(hot[...], coarse[...])
    out[...] = (tokens[...].astype(F32) + picked).astype(BF16)


def output(products, hot, tokens):
    return pl.pallas_call(
        output_kernel,
        grid=(TOK // BLOCK,),
        out_shape=shape((TOK, FEAT), BF16),
        in_specs=[WHOLE] * 3
        + [pl.BlockSpec((BLOCK, TALL), lambda i: (i, 0)), pl.BlockSpec((BLOCK, FEAT), lambda i: (i, 0))],
        out_specs=pl.BlockSpec((BLOCK, FEAT), lambda i: (i, 0)),
        scratch_shapes=[pltpu.VMEM((TALL, FEAT), BF16)],
        compiler_params=pltpu.CompilerParams(vmem_limit_bytes=VMEM_LIMIT),
        cost_estimate=pl.CostEstimate(flops=2 << 30, bytes_accessed=6 << 20, transcendentals=0),
    )(*products, hot, tokens)


def cut_kernel(info, w_out, _, sibling, sems):
    copies = []
    for i in range(4):
        start = pl.multiple_of(info[I_CUT + 4 + i] * FEAT, FEAT)
        copies.append(pltpu.make_async_copy(w_out.at[:, pl.ds(start, FEAT)], sibling.at[i], sems.at[i]))
        copies[-1].start()
    for copy in copies:
        copy.wait()


def product_kernel(info, attended, other, w_out, theirs, means, own_out, *outs):
    for i in range(4):
        start = pl.multiple_of(info[I_CUT + i] * FEAT, FEAT)
        part = dot(attended[...], w_out[:, pl.ds(start, FEAT)]) + dot(other[...], theirs[i])
        if i == 0:
            own_out[...] = part + means[...]
        else:
            outs[i - 1][...] = part.astype(outs[i - 1].dtype)


def add_kernel(a, b, out):
    out[...] = (a[...] + b[...].astype(F32)).astype(BF16)


def shards(tokens, flags, norm_gain, w_query, w_key, w_value, w_out):
    seq, mp = lax.axis_index("seq"), lax.axis_index("mp")
    info = jnp.asarray(device_table())[seq * (NY * NC) + mp]
    edge = shape((8, FEAT + 128), F32)
    tokens, ids, head, tail = call(
        edge_kernel,
        [shape((TOK, FEAT), BF16), shape((16, 128), jnp.int32), edge, edge],
        [flags.reshape(16, 128), tokens],
        scalars=None,
        flops=1 << 28,
        moved=2 << 20,
        scratch=[
            pltpu.VMEM((16, TOK), BF16),
            pltpu.VMEM((16, 128), jnp.int32),
            pltpu.SemaphoreType.DMA((PIECES + 1,)),
        ],
        far_in=(0, 1),
        room=EDGE_ROOM,
    )
    count = NZ * NX
    above = lax.ppermute(head, "seq", [(i, i - 1) for i in range(1, count)])
    below = lax.ppermute(tail, "seq", [(i, i + 1) for i in range(count - 1)])
    *weights, loaded = call(
        load_kernel,
        [shape((WIDTH, COLS), BF16)] * 3 + [shape((8, 128), F32)],
        [tail, w_query, w_key, w_value],
        scalars=None,
        moved=12 << 20,
        scratch=[pltpu.SemaphoreType.DMA((3, 4))],
        far_in=range(4),
        room=ROOM,
    )
    sums, sizes = call(
        pool_kernel,
        [shape((SEG, FEAT), F32), shape((SEG, 128), F32)],
        [ids, tokens],
        scalars=None,
        flops=1 << 30,
        moved=2 << 20,
        scratch=[pltpu.VMEM((SEG, TOK), BF16)],
    )
    means, u, bias = call(
        norm_kernel,
        [shape((ROWS, FEAT), F32), shape((ROWS, FEAT), BF16), shape((16, FEAT), BF16)],
        [info, sums, sizes, head, above, below, norm_gain.reshape(8, FEAT), loaded],
    )
    first, sibling, second = y_one(u), swap(u), y_other(u)
    across = swap(first)
    part, part_query = shape((SEG, COLS), F32), shape((ROWS, COLS), F32)
    queried, keyed, valued = call(
        early_kernel,
        [part_query, part, part],
        [info, u, first, second, sibling, *weights],
        flops=ROWS * WIDTH * 3 * COLS,
        moved=3 << 20,
    )
    far = y_one(first)
    blocks = [u, first, second, far, sibling, across, swap(second), swap(far)]
    (kv,) = call(
        key_value_kernel,
        [shape((ROWS, 2 * COLS), BF16)],
        [info] + blocks + [weights[1], weights[2], keyed, valued, bias],
    )
    (query,) = call(
        query_kernel,
        [shape((ROWS, COLS), BF16)],
        [info] + blocks + [weights[0], queried, kv],
        far_in=(11,),
    )
    queries = [query] + [x_by(query, k) for k in (1, 2, 3)]
    one, other = z_one(kv), z_other(kv)
    one2, other2 = z_one(one), z_other(other)
    *state, done = attend_step(1, info, queries, None, [one, other], None)
    (theirs,) = call(
        cut_kernel,
        [shape((4, SEG, FEAT), BF16)],
        [info, w_out, done],
        scratch=[pltpu.SemaphoreType.DMA((4,))],
        far_in=(1, 2),
        far_out=(0,),
    )
    theirs = swap(theirs)
    one2, other2 = gate(info, [one2, other2], done)
    one3, other3 = z_one(one2), z_other(other2)
    *state, done = attend_step(2, info, queries, kv, [one2, other2], state)
    (one3_sent,) = gate(info, [one3], done)
    one4 = z_one(one3_sent)
    *state, done = attend_step(3, info, queries, None, [one3_sent, other3], state)
    partial = attend_step(4, info, queries, None, [one4], state)
    partial = [partial[0]] + [x_by(partial[k], -k) for k in (1, 2, 3)]
    (attended,) = call(merge_kernel, [shape((ROWS, COLS), BF16)], [info] + partial, moved=1 << 20)
    block = shape((ROWS, FEAT), BF16)
    own, first, second, third = call(
        product_kernel,
        [shape((ROWS, FEAT), F32)] * 2 + [block] * 2,
        [info, attended, swap(attended), w_out, theirs, means],
        flops=2 * ROWS * 2 * COLS * 4 * FEAT,
        moved=4 << 20,
    )
    (hot,) = call(mark_kernel, [shape((TOK, TALL), BF16)], [ids], flops=1 << 29, moved=3 << 20, scalars=None)
    (first,) = call(add_kernel, [block], [first, y_one(third)], scalars=None)
    return output([own, y_one(first), y_other(second)], hot, tokens)


def solution(mesh):
    placed = (
        P(("dp", "seq"), "mp"),
        P(("dp", "seq")),
        P(),
        P(None, "mp"),
        P(None, "mp"),
        P(None, "mp"),
        P("mp", None),
    )
    return jax.shard_map(
        shards, mesh=mesh, in_specs=placed, out_specs=P(("dp", "seq"), "mp"), check_vma=False
    )
```

```python
import functools

import jax
import jax.numpy as jnp
import numpy as np
from jax import lax
from jax.experimental import pallas as pl
from jax.experimental.pallas import tpu as pltpu
from jax.sharding import PartitionSpec as P

HD = 128
NZ, NX, NY, NC = 8, 4, 4, 2
SEG = 256
ROWS = SEG + 16
TOK = 2048
FEAT = 512
COLS = 256
WIDTH = 4096
SCORE = 1.4426950408889634 * HD**-0.5
LOG2E = 1.4426950408889634
LOW = -1e30
VMEM_LIMIT = 20 * 1024 * 1024
ROOM = 47 * 1024 * 1024
EDGE_ROOM = 51 * 1024 * 1024
PIECES = 8
F32, BF16 = jnp.float32, jnp.bfloat16


def number(z, x, y, c):
    return ((z % NZ) * NX + x % NX) * (NY * NC) + (y % NY) * NC + c % NC


def everywhere():
    return [(z, x, y, c) for z in range(NZ) for x in range(NX) for y in range(NY) for c in range(NC)]


def way(c):
    return 1 if c == 0 else -1


def move(value, target):
    pairs = [(number(*d), number(*target(*d))) for d in everywhere()]
    return lax.ppermute(value, ("seq", "mp"), pairs)


def swap(value):
    return move(value, lambda z, x, y, c: (z, x, y, 1 - c))


def y_one(value):
    return move(value, lambda z, x, y, c: (z, x, y + way(c), c))


def y_other(value):
    return move(value, lambda z, x, y, c: (z, x, y - way(c), c))


def z_one(value):
    return move(value, lambda z, x, y, c: (z + way(c), x, y, c))


def z_other(value):
    return move(value, lambda z, x, y, c: (z - way(c), x, y, c))


def x_by(value, by):
    return move(value, lambda z, x, y, c: (z, x + by, y, c))


def sources(y, c):
    own = [(y, c), (y - way(c), c), (y + way(c), c), (y + 2, c)]
    o = 1 - c
    other = [(y, o), (y - way(o), o), (y + way(o), o), (y + 2, o)]
    return [((b[0] % NY) * NC + b[1]) for b in own + other]


def mp_exchange(value):
    first = y_one(value)
    second = y_other(value)
    sibling = swap(value)
    far = y_one(first)
    return [value, first, second, far, sibling, swap(first), swap(second), swap(far)]


def device_table():
    rows = []
    for z, x, y, c in everywhere():
        row = [y * NC + c] + sources(y, c)
        row += [x] + [(x - k) % NX for k in (1, 2, 3)]
        for k in (1, 2, 3, 4):
            row += [int((z - way(c) * k) % NZ < z), int((z + way(c) * k) % NZ < z)]
        for o in (c, 1 - c):
            row += [(v % NY) * NC + o for v in (y, y + way(o), y - way(o), y + 2)]
        row += [0] * (32 - len(row))
        rows.append(row)
    return np.asarray(rows, np.int32)


I_MP, I_SRC, I_X, I_OK, I_CUT = 0, 1, 9, 13, 21
SMEM = pl.BlockSpec(memory_space=pltpu.SMEM)
WHOLE = pl.BlockSpec(memory_space=pltpu.VMEM)
FAR = pl.BlockSpec(memory_space=pl.ANY)
DISTANT = pl.BlockSpec(memory_space=pltpu.HBM)


def call(body, outs, ins, flops=0, moved=0, scratch=(), aliases=None, far_in=(), far_out=(), far=FAR, scalars=0, room=VMEM_LIMIT):
    return pl.pallas_call(
        body,
        out_shape=outs,
        in_specs=[SMEM if i == scalars else far if i in far_in else WHOLE for i in range(len(ins))],
        out_specs=[far if i in far_out else WHOLE for i in range(len(outs))],
        scratch_shapes=list(scratch),
        input_output_aliases=aliases or {},
        compiler_params=pltpu.CompilerParams(vmem_limit_bytes=room),
        cost_estimate=pl.CostEstimate(flops=flops, bytes_accessed=moved, transcendentals=0),
    )(*ins)


def gate_kernel(info, *refs):
    pass


def gate(info, values, token):
    ins = [info] + list(values) + [token]
    count = len(values)
    return call(
        gate_kernel,
        [shape(v.shape, v.dtype) for v in values],
        ins,
        aliases={i + 1: i for i in range(count)},
        far_in=range(1, count + 2),
        far_out=range(count),
    )


def shape(dims, dtype):
    return jax.ShapeDtypeStruct(dims, dtype)


def dot(a, b):
    return jnp.dot(a, b, preferred_element_type=F32)


def iota(dims, axis):
    return lax.broadcasted_iota(jnp.int32, dims, axis)


def ones_where(condition):
    return jnp.where(condition, 1.0, 0.0).astype(BF16)


def edge_kernel(flags_in, tokens_in, tokens, ids_out, head_out, tail_out, marks, flags, sems):
    copies = [pltpu.make_async_copy(flags_in, flags, sems.at[PIECES])]
    for i in range(PIECES):
        rows = pl.ds(i * (TOK // PIECES), TOK // PIECES)
        copies.append(pltpu.make_async_copy(tokens_in.at[rows, :], tokens.at[rows, :], sems.at[i]))
    for copy in copies:
        copy.start()
    copies[0].wait()
    f = flags[...].astype(F32).astype(BF16)
    upto = ones_where(iota((128, 128), 0) <= iota((128, 128), 1))
    inside = dot(f, upto)
    rows = dot(f, jnp.ones((128, 128), BF16)).astype(BF16)
    before = dot(ones_where(iota((16, 16), 1) < iota((16, 16), 0)), rows)
    ids_out[...] = (inside + before - 1.0).astype(jnp.int32)
    wanted = jnp.where(iota((16, 128), 0) < 8, -1, SEG - 1)
    for r in range(16):
        marks[:, r * 128 : (r + 1) * 128] = ones_where(ids_out[r : r + 1, :] == wanted)
    for copy in copies[1:]:
        copy.wait()
    sums = dot(marks[...], tokens[...])
    counts = dot(marks[...], jnp.ones((TOK, 128), BF16))
    head_out[:, :FEAT] = sums[:8]
    head_out[:, FEAT:] = counts[:8]
    tail_out[:, :FEAT] = sums[8:]
    tail_out[:, FEAT:] = counts[8:]


def pool_kernel(ids, tokens, sums_out, counts_out, hot):
    segment = iota((SEG, 128), 0)
    for r in range(16):
        hot[:, r * 128 : (r + 1) * 128] = ones_where(ids[r : r + 1, :] == segment)
    sums_out[...] = dot(hot[...], tokens[...])
    counts_out[...] = dot(hot[...], jnp.ones((TOK, 128), BF16))


def wide(column, times):
    return jnp.concatenate([column] * times, axis=1)


def split(value, parts):
    out = []
    for _ in range(parts):
        high = value.astype(BF16).astype(F32)
        out.append(high)
        value = value - high
    return out


def norm_kernel(info, sums, counts, head, above, below, gain, means_out, u_out, bias_out):
    g = gain[pl.ds(info[I_MP], 1), :]
    last = iota((SEG, 128), 0) == SEG - 1
    size = counts[...] + jnp.where(last, above[0:1, FEAT:], 0.0)
    total = sums[...] + jnp.where(iota((SEG, FEAT), 0) == SEG - 1, above[0:1, :FEAT], 0.0)
    size = jnp.maximum(size, 1.0)
    means = total / wide(size, 4)
    means_out[:SEG, :] = means
    u_out[:SEG, :] = (means * g).astype(BF16)
    squares = jnp.sum(means * means, axis=1, keepdims=True)
    squares = jnp.transpose(jnp.broadcast_to(squares, (SEG, 128)))[:16]
    high, low = split(squares, 2)
    extra_size = jnp.maximum(head[0:1, FEAT:] + below[0:1, FEAT:], 1.0)
    extra = (head[0:1, :FEAT] + below[0:1, :FEAT]) / wide(extra_size, 4)
    extra_squares = jnp.broadcast_to(jnp.sum(extra * extra, axis=1, keepdims=True), (16, SEG))
    extra_high, extra_low = split(extra_squares, 2)
    row = iota((16, FEAT), 0)
    means_out[SEG:, :] = jnp.where(row == 0, extra, 0.0)
    tail = jnp.where(row == 0, extra * g, 0.0)
    tail = jnp.where(row == 1, jnp.concatenate([high, low], axis=1), tail)
    tail = jnp.where(row == 2, jnp.concatenate([extra_high, extra_low], axis=1), tail)
    u_out[SEG:, :] = tail.astype(BF16)
    bias = jnp.log(jnp.transpose(size)[:16])
    bias_out[...] = jnp.concatenate([bias, bias], axis=1).astype(BF16)


EARLY = (0, 1, 2, 4)
LATE = (3, 5, 6, 7)


def row_scale(tail):
    squares = tail[:, :SEG] + tail[:, SEG:]
    scale = lax.rsqrt(squares / WIDTH + 1e-05)
    column = jnp.transpose(jnp.broadcast_to(scale[1:2, :], (128, SEG)))
    return scale, wide(column, 2)


def load_kernel(*refs):
    sources, outs, sems = refs[:3], refs[4:7], refs[8]
    copies = []
    for n in range(3):
        for i in range(4):
            rows = pl.ds(i * (WIDTH // 4), WIDTH // 4)
            copies.append(pltpu.make_async_copy(sources[n].at[rows, :], outs[n].at[rows, :], sems.at[n, i]))
            copies[-1].start()
    for copy in copies:
        copy.wait()


def product(info, acc, blocks, which, weight, rows):
    for i, u in zip(which, blocks):
        start = pl.multiple_of(info[I_SRC + i] * FEAT, FEAT)
        part = dot(u[:rows, :], weight[pl.ds(start, FEAT), :])
        acc = part if acc is None else acc + part
    return acc


def early_kernel(info, *refs):
    blocks, weights, sums = refs[:4], refs[4:7], refs[7:]
    for n, rows in enumerate((ROWS, SEG, SEG)):
        sums[n][...] = product(info, None, blocks, EARLY, weights[n], rows)


def square_rows(blocks):
    tail = jnp.zeros((16, FEAT), F32)
    for u in blocks:
        tail = tail + u[SEG:, :].astype(F32)
    return tail


def key_value_kernel(info, *refs):
    blocks, late = refs[:8], [refs[i] for i in LATE]
    w_key, w_value, keys, values, bias, kv_out = refs[8:]
    _, column = row_scale(square_rows(blocks))
    kv_out[:SEG, :COLS] = (product(info, keys[...], late, LATE, w_key, SEG) * column).astype(BF16)
    kv_out[:SEG, COLS:] = (product(info, values[...], late, LATE, w_value, SEG) * column).astype(BF16)
    kv_out[SEG:, :] = bias[...]


def query_kernel(info, *refs):
    blocks, late = refs[:8], [refs[i] for i in LATE]
    w_query, partial, _, q_out = refs[8:]
    scale, column = row_scale(square_rows(blocks))
    query = product(info, partial[...], late, LATE, w_query, ROWS)
    q_out[:SEG, :] = (query[:SEG] * column * SCORE).astype(BF16)
    extra = query[SEG:] * scale[2:3, :] * SCORE
    q_out[SEG:, :] = jnp.where(iota((16, COLS), 0) == 0, extra, 0.0).astype(BF16)


def nt_dot(a, b):
    return lax.dot_general(a, b, (((1,), (1,)), ((), ())), preferred_element_type=F32)


def attend(q, k, v, bias, acc_ref, m_ref, j, h, mask=None):
    scores = nt_dot(q[:, h * HD : (h + 1) * HD], k) + bias
    if mask is not None:
        scores = jnp.where(mask, scores, LOW)
    old = m_ref[j, h]
    peak = jnp.maximum(old, jnp.max(scores, axis=1, keepdims=True))
    expo = jnp.exp2(scores - wide(peak, scores.shape[1] // 128))
    if mask is not None:
        expo = jnp.where(mask, expo, 0.0)
    m_ref[j, h] = peak
    acc_ref[j, h] = acc_ref[j, h] * wide(jnp.exp2(old - peak), 2) + dot(expo.astype(BF16), v)


def keys_of(blocks, h):
    return jnp.concatenate([kv[:SEG, h * HD : (h + 1) * HD] for kv in blocks], axis=0)


def values_of(blocks, h):
    lanes = slice(COLS + h * HD, COLS + (h + 1) * HD)
    values = jnp.concatenate([kv[:SEG, lanes] for kv in blocks], axis=0)
    return jnp.concatenate([values, jnp.ones(values.shape, BF16)], axis=1)


def attend_kernel(step, has_own, info, *refs):
    first, final = step == 1, step == 4
    refs = list(refs)
    queries = [refs.pop(0) for _ in range(4)]
    own = refs.pop(0) if has_own else None
    others = [refs.pop(0) for _ in range(1 if final else 2)]
    if not first:
        state_in = [refs.pop(0) for _ in range(2)]
    if final:
        payloads = [refs.pop(0) for _ in range(4)]
        acc, m = state_in
    else:
        acc, m, done = refs[:3]
        done[...] = jnp.zeros_like(done)
    if first:
        acc[...] = jnp.zeros_like(acc)
        m[...] = jnp.full(m.shape, LOW, F32)
    if has_own:
        bias = own[SEG : SEG + 1, :SEG].astype(F32) * LOG2E
        for j in range(4):

            def one(j=j):
                mask = None
                if j == 0:
                    r, k = iota((ROWS, SEG), 0), iota((ROWS, SEG), 1)
                    mask = (k <= r) & (r < SEG)
                for h in range(2):
                    attend(queries[j], keys_of([own], h), values_of([own], h), bias, acc, m, j, h, mask)

            if j == 0:
                one()
            else:
                pl.when(info[I_X] < info[I_X + j])(one)
    ok = [info[I_OK + 2 * (step - 1) + i] for i in range(len(others))]
    some = ok[0] if final else ok[0] + ok[1]

    @pl.when(some > 0)
    def _():
        biases = []
        for kv, good in zip(others, ok):
            row = kv[SEG : SEG + 1, :SEG].astype(F32) * LOG2E
            biases.append(jnp.where(good > 0, row, LOW))
        bias = jnp.concatenate(biases, axis=1)
        for h in range(2):
            k, v = keys_of(others, h), values_of(others, h)
            for j in range(4):
                attend(queries[j], k, v, bias, acc, m, j, h)

    if final:
        row = iota((16, COLS), 0)
        for j in range(4):
            tail = jnp.zeros((16, COLS), F32)
            ends = []
            for h in range(2):
                total = acc[j, h][:, HD:]
                some_keys = total > 0.0
                total = jnp.where(some_keys, total, 1.0)
                out = acc[j, h][:, :HD] / total
                logs = jnp.where(some_keys, m[j, h] + jnp.log2(total), LOW)
                payloads[j][:SEG, h * HD : (h + 1) * HD] = out[:SEG].astype(BF16)
                ends.append(out[SEG:])
                parts = split(jnp.transpose(logs[:SEG])[:16], 3)
                for i, part in enumerate(parts):
                    tail = jnp.where(row == 1 + 3 * h + i, part, tail)
                parts = split(wide(logs[SEG : SEG + 1], 2), 3)
                for i, part in enumerate(parts):
                    tail = jnp.where(row == 7 + 3 * h + i, part, tail)
            tail = jnp.where(row == 0, jnp.concatenate(ends, axis=1), tail)
            payloads[j][SEG:, :] = tail.astype(BF16)


STATE = [shape((4, 2, ROWS, 2 * HD), F32), shape((4, 2, ROWS, HD), F32), shape((8, 128), F32)]


def attend_step(step, info, queries, own, others, state):
    first, final, has_own = step == 1, step == 4, own is not None
    ins = [info] + queries + ([own] if has_own else []) + others + list(state or [])
    flops = 4 * 1088 * SEG * (len(others) + 1) * COLS
    body = functools.partial(attend_kernel, step, has_own)
    if final:
        outs = [shape((ROWS, COLS), BF16)] * 4 + STATE[:2]
        aliases = {len(ins) - 2: 4, len(ins) - 1: 5}

        def body(*refs):
            refs = list(refs)
            payloads, state = refs[-6:-2], refs[-2:]
            attend_kernel(step, has_own, *refs[:-8], *state, *payloads)

        return call(body, outs, ins, flops=flops, moved=4 << 20, aliases=aliases)[:4]
    aliases = {} if first else {len(ins) - 2: 0, len(ins) - 1: 1}
    return call(body, STATE, ins, flops=flops, moved=4 << 20, aliases=aliases)


def merge_kernel(info, a, b, c, d, out):
    parts = (a, b, c, d)
    tails = [p[SEG:, :].astype(F32) for p in parts]
    weights, end_weights = [], []
    for h in range(2):
        for base, store in ((1 + 3 * h, weights), (7 + 3 * h, end_weights)):
            logs = [t[base : base + 1] + t[base + 1 : base + 2] + t[base + 2 : base + 3] for t in tails]
            peak = functools.reduce(jnp.maximum, logs)
            expo = [jnp.exp2(v - peak) for v in logs]
            whole = functools.reduce(jnp.add, expo)
            store.append([e / whole for e in expo])
    flat = weights[0] + weights[1]
    columns = jnp.transpose(jnp.concatenate(flat + [jnp.zeros((120, SEG), F32)], axis=0))
    ends = []
    for h in range(2):
        lanes = slice(h * HD, (h + 1) * HD)
        acc = jnp.zeros((SEG, HD), F32)
        end = jnp.zeros((16, HD), F32)
        for j, p in enumerate(parts):
            acc = acc + columns[:, 4 * h + j : 4 * h + j + 1] * p[:SEG, lanes].astype(F32)
            end = end + end_weights[h][j][:, :HD] * tails[j][:, lanes]
        out[:SEG, lanes] = acc.astype(BF16)
        ends.append(end)
    end = jnp.concatenate(ends, axis=1)
    out[SEG:, :] = jnp.where(iota((16, COLS), 0) == 0, end, 0.0).astype(BF16)


BLOCK = 512
TALL = 384


def mark_kernel(ids, out):
    lane = iota((128, 128), 1)
    for r in range(TOK // 128):
        row = ids[r : r + 1, :].astype(F32)
        column = jnp.transpose(jnp.broadcast_to(row, (128, 128))).astype(jnp.int32)
        rows = slice(r * 128, (r + 1) * 128)
        out[rows, :128] = ones_where(column == lane)
        out[rows, 128:256] = ones_where(column == lane + 128)
        out[rows, 256:] = ones_where((column == -1) & (lane == 0))


def output_kernel(own, first, second, hot, tokens, out, coarse):
    @pl.when(pl.program_id(0) == 0)
    def _():
        total = own[...] + first[...].astype(F32) + second[...].astype(F32)
        coarse[:ROWS, :] = total.astype(BF16)
        coarse[ROWS:, :] = jnp.zeros((TALL - ROWS, FEAT), BF16)

    picked = dot(hot[...], coarse[...])
    out[...] = (tokens[...].astype(F32) + picked).astype(BF16)


def output(products, hot, tokens):
    return pl.pallas_call(
        output_kernel,
        grid=(TOK // BLOCK,),
        out_shape=shape((TOK, FEAT), BF16),
        in_specs=[WHOLE] * 3
        + [pl.BlockSpec((BLOCK, TALL), lambda i: (i, 0)), pl.BlockSpec((BLOCK, FEAT), lambda i: (i, 0))],
        out_specs=pl.BlockSpec((BLOCK, FEAT), lambda i: (i, 0)),
        scratch_shapes=[pltpu.VMEM((TALL, FEAT), BF16)],
        compiler_params=pltpu.CompilerParams(vmem_limit_bytes=VMEM_LIMIT),
        cost_estimate=pl.CostEstimate(flops=2 << 30, bytes_accessed=6 << 20, transcendentals=0),
    )(*products, hot, tokens)


def cut_kernel(info, w_out, _, sibling, sems):
    copies = []
    for i in range(4):
        start = pl.multiple_of(info[I_CUT + 4 + i] * FEAT, FEAT)
        copies.append(pltpu.make_async_copy(w_out.at[:, pl.ds(start, FEAT)], sibling.at[i], sems.at[i]))
        copies[-1].start()
    for copy in copies:
        copy.wait()


def product_kernel(info, attended, other, w_out, theirs, means, own_out, *outs):
    for i in range(4):
        start = pl.multiple_of(info[I_CUT + i] * FEAT, FEAT)
        part = dot(attended[...], w_out[:, pl.ds(start, FEAT)]) + dot(other[...], theirs[i])
        if i == 0:
            own_out[...] = part + means[...]
        else:
            outs[i - 1][...] = part.astype(outs[i - 1].dtype)


def add_kernel(a, b, out):
    out[...] = (a[...] + b[...].astype(F32)).astype(BF16)


def shards(tokens, flags, norm_gain, w_query, w_key, w_value, w_out):
    seq, mp = lax.axis_index("seq"), lax.axis_index("mp")
    info = jnp.asarray(device_table())[seq * (NY * NC) + mp]
    edge = shape((8, FEAT + 128), F32)
    tokens, ids, head, tail = call(
        edge_kernel,
        [shape((TOK, FEAT), BF16), shape((16, 128), jnp.int32), edge, edge],
        [flags.reshape(16, 128), tokens],
        scalars=None,
        flops=1 << 28,
        moved=2 << 20,
        scratch=[
            pltpu.VMEM((16, TOK), BF16),
            pltpu.VMEM((16, 128), jnp.int32),
            pltpu.SemaphoreType.DMA((PIECES + 1,)),
        ],
        far_in=(0, 1),
        room=EDGE_ROOM,
    )
    count = NZ * NX
    above = lax.ppermute(head, "seq", [(i, i - 1) for i in range(1, count)])
    below = lax.ppermute(tail, "seq", [(i, i + 1) for i in range(count - 1)])
    sums, sizes = call(
        pool_kernel,
        [shape((SEG, FEAT), F32), shape((SEG, 128), F32)],
        [ids, tokens],
        scalars=None,
        flops=1 << 30,
        moved=2 << 20,
        scratch=[pltpu.VMEM((SEG, TOK), BF16)],
    )
    means, u, bias = call(
        norm_kernel,
        [shape((ROWS, FEAT), F32), shape((ROWS, FEAT), BF16), shape((16, FEAT), BF16)],
        [info, sums, sizes, head, above, below, norm_gain.reshape(8, FEAT)],
    )
    *weights, handed = call(
        load_kernel,
        [shape((WIDTH, COLS), BF16)] * 3 + [shape(u.shape, BF16)],
        [w_query, w_key, w_value, u],
        scalars=None,
        moved=12 << 20,
        scratch=[pltpu.SemaphoreType.DMA((3, 4))],
        aliases={3: 3},
        far_in=range(4),
        far_out=(3,),
        room=ROOM,
    )
    first, sibling, second = y_one(u), swap(handed), y_other(u)
    across = swap(first)
    part, part_query = shape((SEG, COLS), F32), shape((ROWS, COLS), F32)
    queried, keyed, valued = call(
        early_kernel,
        [part_query, part, part],
        [info, u, first, second, sibling, *weights],
        flops=ROWS * WIDTH * 3 * COLS,
        moved=3 << 20,
    )
    far = y_one(first)
    blocks = [u, first, second, far, sibling, across, swap(second), swap(far)]
    (kv,) = call(
        key_value_kernel,
        [shape((ROWS, 2 * COLS), BF16)],
        [info] + blocks + [weights[1], weights[2], keyed, valued, bias],
    )
    (query,) = call(
        query_kernel,
        [shape((ROWS, COLS), BF16)],
        [info] + blocks + [weights[0], queried, kv],
        far_in=(11,),
    )
    queries = [query] + [x_by(query, k) for k in (1, 2, 3)]
    one, other = z_one(kv), z_other(kv)
    one2, other2 = z_one(one), z_other(other)
    *state, done = attend_step(1, info, queries, None, [one, other], None)
    (theirs,) = call(
        cut_kernel,
        [shape((4, SEG, FEAT), BF16)],
        [info, w_out, done],
        scratch=[pltpu.SemaphoreType.DMA((4,))],
        far_in=(1, 2),
        far_out=(0,),
    )
    theirs = swap(theirs)
    one2, other2 = gate(info, [one2, other2], done)
    one3, other3 = z_one(one2), z_other(other2)
    *state, done = attend_step(2, info, queries, kv, [one2, other2], state)
    (one3_sent,) = gate(info, [one3], done)
    one4 = z_one(one3_sent)
    *state, done = attend_step(3, info, queries, None, [one3_sent, other3], state)
    partial = attend_step(4, info, queries, None, [one4], state)
    partial = [partial[0]] + [x_by(partial[k], -k) for k in (1, 2, 3)]
    (attended,) = call(merge_kernel, [shape((ROWS, COLS), BF16)], [info] + partial, moved=1 << 20)
    block = shape((ROWS, FEAT), BF16)
    own, first, second, third = call(
        product_kernel,
        [shape((ROWS, FEAT), F32)] * 2 + [block] * 2,
        [info, attended, swap(attended), w_out, theirs, means],
        flops=2 * ROWS * 2 * COLS * 4 * FEAT,
        moved=4 << 20,
    )
    (hot,) = call(mark_kernel, [shape((TOK, TALL), BF16)], [ids], flops=1 << 29, moved=3 << 20, scalars=None)
    (first,) = call(add_kernel, [block], [first, y_one(third)], scalars=None)
    return output([own, y_one(first), y_other(second)], hot, tokens)


def solution(mesh):
    placed = (
        P(("dp", "seq"), "mp"),
        P(("dp", "seq")),
        P(),
        P(None, "mp"),
        P(None, "mp"),
        P(None, "mp"),
        P("mp", None),
    )
    return jax.shard_map(
        shards, mesh=mesh, in_specs=placed, out_specs=P(("dp", "seq"), "mp"), check_vma=False
    )
```

```python
import functools

import jax
import jax.numpy as jnp
import numpy as np
from jax import lax
from jax.experimental import pallas as pl
from jax.experimental.pallas import tpu as pltpu
from jax.sharding import PartitionSpec as P

HD = 128
NZ, NX, NY, NC = 8, 4, 4, 2
SEG = 256
ROWS = SEG + 16
TOK = 2048
FEAT = 512
COLS = 256
WIDTH = 4096
SCORE = 1.4426950408889634 * HD**-0.5
LOG2E = 1.4426950408889634
LOW = -1e30
VMEM_LIMIT = 20 * 1024 * 1024
ROOM = 47 * 1024 * 1024
EDGE_ROOM = 51 * 1024 * 1024
PIECES = 8
F32, BF16 = jnp.float32, jnp.bfloat16


def number(z, x, y, c):
    return ((z % NZ) * NX + x % NX) * (NY * NC) + (y % NY) * NC + c % NC


def everywhere():
    return [(z, x, y, c) for z in range(NZ) for x in range(NX) for y in range(NY) for c in range(NC)]


def way(c):
    return 1 if c == 0 else -1


def move(value, target):
    pairs = [(number(*d), number(*target(*d))) for d in everywhere()]
    return lax.ppermute(value, ("seq", "mp"), pairs)


def swap(value):
    return move(value, lambda z, x, y, c: (z, x, y, 1 - c))


def y_one(value):
    return move(value, lambda z, x, y, c: (z, x, y + way(c), c))


def y_other(value):
    return move(value, lambda z, x, y, c: (z, x, y - way(c), c))


def z_one(value):
    return move(value, lambda z, x, y, c: (z + way(c), x, y, c))


def z_other(value):
    return move(value, lambda z, x, y, c: (z - way(c), x, y, c))


def x_by(value, by):
    return move(value, lambda z, x, y, c: (z, x + by, y, c))


def sources(y, c):
    own = [(y, c), (y - way(c), c), (y + way(c), c), (y + 2, c)]
    o = 1 - c
    other = [(y, o), (y - way(o), o), (y + way(o), o), (y + 2, o)]
    return [((b[0] % NY) * NC + b[1]) for b in own + other]


def mp_exchange(value):
    first = y_one(value)
    second = y_other(value)
    sibling = swap(value)
    far = y_one(first)
    return [value, first, second, far, sibling, swap(first), swap(second), swap(far)]


def device_table():
    rows = []
    for z, x, y, c in everywhere():
        row = [y * NC + c] + sources(y, c)
        row += [x] + [(x - k) % NX for k in (1, 2, 3)]
        for k in (1, 2, 3, 4):
            row += [int((z - way(c) * k) % NZ < z), int((z + way(c) * k) % NZ < z)]
        for o in (c, 1 - c):
            row += [(v % NY) * NC + o for v in (y, y + way(o), y - way(o), y + 2)]
        row += [0] * (32 - len(row))
        rows.append(row)
    return np.asarray(rows, np.int32)


I_MP, I_SRC, I_X, I_OK, I_CUT = 0, 1, 9, 13, 21
SMEM = pl.BlockSpec(memory_space=pltpu.SMEM)
WHOLE = pl.BlockSpec(memory_space=pltpu.VMEM)
FAR = pl.BlockSpec(memory_space=pl.ANY)
DISTANT = pl.BlockSpec(memory_space=pltpu.HBM)


def call(body, outs, ins, flops=0, moved=0, scratch=(), aliases=None, far_in=(), far_out=(), far=FAR, scalars=0, room=VMEM_LIMIT):
    return pl.pallas_call(
        body,
        out_shape=outs,
        in_specs=[SMEM if i == scalars else far if i in far_in else WHOLE for i in range(len(ins))],
        out_specs=[far if i in far_out else WHOLE for i in range(len(outs))],
        scratch_shapes=list(scratch),
        input_output_aliases=aliases or {},
        compiler_params=pltpu.CompilerParams(vmem_limit_bytes=room),
        cost_estimate=pl.CostEstimate(flops=flops, bytes_accessed=moved, transcendentals=0),
    )(*ins)


def gate_kernel(info, *refs):
    pass


def gate(info, values, token):
    ins = [info] + list(values) + [token]
    count = len(values)
    return call(
        gate_kernel,
        [shape(v.shape, v.dtype) for v in values],
        ins,
        aliases={i + 1: i for i in range(count)},
        far_in=range(1, count + 2),
        far_out=range(count),
    )


def shape(dims, dtype):
    return jax.ShapeDtypeStruct(dims, dtype)


def dot(a, b):
    return jnp.dot(a, b, preferred_element_type=F32)


def iota(dims, axis):
    return lax.broadcasted_iota(jnp.int32, dims, axis)


def ones_where(condition):
    return jnp.where(condition, 1.0, 0.0).astype(BF16)


def edge_kernel(flags_in, tokens_in, tokens, ids_out, head_out, tail_out, marks, flags, sems):
    copies = [pltpu.make_async_copy(flags_in, flags, sems.at[PIECES])]
    for i in range(PIECES):
        rows = pl.ds(i * (TOK // PIECES), TOK // PIECES)
        copies.append(pltpu.make_async_copy(tokens_in.at[rows, :], tokens.at[rows, :], sems.at[i]))
    for copy in copies:
        copy.start()
    copies[0].wait()
    f = flags[...].astype(F32).astype(BF16)
    upto = ones_where(iota((128, 128), 0) <= iota((128, 128), 1))
    inside = dot(f, upto)
    rows = dot(f, jnp.ones((128, 128), BF16)).astype(BF16)
    before = dot(ones_where(iota((16, 16), 1) < iota((16, 16), 0)), rows)
    ids_out[...] = (inside + before - 1.0).astype(jnp.int32)
    wanted = jnp.where(iota((16, 128), 0) < 8, -1, SEG - 1)
    for r in range(16):
        marks[:, r * 128 : (r + 1) * 128] = ones_where(ids_out[r : r + 1, :] == wanted)
    for copy in copies[1:]:
        copy.wait()
    sums = dot(marks[...], tokens[...])
    counts = dot(marks[...], jnp.ones((TOK, 128), BF16))
    head_out[:, :FEAT] = sums[:8]
    head_out[:, FEAT:] = counts[:8]
    tail_out[:, :FEAT] = sums[8:]
    tail_out[:, FEAT:] = counts[8:]


def pool_kernel(ids, tokens, sums_out, counts_out, hot):
    segment = iota((SEG, 128), 0)
    for r in range(16):
        hot[:, r * 128 : (r + 1) * 128] = ones_where(ids[r : r + 1, :] == segment)
    sums_out[...] = dot(hot[...], tokens[...])
    counts_out[...] = dot(hot[...], jnp.ones((TOK, 128), BF16))


def wide(column, times):
    return jnp.concatenate([column] * times, axis=1)


def split(value, parts):
    out = []
    for _ in range(parts):
        high = value.astype(BF16).astype(F32)
        out.append(high)
        value = value - high
    return out


def norm_kernel(info, sums, counts, head, above, below, gain, means_out, u_out, bias_out):
    g = gain[pl.ds(info[I_MP], 1), :]
    last = iota((SEG, 128), 0) == SEG - 1
    size = counts[...] + jnp.where(last, above[0:1, FEAT:], 0.0)
    total = sums[...] + jnp.where(iota((SEG, FEAT), 0) == SEG - 1, above[0:1, :FEAT], 0.0)
    size = jnp.maximum(size, 1.0)
    means = total / wide(size, 4)
    means_out[:SEG, :] = means
    u_out[:SEG, :] = (means * g).astype(BF16)
    squares = jnp.sum(means * means, axis=1, keepdims=True)
    squares = jnp.transpose(jnp.broadcast_to(squares, (SEG, 128)))[:16]
    high, low = split(squares, 2)
    extra_size = jnp.maximum(head[0:1, FEAT:] + below[0:1, FEAT:], 1.0)
    extra = (head[0:1, :FEAT] + below[0:1, :FEAT]) / wide(extra_size, 4)
    extra_squares = jnp.broadcast_to(jnp.sum(extra * extra, axis=1, keepdims=True), (16, SEG))
    extra_high, extra_low = split(extra_squares, 2)
    row = iota((16, FEAT), 0)
    means_out[SEG:, :] = jnp.where(row == 0, extra, 0.0)
    tail = jnp.where(row == 0, extra * g, 0.0)
    tail = jnp.where(row == 1, jnp.concatenate([high, low], axis=1), tail)
    tail = jnp.where(row == 2, jnp.concatenate([extra_high, extra_low], axis=1), tail)
    u_out[SEG:, :] = tail.astype(BF16)
    bias = jnp.log(jnp.transpose(size)[:16])
    bias_out[...] = jnp.concatenate([bias, bias], axis=1).astype(BF16)


EARLY = (0, 1, 2, 4)
LATE = (3, 5, 6, 7)


def row_scale(tail):
    squares = tail[:, :SEG] + tail[:, SEG:]
    scale = lax.rsqrt(squares / WIDTH + 1e-05)
    column = jnp.transpose(jnp.broadcast_to(scale[1:2, :], (128, SEG)))
    return scale, wide(column, 2)


def load_kernel(*refs):
    sources, outs, sems = refs[:3], refs[4:7], refs[8]
    copies = []
    for n in range(3):
        for i in range(4):
            rows = pl.ds(i * (WIDTH // 4), WIDTH // 4)
            copies.append(pltpu.make_async_copy(sources[n].at[rows, :], outs[n].at[rows, :], sems.at[n, i]))
            copies[-1].start()
    for copy in copies:
        copy.wait()


def product(info, acc, blocks, which, weight, rows):
    for i, u in zip(which, blocks):
        start = pl.multiple_of(info[I_SRC + i] * FEAT, FEAT)
        part = dot(u[:rows, :], weight[pl.ds(start, FEAT), :])
        acc = part if acc is None else acc + part
    return acc


def early_kernel(info, *refs):
    blocks, weights, sums = refs[:4], refs[4:7], refs[7:]
    for n, rows in enumerate((ROWS, SEG, SEG)):
        sums[n][...] = product(info, None, blocks, EARLY, weights[n], rows)


def square_rows(blocks):
    tail = jnp.zeros((16, FEAT), F32)
    for u in blocks:
        tail = tail + u[SEG:, :].astype(F32)
    return tail


def key_value_kernel(info, *refs):
    blocks, late = refs[:8], [refs[i] for i in LATE]
    w_key, w_value, keys, values, bias, kv_out = refs[8:]
    _, column = row_scale(square_rows(blocks))
    kv_out[:SEG, :COLS] = (product(info, keys[...], late, LATE, w_key, SEG) * column).astype(BF16)
    kv_out[:SEG, COLS:] = (product(info, values[...], late, LATE, w_value, SEG) * column).astype(BF16)
    kv_out[SEG:, :] = bias[...]


def query_kernel(info, *refs):
    blocks, late = refs[:8], [refs[i] for i in LATE]
    w_query, partial, _, q_out = refs[8:]
    scale, column = row_scale(square_rows(blocks))
    query = product(info, partial[...], late, LATE, w_query, ROWS)
    q_out[:SEG, :] = (query[:SEG] * column * SCORE).astype(BF16)
    extra = query[SEG:] * scale[2:3, :] * SCORE
    q_out[SEG:, :] = jnp.where(iota((16, COLS), 0) == 0, extra, 0.0).astype(BF16)


def nt_dot(a, b):
    return lax.dot_general(a, b, (((1,), (1,)), ((), ())), preferred_element_type=F32)


def attend(q, k, v, bias, acc_ref, m_ref, j, h, mask=None):
    scores = nt_dot(q[:, h * HD : (h + 1) * HD], k) + bias
    if mask is not None:
        scores = jnp.where(mask, scores, LOW)
    old = m_ref[j, h]
    peak = jnp.maximum(old, jnp.max(scores, axis=1, keepdims=True))
    expo = jnp.exp2(scores - wide(peak, scores.shape[1] // 128))
    if mask is not None:
        expo = jnp.where(mask, expo, 0.0)
    m_ref[j, h] = peak
    acc_ref[j, h] = acc_ref[j, h] * wide(jnp.exp2(old - peak), 2) + dot(expo.astype(BF16), v)


def keys_of(blocks, h):
    return jnp.concatenate([kv[:SEG, h * HD : (h + 1) * HD] for kv in blocks], axis=0)


def values_of(blocks, h):
    lanes = slice(COLS + h * HD, COLS + (h + 1) * HD)
    values = jnp.concatenate([kv[:SEG, lanes] for kv in blocks], axis=0)
    return jnp.concatenate([values, jnp.ones(values.shape, BF16)], axis=1)


def attend_kernel(step, has_own, info, *refs):
    first, final = step == 1, step == 4
    refs = list(refs)
    queries = [refs.pop(0) for _ in range(4)]
    own = refs.pop(0) if has_own else None
    others = [refs.pop(0) for _ in range(1 if final else 2)]
    if not first:
        state_in = [refs.pop(0) for _ in range(2)]
    if final:
        payloads = [refs.pop(0) for _ in range(4)]
        acc, m = state_in
    else:
        acc, m, done = refs[:3]
        done[...] = jnp.zeros_like(done)
    if first:
        acc[...] = jnp.zeros_like(acc)
        m[...] = jnp.full(m.shape, LOW, F32)
    if has_own:
        bias = own[SEG : SEG + 1, :SEG].astype(F32) * LOG2E
        for j in range(4):

            def one(j=j):
                mask = None
                if j == 0:
                    r, k = iota((ROWS, SEG), 0), iota((ROWS, SEG), 1)
                    mask = (k <= r) & (r < SEG)
                for h in range(2):
                    attend(queries[j], keys_of([own], h), values_of([own], h), bias, acc, m, j, h, mask)

            if j == 0:
                one()
            else:
                pl.when(info[I_X] < info[I_X + j])(one)
    ok = [info[I_OK + 2 * (step - 1) + i] for i in range(len(others))]
    some = ok[0] if final else ok[0] + ok[1]

    @pl.when(some > 0)
    def _():
        biases = []
        for kv, good in zip(others, ok):
            row = kv[SEG : SEG + 1, :SEG].astype(F32) * LOG2E
            biases.append(jnp.where(good > 0, row, LOW))
        bias = jnp.concatenate(biases, axis=1)
        for h in range(2):
            k, v = keys_of(others, h), values_of(others, h)
            for j in range(4):
                attend(queries[j], k, v, bias, acc, m, j, h)

    if final:
        row = iota((16, COLS), 0)
        for j in range(4):
            tail = jnp.zeros((16, COLS), F32)
            ends = []
            for h in range(2):
                total = acc[j, h][:, HD:]
                some_keys = total > 0.0
                total = jnp.where(some_keys, total, 1.0)
                out = acc[j, h][:, :HD] / total
                logs = jnp.where(some_keys, m[j, h] + jnp.log2(total), LOW)
                payloads[j][:SEG, h * HD : (h + 1) * HD] = out[:SEG].astype(BF16)
                ends.append(out[SEG:])
                parts = split(jnp.transpose(logs[:SEG])[:16], 3)
                for i, part in enumerate(parts):
                    tail = jnp.where(row == 1 + 3 * h + i, part, tail)
                parts = split(wide(logs[SEG : SEG + 1], 2), 3)
                for i, part in enumerate(parts):
                    tail = jnp.where(row == 7 + 3 * h + i, part, tail)
            tail = jnp.where(row == 0, jnp.concatenate(ends, axis=1), tail)
            payloads[j][SEG:, :] = tail.astype(BF16)


STATE = [shape((4, 2, ROWS, 2 * HD), F32), shape((4, 2, ROWS, HD), F32), shape((8, 128), F32)]


def attend_step(step, info, queries, own, others, state):
    first, final, has_own = step == 1, step == 4, own is not None
    ins = [info] + queries + ([own] if has_own else []) + others + list(state or [])
    flops = 4 * 1088 * SEG * (len(others) + 1) * COLS
    body = functools.partial(attend_kernel, step, has_own)
    if final:
        outs = [shape((ROWS, COLS), BF16)] * 4 + STATE[:2]
        aliases = {len(ins) - 2: 4, len(ins) - 1: 5}

        def body(*refs):
            refs = list(refs)
            payloads, state = refs[-6:-2], refs[-2:]
            attend_kernel(step, has_own, *refs[:-8], *state, *payloads)

        return call(body, outs, ins, flops=flops, moved=4 << 20, aliases=aliases)[:4]
    aliases = {} if first else {len(ins) - 2: 0, len(ins) - 1: 1}
    return call(body, STATE, ins, flops=flops, moved=4 << 20, aliases=aliases)


def merge_kernel(info, a, b, c, d, out):
    parts = (a, b, c, d)
    tails = [p[SEG:, :].astype(F32) for p in parts]
    weights, end_weights = [], []
    for h in range(2):
        for base, store in ((1 + 3 * h, weights), (7 + 3 * h, end_weights)):
            logs = [t[base : base + 1] + t[base + 1 : base + 2] + t[base + 2 : base + 3] for t in tails]
            peak = functools.reduce(jnp.maximum, logs)
            expo = [jnp.exp2(v - peak) for v in logs]
            whole = functools.reduce(jnp.add, expo)
            store.append([e / whole for e in expo])
    flat = weights[0] + weights[1]
    columns = jnp.transpose(jnp.concatenate(flat + [jnp.zeros((120, SEG), F32)], axis=0))
    ends = []
    for h in range(2):
        lanes = slice(h * HD, (h + 1) * HD)
        acc = jnp.zeros((SEG, HD), F32)
        end = jnp.zeros((16, HD), F32)
        for j, p in enumerate(parts):
            acc = acc + columns[:, 4 * h + j : 4 * h + j + 1] * p[:SEG, lanes].astype(F32)
            end = end + end_weights[h][j][:, :HD] * tails[j][:, lanes]
        out[:SEG, lanes] = acc.astype(BF16)
        ends.append(end)
    end = jnp.concatenate(ends, axis=1)
    out[SEG:, :] = jnp.where(iota((16, COLS), 0) == 0, end, 0.0).astype(BF16)


BLOCK = 512
TALL = 384


def mark_kernel(ids, out):
    lane = iota((128, 128), 1)
    for r in range(TOK // 128):
        row = ids[r : r + 1, :].astype(F32)
        column = jnp.transpose(jnp.broadcast_to(row, (128, 128))).astype(jnp.int32)
        rows = slice(r * 128, (r + 1) * 128)
        out[rows, :128] = ones_where(column == lane)
        out[rows, 128:256] = ones_where(column == lane + 128)
        out[rows, 256:] = ones_where((column == -1) & (lane == 0))


def output_kernel(own, first, second, hot, tokens, out, coarse):
    @pl.when(pl.program_id(0) == 0)
    def _():
        total = own[...] + first[...].astype(F32) + second[...].astype(F32)
        coarse[:ROWS, :] = total.astype(BF16)
        coarse[ROWS:, :] = jnp.zeros((TALL - ROWS, FEAT), BF16)

    picked = dot(hot[...], coarse[...])
    out[...] = (tokens[...].astype(F32) + picked).astype(BF16)


def output(products, hot, tokens):
    return pl.pallas_call(
        output_kernel,
        grid=(TOK // BLOCK,),
        out_shape=shape((TOK, FEAT), BF16),
        in_specs=[WHOLE] * 3
        + [pl.BlockSpec((BLOCK, TALL), lambda i: (i, 0)), pl.BlockSpec((BLOCK, FEAT), lambda i: (i, 0))],
        out_specs=pl.BlockSpec((BLOCK, FEAT), lambda i: (i, 0)),
        scratch_shapes=[pltpu.VMEM((TALL, FEAT), BF16)],
        compiler_params=pltpu.CompilerParams(vmem_limit_bytes=VMEM_LIMIT),
        cost_estimate=pl.CostEstimate(flops=2 << 30, bytes_accessed=6 << 20, transcendentals=0),
    )(*products, hot, tokens)


def first_step_kernel(*refs):
    info, w_out, sibling, sems = refs[0], refs[7], refs[11], refs[12]
    copies = []
    for i in range(4):
        start = pl.multiple_of(info[I_CUT + 4 + i] * FEAT, FEAT)
        copies.append(pltpu.make_async_copy(w_out.at[:, pl.ds(start, FEAT)], sibling.at[i], sems.at[i]))
        copies[-1].start()
    attend_kernel(1, False, *refs[:7], *refs[8:11])
    for copy in copies:
        copy.wait()


def product_kernel(info, attended, other, w_out, theirs, means, own_out, *outs):
    for i in range(4):
        start = pl.multiple_of(info[I_CUT + i] * FEAT, FEAT)
        part = dot(attended[...], w_out[:, pl.ds(start, FEAT)]) + dot(other[...], theirs[i])
        if i == 0:
            own_out[...] = part + means[...]
        else:
            outs[i - 1][...] = part.astype(outs[i - 1].dtype)


def add_kernel(a, b, out):
    out[...] = (a[...] + b[...].astype(F32)).astype(BF16)


def shards(tokens, flags, norm_gain, w_query, w_key, w_value, w_out):
    seq, mp = lax.axis_index("seq"), lax.axis_index("mp")
    info = jnp.asarray(device_table())[seq * (NY * NC) + mp]
    edge = shape((8, FEAT + 128), F32)
    tokens, ids, head, tail = call(
        edge_kernel,
        [shape((TOK, FEAT), BF16), shape((16, 128), jnp.int32), edge, edge],
        [flags.reshape(16, 128), tokens],
        scalars=None,
        flops=1 << 28,
        moved=2 << 20,
        scratch=[
            pltpu.VMEM((16, TOK), BF16),
            pltpu.VMEM((16, 128), jnp.int32),
            pltpu.SemaphoreType.DMA((PIECES + 1,)),
        ],
        far_in=(0, 1),
        room=EDGE_ROOM,
    )
    count = NZ * NX
    above = lax.ppermute(head, "seq", [(i, i - 1) for i in range(1, count)])
    below = lax.ppermute(tail, "seq", [(i, i + 1) for i in range(count - 1)])
    sums, sizes = call(
        pool_kernel,
        [shape((SEG, FEAT), F32), shape((SEG, 128), F32)],
        [ids, tokens],
        scalars=None,
        flops=1 << 30,
        moved=2 << 20,
        scratch=[pltpu.VMEM((SEG, TOK), BF16)],
    )
    means, u, bias = call(
        norm_kernel,
        [shape((ROWS, FEAT), F32), shape((ROWS, FEAT), BF16), shape((16, FEAT), BF16)],
        [info, sums, sizes, head, above, below, norm_gain.reshape(8, FEAT)],
    )
    *weights, handed = call(
        load_kernel,
        [shape((WIDTH, COLS), BF16)] * 3 + [shape(u.shape, BF16)],
        [w_query, w_key, w_value, u],
        scalars=None,
        moved=12 << 20,
        scratch=[pltpu.SemaphoreType.DMA((3, 4))],
        aliases={3: 3},
        far_in=range(4),
        far_out=(3,),
        room=ROOM,
    )
    first, sibling, second = y_one(u), swap(handed), y_other(u)
    across = swap(first)
    part, part_query = shape((SEG, COLS), F32), shape((ROWS, COLS), F32)
    queried, keyed, valued = call(
        early_kernel,
        [part_query, part, part],
        [info, u, first, second, sibling, *weights],
        flops=ROWS * WIDTH * 3 * COLS,
        moved=3 << 20,
    )
    far = y_one(first)
    blocks = [u, first, second, far, sibling, across, swap(second), swap(far)]
    (kv,) = call(
        key_value_kernel,
        [shape((ROWS, 2 * COLS), BF16)],
        [info] + blocks + [weights[1], weights[2], keyed, valued, bias],
    )
    (query,) = call(
        query_kernel,
        [shape((ROWS, COLS), BF16)],
        [info] + blocks + [weights[0], queried, kv],
        far_in=(11,),
    )
    queries = [query] + [x_by(query, k) for k in (1, 2, 3)]
    one, other = z_one(kv), z_other(kv)
    one2, other2 = z_one(one), z_other(other)
    *state, done, theirs = call(
        first_step_kernel,
        STATE + [shape((4, SEG, FEAT), BF16)],
        [info] + queries + [one, other, w_out],
        flops=4 * 1088 * SEG * 3 * COLS,
        moved=4 << 20,
        scratch=[pltpu.SemaphoreType.DMA((4,))],
        far_in=(7,),
        far_out=(3,),
    )
    theirs = swap(theirs)
    one2, other2 = gate(info, [one2, other2], done)
    one3, other3 = z_one(one2), z_other(other2)
    *state, done = attend_step(2, info, queries, kv, [one2, other2], state)
    (one3_sent,) = gate(info, [one3], done)
    one4 = z_one(one3_sent)
    *state, done = attend_step(3, info, queries, None, [one3_sent, other3], state)
    partial = attend_step(4, info, queries, None, [one4], state)
    partial = [partial[0]] + [x_by(partial[k], -k) for k in (1, 2, 3)]
    (attended,) = call(merge_kernel, [shape((ROWS, COLS), BF16)], [info] + partial, moved=1 << 20)
    block = shape((ROWS, FEAT), BF16)
    own, first, second, third = call(
        product_kernel,
        [shape((ROWS, FEAT), F32)] * 2 + [block] * 2,
        [info, attended, swap(attended), w_out, theirs, means],
        flops=2 * ROWS * 2 * COLS * 4 * FEAT,
        moved=4 << 20,
    )
    (hot,) = call(mark_kernel, [shape((TOK, TALL), BF16)], [ids], flops=1 << 29, moved=3 << 20, scalars=None)
    (first,) = call(add_kernel, [block], [first, y_one(third)], scalars=None)
    return output([own, y_one(first), y_other(second)], hot, tokens)


def solution(mesh):
    placed = (
        P(("dp", "seq"), "mp"),
        P(("dp", "seq")),
        P(),
        P(None, "mp"),
        P(None, "mp"),
        P(None, "mp"),
        P("mp", None),
    )
    return jax.shard_map(
        shards, mesh=mesh, in_specs=placed, out_specs=P(("dp", "seq"), "mp"), check_vma=False
    )
```

```python
import functools

import jax
import jax.numpy as jnp
import numpy as np
from jax import lax
from jax.experimental import pallas as pl
from jax.experimental.pallas import tpu as pltpu
from jax.sharding import PartitionSpec as P

HD = 128
NZ, NX, NY, NC = 8, 4, 4, 2
SEG = 256
ROWS = SEG + 16
TOK = 2048
FEAT = 512
COLS = 256
WIDTH = 4096
SCORE = 1.4426950408889634 * HD**-0.5
LOG2E = 1.4426950408889634
LOW = -1e30
VMEM_LIMIT = 20 * 1024 * 1024
ROOM = 47 * 1024 * 1024
EDGE_ROOM = 51 * 1024 * 1024
PIECES = 8
F32, BF16 = jnp.float32, jnp.bfloat16


def number(z, x, y, c):
    return ((z % NZ) * NX + x % NX) * (NY * NC) + (y % NY) * NC + c % NC


def everywhere():
    return [(z, x, y, c) for z in range(NZ) for x in range(NX) for y in range(NY) for c in range(NC)]


def way(c):
    return 1 if c == 0 else -1


def move(value, target):
    pairs = [(number(*d), number(*target(*d))) for d in everywhere()]
    return lax.ppermute(value, ("seq", "mp"), pairs)


def swap(value):
    return move(value, lambda z, x, y, c: (z, x, y, 1 - c))


def y_one(value):
    return move(value, lambda z, x, y, c: (z, x, y + way(c), c))


def y_other(value):
    return move(value, lambda z, x, y, c: (z, x, y - way(c), c))


def z_one(value):
    return move(value, lambda z, x, y, c: (z + way(c), x, y, c))


def z_other(value):
    return move(value, lambda z, x, y, c: (z - way(c), x, y, c))


def x_by(value, by):
    return move(value, lambda z, x, y, c: (z, x + by, y, c))


def sources(y, c):
    own = [(y, c), (y - way(c), c), (y + way(c), c), (y + 2, c)]
    o = 1 - c
    other = [(y, o), (y - way(o), o), (y + way(o), o), (y + 2, o)]
    return [((b[0] % NY) * NC + b[1]) for b in own + other]


def mp_exchange(value):
    first = y_one(value)
    second = y_other(value)
    sibling = swap(value)
    far = y_one(first)
    return [value, first, second, far, sibling, swap(first), swap(second), swap(far)]


def device_table():
    rows = []
    for z, x, y, c in everywhere():
        row = [y * NC + c] + sources(y, c)
        row += [x] + [(x - k) % NX for k in (1, 2, 3)]
        for k in (1, 2, 3, 4):
            row += [int((z - way(c) * k) % NZ < z), int((z + way(c) * k) % NZ < z)]
        for o in (c, 1 - c):
            row += [(v % NY) * NC + o for v in (y, y + way(o), y - way(o), y + 2)]
        row += [0] * (32 - len(row))
        rows.append(row)
    return np.asarray(rows, np.int32)


I_MP, I_SRC, I_X, I_OK, I_CUT = 0, 1, 9, 13, 21
SMEM = pl.BlockSpec(memory_space=pltpu.SMEM)
WHOLE = pl.BlockSpec(memory_space=pltpu.VMEM)
FAR = pl.BlockSpec(memory_space=pl.ANY)
DISTANT = pl.BlockSpec(memory_space=pltpu.HBM)


def call(body, outs, ins, flops=0, moved=0, scratch=(), aliases=None, far_in=(), far_out=(), far=FAR, scalars=0, room=VMEM_LIMIT):
    return pl.pallas_call(
        body,
        out_shape=outs,
        in_specs=[SMEM if i == scalars else far if i in far_in else WHOLE for i in range(len(ins))],
        out_specs=[far if i in far_out else WHOLE for i in range(len(outs))],
        scratch_shapes=list(scratch),
        input_output_aliases=aliases or {},
        compiler_params=pltpu.CompilerParams(vmem_limit_bytes=room),
        cost_estimate=pl.CostEstimate(flops=flops, bytes_accessed=moved, transcendentals=0),
    )(*ins)


def gate_kernel(info, *refs):
    pass


def gate(info, values, token):
    ins = [info] + list(values) + [token]
    count = len(values)
    return call(
        gate_kernel,
        [shape(v.shape, v.dtype) for v in values],
        ins,
        aliases={i + 1: i for i in range(count)},
        far_in=range(1, count + 2),
        far_out=range(count),
    )


def shape(dims, dtype):
    return jax.ShapeDtypeStruct(dims, dtype)


def dot(a, b):
    return jnp.dot(a, b, preferred_element_type=F32)


def iota(dims, axis):
    return lax.broadcasted_iota(jnp.int32, dims, axis)


def ones_where(condition):
    return jnp.where(condition, 1.0, 0.0).astype(BF16)


def edge_kernel(flags_in, tokens_in, tokens, ids_out, head_out, tail_out, marks, flags, sems):
    copies = [pltpu.make_async_copy(flags_in, flags, sems.at[PIECES])]
    for i in range(PIECES):
        rows = pl.ds(i * (TOK // PIECES), TOK // PIECES)
        copies.append(pltpu.make_async_copy(tokens_in.at[rows, :], tokens.at[rows, :], sems.at[i]))
    for copy in copies:
        copy.start()
    copies[0].wait()
    f = flags[...].astype(F32).astype(BF16)
    upto = ones_where(iota((128, 128), 0) <= iota((128, 128), 1))
    inside = dot(f, upto)
    rows = dot(f, jnp.ones((128, 128), BF16)).astype(BF16)
    before = dot(ones_where(iota((16, 16), 1) < iota((16, 16), 0)), rows)
    ids_out[...] = (inside + before - 1.0).astype(jnp.int32)
    wanted = jnp.where(iota((16, 128), 0) < 8, -1, SEG - 1)
    for r in range(16):
        marks[:, r * 128 : (r + 1) * 128] = ones_where(ids_out[r : r + 1, :] == wanted)
    for copy in copies[1:]:
        copy.wait()
    sums = dot(marks[...], tokens[...])
    counts = dot(marks[...], jnp.ones((TOK, 128), BF16))
    head_out[:, :FEAT] = sums[:8]
    head_out[:, FEAT:] = counts[:8]
    tail_out[:, :FEAT] = sums[8:]
    tail_out[:, FEAT:] = counts[8:]


def pool_kernel(ids, tokens, sums_out, counts_out, hot):
    segment = iota((SEG, 128), 0)
    for r in range(16):
        hot[:, r * 128 : (r + 1) * 128] = ones_where(ids[r : r + 1, :] == segment)
    sums_out[...] = dot(hot[...], tokens[...])
    counts_out[...] = dot(hot[...], jnp.ones((TOK, 128), BF16))


def wide(column, times):
    return jnp.concatenate([column] * times, axis=1)


def split(value, parts):
    out = []
    for _ in range(parts):
        high = value.astype(BF16).astype(F32)
        out.append(high)
        value = value - high
    return out


def norm_kernel(info, sums, counts, head, above, below, gain, means_out, u_out, bias_out):
    g = gain[pl.ds(info[I_MP], 1), :]
    last = iota((SEG, 128), 0) == SEG - 1
    size = counts[...] + jnp.where(last, above[0:1, FEAT:], 0.0)
    total = sums[...] + jnp.where(iota((SEG, FEAT), 0) == SEG - 1, above[0:1, :FEAT], 0.0)
    size = jnp.maximum(size, 1.0)
    means = total / wide(size, 4)
    means_out[:SEG, :] = means
    u_out[:SEG, :] = (means * g).astype(BF16)
    squares = jnp.sum(means * means, axis=1, keepdims=True)
    squares = jnp.transpose(jnp.broadcast_to(squares, (SEG, 128)))[:16]
    high, low = split(squares, 2)
    extra_size = jnp.maximum(head[0:1, FEAT:] + below[0:1, FEAT:], 1.0)
    extra = (head[0:1, :FEAT] + below[0:1, :FEAT]) / wide(extra_size, 4)
    extra_squares = jnp.broadcast_to(jnp.sum(extra * extra, axis=1, keepdims=True), (16, SEG))
    extra_high, extra_low = split(extra_squares, 2)
    row = iota((16, FEAT), 0)
    means_out[SEG:, :] = jnp.where(row == 0, extra, 0.0)
    tail = jnp.where(row == 0, extra * g, 0.0)
    tail = jnp.where(row == 1, jnp.concatenate([high, low], axis=1), tail)
    tail = jnp.where(row == 2, jnp.concatenate([extra_high, extra_low], axis=1), tail)
    u_out[SEG:, :] = tail.astype(BF16)
    bias = jnp.log(jnp.transpose(size)[:16])
    bias_out[...] = jnp.concatenate([bias, bias], axis=1).astype(BF16)


EARLY = (0, 1, 2, 4)
LATE = (3, 5, 6, 7)


def row_scale(tail):
    squares = tail[:, :SEG] + tail[:, SEG:]
    scale = lax.rsqrt(squares / WIDTH + 1e-05)
    column = jnp.transpose(jnp.broadcast_to(scale[1:2, :], (128, SEG)))
    return scale, wide(column, 2)


def load_kernel(*refs):
    sources, outs, sems = refs[:3], refs[4:7], refs[8]
    copies = []
    for n in range(3):
        for i in range(4):
            rows = pl.ds(i * (WIDTH // 4), WIDTH // 4)
            copies.append(pltpu.make_async_copy(sources[n].at[rows, :], outs[n].at[rows, :], sems.at[n, i]))
            copies[-1].start()
    for copy in copies:
        copy.wait()


def product(info, acc, blocks, which, weight, rows):
    for i, u in zip(which, blocks):
        start = pl.multiple_of(info[I_SRC + i] * FEAT, FEAT)
        part = dot(u[:rows, :], weight[pl.ds(start, FEAT), :])
        acc = part if acc is None else acc + part
    return acc


def early_kernel(info, *refs):
    blocks, weights, sums = refs[:4], refs[4:7], refs[7:]
    for n, rows in enumerate((ROWS, SEG, SEG)):
        sums[n][...] = product(info, None, blocks, EARLY, weights[n], rows)


def square_rows(blocks):
    tail = jnp.zeros((16, FEAT), F32)
    for u in blocks:
        tail = tail + u[SEG:, :].astype(F32)
    return tail


def key_value_kernel(info, *refs):
    blocks, late = refs[:8], [refs[i] for i in LATE]
    w_key, w_value, keys, values, bias, kv_out = refs[8:]
    _, column = row_scale(square_rows(blocks))
    kv_out[:SEG, :COLS] = (product(info, keys[...], late, LATE, w_key, SEG) * column).astype(BF16)
    kv_out[:SEG, COLS:] = (product(info, values[...], late, LATE, w_value, SEG) * column).astype(BF16)
    kv_out[SEG:, :] = bias[...]


def query_kernel(info, *refs):
    blocks, late = refs[:8], [refs[i] for i in LATE]
    w_query, partial, _, q_out = refs[8:]
    scale, column = row_scale(square_rows(blocks))
    query = product(info, partial[...], late, LATE, w_query, ROWS)
    q_out[:SEG, :] = (query[:SEG] * column * SCORE).astype(BF16)
    extra = query[SEG:] * scale[2:3, :] * SCORE
    q_out[SEG:, :] = jnp.where(iota((16, COLS), 0) == 0, extra, 0.0).astype(BF16)


def nt_dot(a, b):
    return lax.dot_general(a, b, (((1,), (1,)), ((), ())), preferred_element_type=F32)


def attend(q, k, v, bias, acc_ref, m_ref, j, h, mask=None):
    scores = nt_dot(q[:, h * HD : (h + 1) * HD], k) + bias
    if mask is not None:
        scores = jnp.where(mask, scores, LOW)
    old = m_ref[j, h]
    peak = jnp.maximum(old, jnp.max(scores, axis=1, keepdims=True))
    expo = jnp.exp2(scores - wide(peak, scores.shape[1] // 128))
    if mask is not None:
        expo = jnp.where(mask, expo, 0.0)
    m_ref[j, h] = peak
    acc_ref[j, h] = acc_ref[j, h] * wide(jnp.exp2(old - peak), 2) + dot(expo.astype(BF16), v)


def keys_of(blocks, h):
    return jnp.concatenate([kv[:SEG, h * HD : (h + 1) * HD] for kv in blocks], axis=0)


def values_of(blocks, h):
    lanes = slice(COLS + h * HD, COLS + (h + 1) * HD)
    values = jnp.concatenate([kv[:SEG, lanes] for kv in blocks], axis=0)
    return jnp.concatenate([values, jnp.ones(values.shape, BF16)], axis=1)


def attend_kernel(step, has_own, info, *refs):
    first, final = step == 1, step == 4
    refs = list(refs)
    queries = [refs.pop(0) for _ in range(4)]
    own = refs.pop(0) if has_own else None
    others = [refs.pop(0) for _ in range(1 if final else 2)]
    if not first:
        state_in = [refs.pop(0) for _ in range(2)]
    if final:
        payloads = [refs.pop(0) for _ in range(4)]
        acc, m = state_in
    else:
        acc, m, done = refs[:3]
        done[...] = jnp.zeros_like(done)
    if first:
        acc[...] = jnp.zeros_like(acc)
        m[...] = jnp.full(m.shape, LOW, F32)
    if has_own:
        bias = own[SEG : SEG + 1, :SEG].astype(F32) * LOG2E
        for j in range(4):

            def one(j=j):
                mask = None
                if j == 0:
                    r, k = iota((ROWS, SEG), 0), iota((ROWS, SEG), 1)
                    mask = (k <= r) & (r < SEG)
                for h in range(2):
                    attend(queries[j], keys_of([own], h), values_of([own], h), bias, acc, m, j, h, mask)

            if j == 0:
                one()
            else:
                pl.when(info[I_X] < info[I_X + j])(one)
    ok = [info[I_OK + 2 * (step - 1) + i] for i in range(len(others))]
    some = ok[0] if final else ok[0] + ok[1]

    @pl.when(some > 0)
    def _():
        biases = []
        for kv, good in zip(others, ok):
            row = kv[SEG : SEG + 1, :SEG].astype(F32) * LOG2E
            biases.append(jnp.where(good > 0, row, LOW))
        bias = jnp.concatenate(biases, axis=1)
        for h in range(2):
            k, v = keys_of(others, h), values_of(others, h)
            for j in range(4):
                attend(queries[j], k, v, bias, acc, m, j, h)

    if final:
        row = iota((16, COLS), 0)
        for j in range(4):
            tail = jnp.zeros((16, COLS), F32)
            ends = []
            for h in range(2):
                total = acc[j, h][:, HD:]
                some_keys = total > 0.0
                total = jnp.where(some_keys, total, 1.0)
                out = acc[j, h][:, :HD] / total
                logs = jnp.where(some_keys, m[j, h] + jnp.log2(total), LOW)
                payloads[j][:SEG, h * HD : (h + 1) * HD] = out[:SEG].astype(BF16)
                ends.append(out[SEG:])
                parts = split(jnp.transpose(logs[:SEG])[:16], 3)
                for i, part in enumerate(parts):
                    tail = jnp.where(row == 1 + 3 * h + i, part, tail)
                parts = split(wide(logs[SEG : SEG + 1], 2), 3)
                for i, part in enumerate(parts):
                    tail = jnp.where(row == 7 + 3 * h + i, part, tail)
            tail = jnp.where(row == 0, jnp.concatenate(ends, axis=1), tail)
            payloads[j][SEG:, :] = tail.astype(BF16)


STATE = [shape((4, 2, ROWS, 2 * HD), F32), shape((4, 2, ROWS, HD), F32), shape((8, 128), F32)]


def attend_step(step, info, queries, own, others, state):
    first, final, has_own = step == 1, step == 4, own is not None
    ins = [info] + queries + ([own] if has_own else []) + others + list(state or [])
    flops = 4 * 1088 * SEG * (len(others) + 1) * COLS
    body = functools.partial(attend_kernel, step, has_own)
    if final:
        outs = [shape((ROWS, COLS), BF16)] * 4 + STATE[:2]
        aliases = {len(ins) - 2: 4, len(ins) - 1: 5}

        def body(*refs):
            refs = list(refs)
            payloads, state = refs[-6:-2], refs[-2:]
            attend_kernel(step, has_own, *refs[:-8], *state, *payloads)

        return call(body, outs, ins, flops=flops, moved=4 << 20, aliases=aliases)[:4]
    aliases = {} if first else {len(ins) - 2: 0, len(ins) - 1: 1}
    return call(body, STATE, ins, flops=flops, moved=4 << 20, aliases=aliases)


def merge_kernel(info, a, b, c, d, out):
    parts = (a, b, c, d)
    tails = [p[SEG:, :].astype(F32) for p in parts]
    weights, end_weights = [], []
    for h in range(2):
        for base, store in ((1 + 3 * h, weights), (7 + 3 * h, end_weights)):
            logs = [t[base : base + 1] + t[base + 1 : base + 2] + t[base + 2 : base + 3] for t in tails]
            peak = functools.reduce(jnp.maximum, logs)
            expo = [jnp.exp2(v - peak) for v in logs]
            whole = functools.reduce(jnp.add, expo)
            store.append([e / whole for e in expo])
    flat = weights[0] + weights[1]
    columns = jnp.transpose(jnp.concatenate(flat + [jnp.zeros((120, SEG), F32)], axis=0))
    ends = []
    for h in range(2):
        lanes = slice(h * HD, (h + 1) * HD)
        acc = jnp.zeros((SEG, HD), F32)
        end = jnp.zeros((16, HD), F32)
        for j, p in enumerate(parts):
            acc = acc + columns[:, 4 * h + j : 4 * h + j + 1] * p[:SEG, lanes].astype(F32)
            end = end + end_weights[h][j][:, :HD] * tails[j][:, lanes]
        out[:SEG, lanes] = acc.astype(BF16)
        ends.append(end)
    end = jnp.concatenate(ends, axis=1)
    out[SEG:, :] = jnp.where(iota((16, COLS), 0) == 0, end, 0.0).astype(BF16)


BLOCK = 1024
TALL = 384


def mark_kernel(ids, out):
    lane = iota((128, 128), 1)
    for r in range(TOK // 128):
        row = ids[r : r + 1, :].astype(F32)
        column = jnp.transpose(jnp.broadcast_to(row, (128, 128))).astype(jnp.int32)
        rows = slice(r * 128, (r + 1) * 128)
        out[rows, :128] = ones_where(column == lane)
        out[rows, 128:256] = ones_where(column == lane + 128)
        out[rows, 256:] = ones_where((column == -1) & (lane == 0))


def output_kernel(own, first, second, hot, tokens, out, coarse):
    @pl.when(pl.program_id(0) == 0)
    def _():
        total = own[...] + first[...].astype(F32) + second[...].astype(F32)
        coarse[:ROWS, :] = total.astype(BF16)
        coarse[ROWS:, :] = jnp.zeros((TALL - ROWS, FEAT), BF16)

    picked = dot(hot[...], coarse[...])
    out[...] = (tokens[...].astype(F32) + picked).astype(BF16)


def output(products, hot, tokens):
    return pl.pallas_call(
        output_kernel,
        grid=(TOK // BLOCK,),
        out_shape=shape((TOK, FEAT), BF16),
        in_specs=[WHOLE] * 3
        + [pl.BlockSpec((BLOCK, TALL), lambda i: (i, 0)), pl.BlockSpec((BLOCK, FEAT), lambda i: (i, 0))],
        out_specs=pl.BlockSpec((BLOCK, FEAT), lambda i: (i, 0)),
        scratch_shapes=[pltpu.VMEM((TALL, FEAT), BF16)],
        compiler_params=pltpu.CompilerParams(vmem_limit_bytes=VMEM_LIMIT),
        cost_estimate=pl.CostEstimate(flops=2 << 30, bytes_accessed=6 << 20, transcendentals=0),
    )(*products, hot, tokens)


def first_step_kernel(*refs):
    info, w_out, sibling, sems = refs[0], refs[7], refs[11], refs[12]
    copies = []
    for i in range(4):
        start = pl.multiple_of(info[I_CUT + 4 + i] * FEAT, FEAT)
        copies.append(pltpu.make_async_copy(w_out.at[:, pl.ds(start, FEAT)], sibling.at[i], sems.at[i]))
        copies[-1].start()
    attend_kernel(1, False, *refs[:7], *refs[8:11])
    for copy in copies:
        copy.wait()


def product_kernel(info, attended, other, w_out, theirs, means, own_out, *outs):
    for i in range(4):
        start = pl.multiple_of(info[I_CUT + i] * FEAT, FEAT)
        part = dot(attended[...], w_out[:, pl.ds(start, FEAT)]) + dot(other[...], theirs[i])
        if i == 0:
            own_out[...] = part + means[...]
        else:
            outs[i - 1][...] = part.astype(outs[i - 1].dtype)


def add_kernel(a, b, out):
    out[...] = (a[...] + b[...].astype(F32)).astype(BF16)


def shards(tokens, flags, norm_gain, w_query, w_key, w_value, w_out):
    seq, mp = lax.axis_index("seq"), lax.axis_index("mp")
    info = jnp.asarray(device_table())[seq * (NY * NC) + mp]
    edge = shape((8, FEAT + 128), F32)
    tokens, ids, head, tail = call(
        edge_kernel,
        [shape((TOK, FEAT), BF16), shape((16, 128), jnp.int32), edge, edge],
        [flags.reshape(16, 128), tokens],
        scalars=None,
        flops=1 << 28,
        moved=2 << 20,
        scratch=[
            pltpu.VMEM((16, TOK), BF16),
            pltpu.VMEM((16, 128), jnp.int32),
            pltpu.SemaphoreType.DMA((PIECES + 1,)),
        ],
        far_in=(0, 1),
        room=EDGE_ROOM,
    )
    count = NZ * NX
    above = lax.ppermute(head, "seq", [(i, i - 1) for i in range(1, count)])
    below = lax.ppermute(tail, "seq", [(i, i + 1) for i in range(count - 1)])
    sums, sizes = call(
        pool_kernel,
        [shape((SEG, FEAT), F32), shape((SEG, 128), F32)],
        [ids, tokens],
        scalars=None,
        flops=1 << 30,
        moved=2 << 20,
        scratch=[pltpu.VMEM((SEG, TOK), BF16)],
    )
    means, u, bias = call(
        norm_kernel,
        [shape((ROWS, FEAT), F32), shape((ROWS, FEAT), BF16), shape((16, FEAT), BF16)],
        [info, sums, sizes, head, above, below, norm_gain.reshape(8, FEAT)],
    )
    *weights, handed = call(
        load_kernel,
        [shape((WIDTH, COLS), BF16)] * 3 + [shape(u.shape, BF16)],
        [w_query, w_key, w_value, u],
        scalars=None,
        moved=12 << 20,
        scratch=[pltpu.SemaphoreType.DMA((3, 4))],
        aliases={3: 3},
        far_in=range(4),
        far_out=(3,),
        room=ROOM,
    )
    first, sibling, second = y_one(u), swap(handed), y_other(u)
    across = swap(first)
    part, part_query = shape((SEG, COLS), F32), shape((ROWS, COLS), F32)
    queried, keyed, valued = call(
        early_kernel,
        [part_query, part, part],
        [info, u, first, second, sibling, *weights],
        flops=ROWS * WIDTH * 3 * COLS,
        moved=3 << 20,
    )
    far = y_one(first)
    blocks = [u, first, second, far, sibling, across, swap(second), swap(far)]
    (kv,) = call(
        key_value_kernel,
        [shape((ROWS, 2 * COLS), BF16)],
        [info] + blocks + [weights[1], weights[2], keyed, valued, bias],
    )
    (query,) = call(
        query_kernel,
        [shape((ROWS, COLS), BF16)],
        [info] + blocks + [weights[0], queried, kv],
        far_in=(11,),
    )
    queries = [query] + [x_by(query, k) for k in (1, 2, 3)]
    one, other = z_one(kv), z_other(kv)
    one2, other2 = z_one(one), z_other(other)
    *state, done, theirs = call(
        first_step_kernel,
        STATE + [shape((4, SEG, FEAT), BF16)],
        [info] + queries + [one, other, w_out],
        flops=4 * 1088 * SEG * 3 * COLS,
        moved=4 << 20,
        scratch=[pltpu.SemaphoreType.DMA((4,))],
        far_in=(7,),
        far_out=(3,),
    )
    theirs = swap(theirs)
    one2, other2 = gate(info, [one2, other2], done)
    one3, other3 = z_one(one2), z_other(other2)
    *state, done = attend_step(2, info, queries, kv, [one2, other2], state)
    (one3_sent,) = gate(info, [one3], done)
    one4 = z_one(one3_sent)
    *state, done = attend_step(3, info, queries, None, [one3_sent, other3], state)
    partial = attend_step(4, info, queries, None, [one4], state)
    partial = [partial[0]] + [x_by(partial[k], -k) for k in (1, 2, 3)]
    (attended,) = call(merge_kernel, [shape((ROWS, COLS), BF16)], [info] + partial, moved=1 << 20)
    block = shape((ROWS, FEAT), BF16)
    own, first, second, third = call(
        product_kernel,
        [shape((ROWS, FEAT), F32)] * 2 + [block] * 2,
        [info, attended, swap(attended), w_out, theirs, means],
        flops=2 * ROWS * 2 * COLS * 4 * FEAT,
        moved=4 << 20,
    )
    (hot,) = call(mark_kernel, [shape((TOK, TALL), BF16)], [ids], flops=1 << 29, moved=3 << 20, scalars=None)
    (first,) = call(add_kernel, [block], [first, y_one(third)], scalars=None)
    return output([own, y_one(first), y_other(second)], hot, tokens)


def solution(mesh):
    placed = (
        P(("dp", "seq"), "mp"),
        P(("dp", "seq")),
        P(),
        P(None, "mp"),
        P(None, "mp"),
        P(None, "mp"),
        P("mp", None),
    )
    return jax.shard_map(
        shards, mesh=mesh, in_specs=placed, out_specs=P(("dp", "seq"), "mp"), check_vma=False
    )
```
